256 devices in a mesh: gx: 32 (over x, y, core), gy: 8 (over z).
Axes of the slice: x: 4, y: 4, z: 8, core: 2. Of those that a mesh axis runs over, the one named last changes fastest.
Arguments:
- velocity_u: float32 [10, 256, 8192], P(None, 'gy', 'gx'), may hold values from -3 to 3
- velocity_v: float32 [10, 256, 8192], P(None, 'gy', 'gx'), may hold values from -3 to 3
- tracers: float32 [2, 10, 256, 8192], P(None, None, 'gy', 'gx'), may hold values from -6 to 6
- diffusivity: float32 [10, 256, 8192], P(None, 'gy', 'gx'), may hold values from 0.01 to 10
- surface: float32 [256, 8192], P('gy', 'gx'), may hold values from -2 to 2
- depth: float32 [256, 8192], P('gy', 'gx'), may hold values from 0.5 to 1.5
- wet_mask: int32 [256, 8192], P('gy', 'gx'), may hold values 0 or 1
- level_count: int32 [256, 8192], P('gy', 'gx'), may hold values from 1 to 10
Outputs:
- flow_u: float32 [10, 256, 8192], P(None, 'gy', 'gx')
- flow_v: float32 [10, 256, 8192], P(None, 'gy', 'gx')
- mixed: float32 [2, 10, 256, 8192], P(None, None, 'gy', 'gx')
- height: float32 [256, 8192], P('gy', 'gx')
- overturning: float32 [10, 256], P(None, 'gy')
The draws below stay inside these ranges and needn't reach their ends.
All inputs are finite; a program needn't handle non-finite values. No bound on the sum of `wet_mask` on one device may be relied on, other than what follows from the above.
Results may differ from the reference program's by a relative error of at most 0.0085.
Values sent between devices are 32-bit elements; how exact they have to be, the bound alone decides.
A program may use at most 128 MiB of HBM per device.

```python
import math
import jax
import jax.numpy as jnp

NZ = 10
NB = 4
NX = 8192
NY = 256


def touch_ends(array, stream_key, smallest, high):
    shape = array.shape
    spot = [jax.random.randint(jax.random.fold_in(stream_key, axis), (), 0, shape[axis]) for axis in range(len(shape))]
    array = array.at[tuple(spot)].set(smallest)
    longest = shape.index(max(shape))
    spot[longest] = (spot[longest] + 1) % shape[longest]
    return array.at[tuple(spot)].set(high)


def steps_of(rng, shape, shards, least, high):
    def one(position, blocks):
        heights = jax.random.uniform(jax.random.fold_in(jax.random.fold_in(rng, 6), position), (blocks,), jnp.float32, least / len(shards), high / len(shards))
        return jnp.repeat(jnp.exp(heights), shape[position] // blocks).reshape((-1,) + (1,) * (len(shape) - position - 1))

    factor_of = one(*shards[0])
    for cut in shards[1:]:
        factor_of = factor_of * one(*cut)
    return factor_of


def bell_draw(rng, extent, width, reach, split=(), kind=jnp.bfloat16):
    factor_of = steps_of(rng, extent, split, -0.22, 0.18) if split else 1.0
    values = jax.random.normal(rng, extent, jnp.float32) * width * factor_of
    return jnp.minimum(jnp.maximum(values, -reach), reach).astype(kind)


def setup_inputs(seed: int = 0) -> dict:
    key_list = jax.random.split(jax.random.key(seed), 9)
    velocity_u = bell_draw(key_list[0], (NZ, NY, NX), 0.5, 3.0, ((1, 8), (2, 32)), jnp.float32)
    velocity_v = bell_draw(key_list[1], (NZ, NY, NX), 0.5, 3.0, ((1, 8), (2, 32)), jnp.float32)
    tracers = bell_draw(key_list[2], (2, NZ, NY, NX), 1.0, 6.0, ((2, 8), (3, 32)), jnp.float32)
    diffusivity = jnp.clip(jnp.exp(math.log(10.0) - 6.9077553 * jax.random.uniform(key_list[3], (NZ, NY, NX), jnp.float32) ** steps_of(key_list[3], (NZ, NY, NX), ((1, 8), (2, 32)), -0.2, 0.2)), 0.01, 10.0)
    surface = bell_draw(key_list[4], (NY, NX), 0.3, 2.0, ((0, 8), (1, 32)), jnp.float32)
    depth = jnp.clip(0.5 + 1.0 * jax.random.uniform(key_list[5], (NY, NX), jnp.float32) ** steps_of(key_list[5], (NY, NX), ((0, 8), (1, 32)), -0.2, 0.2), 0.5, 1.5)
    wet_mask = touch_ends((jax.random.randint(key_list[6], (NY, NX), 0, 8) < 7).astype(jnp.int32), jax.random.fold_in(key_list[6], 1), 0, 1)
    level_count = touch_ends(jax.random.randint(key_list[7], (NY, NX), 1, NZ + 1), jax.random.fold_in(key_list[7], 1), 1, NZ).astype(jnp.int32)
    return dict(velocity_u=velocity_u, velocity_v=velocity_v, tracers=tracers, diffusivity=diffusivity, surface=surface, depth=depth, wet_mask=wet_mask, level_count=level_count)


wave_coef = 0.5
press_coef = 0.05
time_step = 0.5


def shift_east(x):
    return jnp.roll(x, -1, axis=-1)


def shift_west(x):
    return jnp.roll(x, 1, axis=-1)


def shift_north(x):
    return jnp.concatenate([x[..., 1:, :], jnp.zeros_like(x[..., :1, :])], axis=-2)


def shift_south(x):
    return jnp.concatenate([jnp.zeros_like(x[..., :1, :]), x[..., :-1, :]], axis=-2)


def level_masks(wet_cells, count_cells, levels):
    layer = jnp.arange(levels).astype(wet_cells.dtype)[:, None, None]
    return jnp.where(layer < count_cells[None], wet_cells[None], jnp.zeros_like(wet_cells[None]))


def wave_substep(height, flow_east, flow_north, wet_cells, east_depth, north_depth, east_wet, north_wet):
    east_flux = east_depth * flow_east
    north_flux = north_depth * flow_north
    height = height - wave_coef * (east_flux - shift_west(east_flux) + north_flux - shift_south(north_flux)) * wet_cells
    flow_east = flow_east - wave_coef * (shift_east(height) - height) * east_wet
    flow_north = flow_north - wave_coef * (shift_north(height) - height) * north_wet
    return height, flow_east, flow_north


def new_flow(tracers, velocity_u, velocity_v, layer_wet, mean_east, mean_north):
    buoyancy = 0.3 * tracers[1] - 0.7 * tracers[0]
    pressure = jnp.cumsum(buoyancy, axis=0)
    face_east = layer_wet * shift_east(layer_wet)
    face_north = layer_wet * shift_north(layer_wet)
    levels = layer_wet.shape[0]
    trial_u = velocity_u - press_coef * (shift_east(pressure) - pressure)
    trial_v = velocity_v - press_coef * (shift_north(pressure) - pressure)
    fixed_u = (levels * mean_east - jnp.sum(trial_u * face_east, axis=0)) / jnp.maximum(jnp.sum(face_east, axis=0), 1.0)
    fixed_v = (levels * mean_north - jnp.sum(trial_v * face_north, axis=0)) / jnp.maximum(jnp.sum(face_north, axis=0), 1.0)
    return (trial_u + fixed_u) * face_east, (trial_v + fixed_v) * face_north


def vertical_update(tracers, horizontal, divergence, layer_wet):
    top_w = -jnp.flip(jnp.cumsum(jnp.flip(divergence, 0), axis=0), 0)
    bottom_w = jnp.concatenate([top_w[1:], jnp.zeros_like(top_w[:1])], axis=0)
    top_face = jnp.concatenate([tracers[:, :1], 0.5 * (tracers[:, :-1] + tracers[:, 1:])], axis=1)
    bottom_face = jnp.concatenate([top_face[:, 1:], tracers[:, -1:]], axis=1)
    tendency = horizontal - (top_w * top_face - bottom_w * bottom_face)
    return (tracers + time_step * tendency) * layer_wet


def mixing(source, diffusivity, layer_wet):
    below = jnp.concatenate([layer_wet[1:], jnp.zeros_like(layer_wet[:1])], axis=0)
    kappa = diffusivity * layer_wet * below
    levels = kappa.shape[0]
    ratios = []
    values = []
    for level in range(levels):
        if level == 0:
            denom = 1.0 + kappa[0]
            value = source[:, 0] / denom
        else:
            lower = kappa[level - 1]
            denom = 1.0 + lower + kappa[level] - lower * ratios[-1]
            value = (source[:, level] + lower * values[-1]) / denom
        ratios.append(kappa[level] / denom)
        values.append(value)
    result = [values[-1]]
    for level in range(levels - 2, -1, -1):
        result.append(values[level] + ratios[level] * result[-1])
    return jnp.stack(result[::-1], axis=1)


def tracer_terms(tracers, flow_u, flow_v):
    face_x = (7.0 * (tracers + shift_east(tracers)) - (shift_west(tracers) + shift_east(shift_east(tracers)))) / 12.0
    flux_x = flow_u * face_x
    face_y = (7.0 * (tracers + shift_north(tracers)) - (shift_south(tracers) + shift_north(shift_north(tracers)))) / 12.0
    flux_y = flow_v * face_y
    return -(flux_x - shift_west(flux_x)) - (flux_y - shift_south(flux_y))


def reference(velocity_u, velocity_v, tracers, diffusivity, surface, depth, wet_mask, level_count):
    levels = velocity_u.shape[0]
    wet_cells = wet_mask.astype(jnp.float32)
    layer_wet = level_masks(wet_cells, level_count.astype(jnp.float32), levels)
    east_wet = wet_cells * shift_east(wet_cells)
    north_wet = wet_cells * shift_north(wet_cells)
    east_depth = 0.5 * (depth + shift_east(depth)) * east_wet
    north_depth = 0.5 * (depth + shift_north(depth)) * north_wet
    flow_east = jnp.sum(velocity_u * layer_wet * shift_east(layer_wet), axis=0) / levels
    flow_north = jnp.sum(velocity_v * layer_wet * shift_north(layer_wet), axis=0) / levels
    height = surface
    total_east = jnp.zeros_like(flow_east)
    total_north = jnp.zeros_like(flow_north)
    for substep in range(3 * NB):
        height, flow_east, flow_north = wave_substep(height, flow_east, flow_north, wet_cells, east_depth, north_depth, east_wet, north_wet)
        total_east = total_east + flow_east
        total_north = total_north + flow_north
    mean_east = total_east / (3 * NB)
    mean_north = total_north / (3 * NB)
    flow_u, flow_v = new_flow(tracers, velocity_u, velocity_v, layer_wet, mean_east, mean_north)
    divergence = flow_u - shift_west(flow_u) + flow_v - shift_south(flow_v)
    horizontal = tracer_terms(tracers, flow_u, flow_v)
    source = vertical_update(tracers, horizontal, divergence, layer_wet)
    mixed = mixing(source, diffusivity, layer_wet)
    row_sums = jnp.sum(flow_v, axis=2)
    overturning = jnp.cumsum(row_sums, axis=1) * (NX * NY) ** -0.5
    return flow_u, flow_v, mixed, height, overturning
```

```python
import jax
import jax.numpy as jnp
from jax import lax
from jax.experimental import pallas as pl
from jax.experimental.pallas import tpu as pltpu
from jax.sharding import PartitionSpec as P

SUBSTEPS = 12
WAVE = 0.5
PRESS = 0.05
DT = 0.5
MESH_ID = pl.DeviceIdType.MESH
F32 = jnp.float32
CW, DP, HT, FE, FN = range(5)
RAW = 80


def lanes(shape):
    return lax.broadcasted_iota(jnp.int32, shape, len(shape) - 1)


def rows(shape):
    return lax.broadcasted_iota(jnp.int32, shape, len(shape) - 2)


def turn(x, by):
    size = x.shape[-1]
    by = by % size if isinstance(by, int) else lax.rem(by + size, size)
    return x if isinstance(by, int) and by == 0 else pltpu.roll(x, by, x.ndim - 1)


def east(x):
    return turn(x, -1)


def west(x):
    return turn(x, 1)


def exact_dot(a, b, dims):
    return lax.dot_general(
        a, b, (dims, ((), ())), precision=lax.Precision.HIGHEST, preferred_element_type=F32
    )


def step_kernel(
    u_in, v_in, t_in, d_in, surface_in, depth_in, wet_in, count_in,
    fu_out, fv_out, m_out, h_out, ov_out,
    ext, u_s, v_s, d_s, t_s, wet_s, count_s,
    pack_e, pack_w, got_w, got_e, got_sw, got_nw, got_se, got_ne, raw_s, raw_n,
    tr_e, tr_w, got_tw, got_te,
    ed, nd, ew, nw, me, mn, gs, te, tn,
    tu, t0, pk, inv, ratio, sums, own_r, peer_r, all_r, south_r, fyb,
    in_sem, send_sem, recv_sem, gx_send, gx_recv, gy_send, gy_recv,
    *, nx, ny,
):
    gx, gy = lax.axis_index("gx"), lax.axis_index("gy")
    levels = u_s.shape[0]

    def at(dx, dy):
        return (lax.rem(gx + dx + nx, nx), lax.rem(gy + dy + ny, ny))

    diagonal = [(1, 1), (1, -1), (-1, 1), (-1, -1)]
    gx_peers = [(dx, 0) for dx in range(1, nx)]
    gy_peers = [(0, dy) for dy in range(1, ny)]

    greeted = diagonal + gx_peers + gy_peers
    barrier = pltpu.get_barrier_semaphore()
    for peer in greeted:
        pl.semaphore_signal(barrier, inc=1, device_id=at(*peer), device_id_type=MESH_ID)

    own = (pl.ds(24, 32), pl.ds(128, 256))
    loads = [
        pltpu.make_async_copy(a, b, in_sem.at[i])
        for i, (a, b) in enumerate(
            [
                (wet_in, wet_s),
                (count_in, count_s),
                (depth_in, ext.at[(DP, *own)]),
                (surface_in, ext.at[(HT, *own)]),
                (u_in, u_s),
                (v_in, v_s.at[:, pl.ds(8, 32), :]),
                (t_in, t_s.at[:, :, pl.ds(16, 32), :]),
                (d_in, d_s),
            ]
        )
    ]
    for load in loads:
        load.start()

    for load in loads[:4]:
        load.wait()
    cw = jnp.where(wet_s[...] > 0, count_s[...], 0).astype(F32)
    ext[CW, 24:56, 128:384] = cw
    m_u = jnp.minimum(cw, east(cw))
    gs[24:56, 128:384] = cw
    gs[56:64, 128:384] = jnp.zeros((8, 256), F32)
    m_v = jnp.minimum(cw, gs[25:57, 128:384])
    loads[4].wait()
    flow = jnp.zeros_like(cw)
    for k in range(levels):
        flow = flow + jnp.where(m_u > k, u_s[k], 0.0)
    flow_e = flow / levels
    ext[FE, 24:56, 128:384] = flow_e
    loads[5].wait()
    flow = jnp.zeros_like(cw)
    for k in range(levels):
        flow = flow + jnp.where(m_v > k, v_s[k, 8:40, :], 0.0)
    flow_n = flow / levels
    ext[FN, 24:56, 128:384] = flow_n

    lane = lanes((32, 128))
    fields = [cw, ext[DP, 24:56, 128:384], ext[HT, 24:56, 128:384], flow_e, flow_n]
    to_e = jnp.zeros((32, 128), F32)
    to_w = jnp.zeros((32, 128), F32)
    for a, field in enumerate(fields):
        here = jnp.logical_and(lane >= 16 * a, lane < 16 * a + 16)
        to_e = jnp.where(here, turn(field[:, 128:], 16 * a - 112), to_e)
        to_w = jnp.where(here, turn(field[:, :128], 16 * a), to_w)
    for k in range(levels):
        to_e = jnp.where(lane == RAW + k, turn(u_s[k, :, 128:], RAW + k - 127), to_e)
    pack_e[0:32, :] = to_e
    pack_w[0:32, :] = to_w
    pack_e[32:48, :] = jnp.zeros((16, 128), F32)
    pack_w[32:48, :] = jnp.zeros((16, 128), F32)
    for k in range(levels):
        pack_e[32 + k : 33 + k, :] = v_s[k, 39:40, 128:256]
        pack_w[32 + k : 33 + k, :] = v_s[k, 39:40, 0:128]

    pl.semaphore_wait(barrier, len(greeted))

    count = [0]

    def send(src, dst, dx, dy):
        i = count[0]
        count[0] += 1
        copy = pltpu.make_async_remote_copy(
            src_ref=src, dst_ref=dst, send_sem=send_sem.at[i], recv_sem=recv_sem.at[i],
            device_id=at(dx, dy), device_id_type=MESH_ID,
        )
        copy.start()
        return copy

    everything = (slice(None), slice(None))
    wide = pl.ds(128, 256)
    halo = [
        send(pack_e.at[pl.ds(16, 32)], got_sw, 1, 1),
        send(pack_w.at[pl.ds(16, 32)], got_se, -1, 1),
        send(pack_e.at[pl.ds(0, 16)], got_nw, 1, -1),
        send(pack_w.at[pl.ds(0, 16)], got_ne, -1, -1),
        send(ext.at[:, pl.ds(40, 16), wide], ext.at[:, pl.ds(8, 16), wide], 0, 1),
        send(ext.at[:, pl.ds(24, 16), wide], ext.at[:, pl.ds(56, 16), wide], 0, -1),
        send(pack_e.at[pl.ds(16, 16)], raw_s, 0, 1),
        send(pack_e.at[pl.ds(0, 16)], raw_n, 0, -1),
        send(v_s.at[:, pl.ds(39, 1), :], v_s.at[:, pl.ds(7, 1), :], 0, 1),
        send(pack_e, got_w, 1, 0),
        send(pack_w, got_e, -1, 0),
    ]

    loads[6].wait()
    to_e = jnp.zeros((32, 128), F32)
    to_w = jnp.zeros((32, 128), F32)
    for tr in range(2):
        for k in range(levels):
            at_lane = 4 * (tr * levels + k)
            first = (at_lane - 2) % 128
            to_e = jnp.where((lane == first) | (lane == first + 1),
                             turn(t_s[tr, k, 16:48, 128:256], at_lane), to_e)
            to_w = jnp.where((lane == at_lane) | (lane == at_lane + 1),
                             turn(t_s[tr, k, 16:48, 0:128], at_lane), to_w)
    tr_e[...] = to_e
    tr_w[...] = to_w
    tracer_halo = [
        send(tr_e, got_tw, 1, 0),
        send(tr_w, got_te, -1, 0),
        send(t_s.at[:, :, pl.ds(46, 2), :], t_s.at[:, :, pl.ds(14, 2), :], 0, 1),
        send(t_s.at[:, :, pl.ds(16, 2), :], t_s.at[:, :, pl.ds(48, 2), :], 0, -1),
    ]

    loads[7].wait()
    below_kappa = jnp.zeros_like(cw)
    below_ratio = jnp.zeros_like(cw)
    for k in range(levels - 1, -1, -1):
        above = jnp.where(cw > k, d_s[k - 1], 0.0) if k else jnp.zeros_like(cw)
        factor = 1.0 / (1.0 + above + below_kappa - below_kappa * below_ratio)
        below_ratio = above * factor
        inv[k] = factor
        ratio[k] = below_ratio
        below_kappa = above

    for copy in halo:
        copy.wait()

    lane = lanes((64, 128))
    from_w = jnp.concatenate([got_sw[0:16], got_w[0:32], got_nw[...]], axis=0)
    from_e = jnp.concatenate([got_se[0:16], got_e[0:32], got_ne[...]], axis=0)
    for a in range(5):
        ext[a, 8:72, 0:128] = jnp.where(
            lane < 64, turn(from_e, -16 * a), turn(from_w, 112 - 16 * a)
        )
    row = rows((64, 384))
    closed = jnp.logical_or(
        jnp.logical_and(row < 16, gy == 0), jnp.logical_and(row >= 48, gy == ny - 1)
    )
    cells = jnp.where(closed, 0.0, ext[CW, 8:72, :])
    ext[CW, 8:72, :] = cells
    ext[CW, 72:80, :] = jnp.zeros((8, 384), F32)
    mask_e = jnp.minimum(cells, east(cells))
    mask_n = jnp.minimum(cells, ext[CW, 9:73, :])
    me[...] = mask_e[16:48]
    mn[...] = mask_n[8:48, 128:384]
    deep = ext[DP, 8:72, :]
    half = 0.5 * WAVE
    ed[...] = jnp.where(mask_e > 0.0, half * (deep + east(deep)), 0.0)
    ew[...] = jnp.where(mask_e > 0.0, WAVE, 0.0)
    ext[DP, 72:80, :] = jnp.zeros((8, 384), F32)
    nd[...] = jnp.where(mask_n > 0.0, half * (deep + ext[DP, 9:73, :]), 0.0)
    nw[...] = jnp.where(mask_n > 0.0, WAVE, 0.0)

    def column_mean(raw, cut):
        hold = jnp.logical_and(lane >= RAW, (lane - RAW).astype(F32) < cut)
        return jnp.sum(jnp.where(hold, raw, 0.0), axis=1, keepdims=True) / levels

    raw_own = jnp.concatenate([raw_s[...], pack_e[0:32], raw_n[...]], axis=0)
    ext[FE, 8:72, 0:128] = jnp.where(
        lane == 127, column_mean(from_w, mask_e[:, 127:128]), ext[FE, 8:72, 0:128]
    )
    ext[FE, 8:72, 256:384] = jnp.where(
        lane == 127, column_mean(raw_own, mask_e[:, 383:384]), ext[FE, 8:72, 256:384]
    )
    for first, tile in ((16, 0), (48, 32)):
        cut = mask_n[first - 8 : first, 128:384]
        total = jnp.zeros_like(cut)
        for k in range(levels):
            total = total + jnp.where(cut > k, v_s[k, tile : tile + 8, :], 0.0)
        ext[FN, first : first + 8, 128:384] = jnp.where(
            rows((8, 256)) == 7, total / levels, ext[FN, first : first + 8, 128:384]
        )
    lane = lanes((16, 128))
    level = rows((16, 128)).astype(F32)
    for line, a, b in ((15, got_se[16:32], got_sw[16:32]), (47, got_e[32:48], got_w[32:48])):
        raw = jnp.where(lane < 64, a, b)
        hold = level < mask_n[line : line + 1, 0:128]
        mean = jnp.sum(jnp.where(hold, raw, 0.0), axis=0, keepdims=True) / levels
        ext[FN, 8 + line : 9 + line, 0:128] = mean

    te[...] = jnp.zeros_like(te)
    tn[...] = jnp.zeros_like(tn)
    gs[...] = jnp.zeros_like(gs)

    def substep(first, last):
        here = slice(8 + first, 8 + last)
        inner = slice(first, last)
        fe = ext[FE, here, :]
        fn = ext[FN, here, :]
        fx = ed[inner, :] * fe
        fy = nd[inner, :] * fn
        gs[here, :] = fy
        height = ext[HT, here, :] - (fx - west(fx) + fy - gs[7 + first : 7 + last, :])
        ext[HT, here, :] = height
        fe = fe - ew[inner, :] * (east(height) - height)
        fn = fn - nw[inner, :] * (ext[HT, 9 + first : 9 + last, :] - height)
        ext[FE, here, :] = fe
        ext[FN, here, :] = fn
        te[...] += fe[16 - first : 48 - first]
        tn[...] += fn[8 - first : 48 - first, 128:384]

    ext[HT, 72:80, :] = jnp.zeros((8, 384), F32)

    def wide_step(_, carry):
        substep(0, 64)
        return carry

    def narrow_step(_, carry):
        substep(8, 56)
        return carry

    lax.fori_loop(0, 5, wide_step, 0)
    lax.fori_loop(0, SUBSTEPS - 5, narrow_step, 0)
    h_out[...] = ext[HT, 24:56, 128:384]

    for copy in tracer_halo:
        copy.wait()
    lane = lanes((32, 128))
    both = jnp.where(lane % 4 >= 2, got_tw[...], got_te[...])
    m_e = me[...]
    m_n = mn[...]

    def trial(k, carry):
        p0, py, su, sv = carry
        for tr in range(2):
            t0[tr, k] = turn(both, 128 - 4 * (tr * levels + k))
            t_s[tr, k, 8:16, :] = jnp.where(gy == 0, 0.0, t_s[tr, k, 8:16, :])
            t_s[tr, k, 48:56, :] = jnp.where(gy == ny - 1, 0.0, t_s[tr, k, 48:56, :])
        p0 = p0 + (0.3 * t0[1, k] - 0.7 * t0[0, k])
        py = py + (0.3 * t_s[1, k, 8:56, :] - 0.7 * t_s[0, k, 8:56, :])
        pk[...] = py
        px = jnp.concatenate([p0, py[8:40]], axis=1)
        uu = jnp.concatenate([turn(got_w[0:32, :], 127 - RAW - k), u_s[k]], axis=1)
        uu = uu - PRESS * (east(px) - px)
        vv = v_s[k] - PRESS * (pk[1:41, :] - py[0:40])
        tu[k] = uu
        v_s[k] = vv
        level = k.astype(F32)
        su = su + jnp.where(m_e > level, uu, 0.0)
        sv = sv + jnp.where(m_n > level, vv, 0.0)
        return p0, py, su, sv

    zero = lambda *shape: jnp.zeros(shape, F32)
    _, _, su, sv = lax.fori_loop(
        0, levels, trial, (zero(32, 128), zero(48, 256), zero(32, 384), zero(40, 256))
    )
    scale = levels / SUBSTEPS
    fix_u = (scale * te[...] - su) / jnp.maximum(m_e, 1.0)
    fix_v = (scale * tn[...] - sv) / jnp.maximum(m_n, 1.0)

    def flows(k, carry):
        level = k.astype(F32)
        uu = jnp.where(m_e > level, tu[k] + fix_u, 0.0)
        vv = jnp.where(m_n > level, v_s[k] + fix_v, 0.0)
        tu[k] = uu
        v_s[k] = vv
        fu_out[k] = uu[:, 128:384]
        fv_out[k] = vv[8:40]
        sums[k] = vv[8:40, 0:128] + vv[8:40, 128:256]
        return carry

    lax.fori_loop(0, levels, flows, 0)
    sums[levels:12] = jnp.zeros((12 - levels, 32, 128), F32)

    part = zero(8, 128)
    for r in range(3):
        pick = (rows((8, 128)) == r).astype(F32)
        part = part + exact_dot(
            pick, sums[4 * r : 4 * r + 4].reshape(128, 128), ((1,), (1,))
        )
    own_r[...] = part[0:4]

    def share(src, dst, peers, send_to, recv_to):
        copies = []
        for i, peer in enumerate(peers):
            copy = pltpu.make_async_remote_copy(
                src_ref=src, dst_ref=dst.at[i], send_sem=send_to.at[i], recv_sem=recv_to.at[i],
                device_id=at(*peer), device_id_type=MESH_ID,
            )
            copy.start()
            copies.append(copy)
        return copies

    first_share = share(own_r, peer_r, gx_peers, gx_send, gx_recv)

    def tracer_level(turn_index, carry):
        k = levels - 1 - turn_index
        up = jnp.maximum(k - 1, 0)
        level = k.astype(F32)
        w_below, wt, value = carry[0], carry[1:3], carry[3:5]
        fu = tu[k]
        fv = v_s[k]
        div = (fu - west(fu))[:, 128:384] + fv[8:40] - v_s[k, 7:39, :]
        w_top = w_below - div
        kappa = jnp.where(cw > level + 1.0, d_s[k], 0.0)
        new_wt, new_value = [], []
        for tr in range(2):
            own_t = t_s[tr, k, 16:48, :]
            tx = jnp.concatenate([t0[tr, k], own_t], axis=1)
            te1 = east(tx)
            face = (7.0 * (tx + te1) - (west(tx) + east(te1))) * (1.0 / 12.0)
            flux = fu * face
            out = (flux - west(flux))[:, 128:384]
            ty = t_s[tr, k, 8:48, :]
            face = (7.0 * (ty + t_s[tr, k, 9:49, :])
                    - (t_s[tr, k, 7:47, :] + t_s[tr, k, 10:50, :])) * (1.0 / 12.0)
            flux = fv * face
            fyb[...] = flux
            out = out + (flux[8:40] - fyb[7:39, :])
            top = jnp.where(k == 0, own_t, 0.5 * (own_t + t_s[tr, up, 16:48, :]))
            through = w_top * top
            source = jnp.where(cw > level, own_t - DT * (out + (through - wt[tr])), 0.0)
            val = (source + kappa * value[tr]) * inv[k]
            m_out[tr, k] = val
            new_wt.append(through)
            new_value.append(val)
        return (w_top, *new_wt, *new_value)

    lax.fori_loop(0, levels, tracer_level, (zero(32, 256),) * 5)

    def back(k, carry):
        out = []
        for tr in range(2):
            val = m_out[tr, k] + ratio[k] * carry[tr]
            m_out[tr, k] = val
            out.append(val)
        return tuple(out)

    lax.fori_loop(0, levels, back, (zero(32, 256),) * 2)

    for copy in first_share:
        copy.wait()
    total = own_r[...]
    for i in range(nx - 1):
        total = total + peer_r[i]
    all_r[...] = total
    second_share = share(all_r, south_r, gy_peers, gy_send, gy_recv)
    a, b = rows((128, 128)), lanes((128, 128))
    block = (a // 32) == (b // 32)
    upto = jnp.where(jnp.logical_and(block, a <= b), 1.0, 0.0)
    whole = jnp.where(block, 1.0, 0.0)
    total = jnp.concatenate([total, jnp.zeros((4, 128), F32)], axis=0)
    running = exact_dot(total, upto, ((1,), (0,)))
    for copy in second_share:
        copy.wait()
    south = jnp.zeros((4, 128), F32)
    for i in range(ny - 1):
        south = south + jnp.where(gy >= i + 1, south_r[i], 0.0)
    south = jnp.concatenate([south, jnp.zeros((4, 128), F32)], axis=0)
    running = running + exact_dot(south, whole, ((1,), (0,)))
    ov_out[...] = running * (nx * 256 * ny * 32) ** -0.5


def store_kernel(fu, fv, m, h, ov, fu_out, fv_out, m_out, h_out, ov_out, sem):
    copies = [
        pltpu.make_async_copy(a, b, sem.at[i])
        for i, (a, b) in enumerate([(m, m_out), (fu, fu_out), (fv, fv_out), (h, h_out)])
    ]
    for copy in copies:
        copy.start()
    for k in range(ov_out.shape[0]):
        ov_out[k : k + 1, :] = ov[k // 4 : k // 4 + 1, 32 * (k % 4) : 32 * (k % 4) + 32]
    for copy in copies:
        copy.wait()


def solution(mesh):
    nx, ny = mesh.shape["gx"], mesh.shape["gy"]
    vmem, anywhere = pltpu.VMEM, pl.ANY
    dma = pltpu.SemaphoreType.DMA

    def shape(*s):
        return jax.ShapeDtypeStruct(s, F32)

    def per_device(u, v, t, d, surface, depth, wet, count):
        operands = [
            pltpu.with_memory_space_constraint(a, pltpu.HBM)
            for a in (u, v, t, d, surface, depth, wet, count)
        ]

        def buf(*s):
            return vmem(s, F32)

        def ibuf(*s):
            return vmem(s, jnp.int32)

        scratch = [
            buf(5, 80, 384), buf(10, 32, 256), buf(10, 40, 256), buf(10, 32, 256),
            buf(2, 10, 56, 256), ibuf(32, 256), ibuf(32, 256),
            buf(48, 128), buf(48, 128), buf(48, 128), buf(48, 128),
            buf(32, 128), buf(16, 128), buf(32, 128), buf(16, 128), buf(16, 128), buf(16, 128),
            buf(32, 128), buf(32, 128), buf(32, 128), buf(32, 128),
            buf(64, 384), buf(64, 384), buf(64, 384), buf(64, 384),
            buf(32, 384), buf(40, 256), buf(80, 384), buf(32, 384), buf(40, 256),
            buf(10, 32, 384), buf(2, 10, 32, 128), buf(48, 256), buf(10, 32, 256), buf(10, 32, 256),
            buf(12, 32, 128), buf(4, 128), buf(nx - 1, 4, 128), buf(4, 128), buf(ny - 1, 4, 128),
            buf(40, 256),
            dma((8,)), dma((15,)), dma((15,)), dma((nx - 1,)), dma((nx - 1,)),
            dma((ny - 1,)), dma((ny - 1,)),
        ]
        sizes = [(10, 32, 256), (10, 32, 256), (2, 10, 32, 256), (32, 256), (8, 128)]

        def body(*refs):
            step_kernel(*refs, nx=nx, ny=ny)

        held = pl.pallas_call(
            body,
            name="ocean_step",
            out_shape=[pltpu.VMEM(s, F32) for s in sizes],
            in_specs=[pl.BlockSpec(memory_space=anywhere)] * 8,
            out_specs=[pl.BlockSpec(memory_space=vmem)] * 5,
            scratch_shapes=scratch,
            compiler_params=pltpu.CompilerParams(
                collective_id=0, has_side_effects=True, vmem_limit_bytes=32 << 20
            ),
        )(*operands)
        return pl.pallas_call(
            store_kernel,
            name="store_results",
            out_shape=[shape(10, 32, 256), shape(10, 32, 256), shape(2, 10, 32, 256),
                       shape(32, 256), shape(10, 32)],
            in_specs=[pl.BlockSpec(memory_space=anywhere)] * 4 + [pl.BlockSpec(memory_space=vmem)],
            out_specs=[pl.BlockSpec(memory_space=anywhere)] * 4 + [pl.BlockSpec(memory_space=vmem)],
            scratch_shapes=[dma((4,))],
            compiler_params=pltpu.CompilerParams(vmem_limit_bytes=4 << 20),
        )(*held)

    field, flat = P(None, "gy", "gx"), P("gy", "gx")
    tracer = P(None, None, "gy", "gx")
    return jax.shard_map(
        per_device,
        mesh=mesh,
        in_specs=(field, field, tracer, field, flat, flat, flat, flat),
        out_specs=(field, field, tracer, flat, P(None, "gy")),
        check_vma=False,
    )
```

```python
import jax
import jax.numpy as jnp
from jax import lax
from jax.experimental import pallas as pl
from jax.experimental.pallas import tpu as pltpu
from jax.sharding import PartitionSpec as P

SUBSTEPS = 12
WAVE = 0.5
PRESS = 0.05
DT = 0.5
MESH_ID = pl.DeviceIdType.MESH
F32 = jnp.float32
CW, DP, HT, FE, FN = range(5)
RAW = 80


def lanes(shape):
    return lax.broadcasted_iota(jnp.int32, shape, len(shape) - 1)


def rows(shape):
    return lax.broadcasted_iota(jnp.int32, shape, len(shape) - 2)


def turn(x, by):
    size = x.shape[-1]
    by = by % size if isinstance(by, int) else lax.rem(by + size, size)
    return x if isinstance(by, int) and by == 0 else pltpu.roll(x, by, x.ndim - 1)


def east(x):
    return turn(x, -1)


def west(x):
    return turn(x, 1)


def exact_dot(a, b, dims):
    return lax.dot_general(
        a, b, (dims, ((), ())), precision=lax.Precision.HIGHEST, preferred_element_type=F32
    )


def step_kernel(
    u_in, v_in, t_in, d_in, surface_in, depth_in, wet_in, count_in,
    fu_out, fv_out, m_out, h_out, ov_out,
    ext, u_s, v_s, d_s, t_s, wet_s, count_s,
    pack_e, pack_w, got_w, got_e, got_sw, got_nw, got_se, got_ne, raw_s, raw_n,
    tr_e, tr_w, got_tw, got_te,
    ed, nd, ew, nw, me, mn, gs, te, tn,
    tu, tv, t0, pp, inv, ratio, sums, own_r, peer_r, all_r, south_r, fyb,
    in_sem, send_sem, recv_sem, gx_send, gx_recv, gy_send, gy_recv, gx_greet, gy_greet,
    *, nx, ny,
):
    gx, gy = lax.axis_index("gx"), lax.axis_index("gy")
    levels = u_s.shape[0]

    def at(dx, dy):
        return (lax.rem(gx + dx + nx, nx), gy + dy)

    def exists(dy):
        if dy == 0:
            return None
        return gy + dy < ny if dy > 0 else gy + dy >= 0

    def given(condition, act):
        if condition is None:
            act()
        else:
            pl.when(condition)(act)

    def greet(semaphore, peers):
        for dx, dy in peers:
            given(exists(dy), lambda dx=dx, dy=dy: pl.semaphore_signal(
                semaphore, inc=1, device_id=at(dx, dy), device_id_type=MESH_ID))

    def number(dy):
        return jnp.where(exists(dy), 1, 0)

    south_r[...] = jnp.zeros_like(south_r)

    barrier = pltpu.get_barrier_semaphore()
    greet(barrier, [(1, 0), (-1, 0)] + [(dx, dy) for dy in (1, -1) for dx in (-1, 1, 0)])

    own = (pl.ds(24, 32), pl.ds(128, 256))
    loads = [
        pltpu.make_async_copy(a, b, in_sem.at[i])
        for i, (a, b) in enumerate(
            [
                (wet_in, wet_s),
                (count_in, count_s),
                (depth_in, ext.at[(DP, *own)]),
                (surface_in, ext.at[(HT, *own)]),
                (u_in, u_s),
                (v_in, v_s.at[:, pl.ds(8, 32), :]),
                (t_in, t_s.at[:, :, pl.ds(16, 32), :]),
                (d_in, d_s),
            ]
        )
    ]
    for load in loads:
        load.start()

    @pl.when(gy == 0)
    def _():
        ext[:, 8:24, 128:384] = jnp.zeros((5, 16, 256), F32)
        v_s[:, 0:8, :] = jnp.zeros((levels, 8, 256), F32)
        t_s[:, :, 8:16, :] = jnp.zeros((2, levels, 8, 256), F32)
        got_sw[...] = jnp.zeros_like(got_sw)
        got_se[...] = jnp.zeros_like(got_se)
        raw_s[...] = jnp.zeros_like(raw_s)

    @pl.when(gy == ny - 1)
    def _():
        ext[:, 56:72, 128:384] = jnp.zeros((5, 16, 256), F32)
        t_s[:, :, 48:56, :] = jnp.zeros((2, levels, 8, 256), F32)
        got_nw[...] = jnp.zeros_like(got_nw)
        got_ne[...] = jnp.zeros_like(got_ne)
        raw_n[...] = jnp.zeros_like(raw_n)

    for load in loads[:4]:
        load.wait()
    cw = jnp.where(wet_s[...] > 0, count_s[...], 0).astype(F32)
    ext[CW, 24:56, 128:384] = cw
    m_u = jnp.minimum(cw, east(cw))
    gs[24:56, 128:384] = cw
    gs[56:64, 128:384] = jnp.zeros((8, 256), F32)
    m_v = jnp.minimum(cw, gs[25:57, 128:384])
    loads[4].wait()
    flow = jnp.zeros_like(cw)
    for k in range(levels):
        flow = flow + jnp.where(m_u > k, u_s[k], 0.0)
    flow_e = flow / levels
    ext[FE, 24:56, 128:384] = flow_e
    loads[5].wait()
    flow = jnp.zeros_like(cw)
    for k in range(levels):
        flow = flow + jnp.where(m_v > k, v_s[k, 8:40, :], 0.0)
    flow_n = flow / levels
    ext[FN, 24:56, 128:384] = flow_n

    lane = lanes((32, 128))
    fields = [cw, ext[DP, 24:56, 128:384], ext[HT, 24:56, 128:384], flow_e, flow_n]
    to_e = jnp.zeros((32, 128), F32)
    to_w = jnp.zeros((32, 128), F32)
    for a, field in enumerate(fields):
        here = jnp.logical_and(lane >= 16 * a, lane < 16 * a + 16)
        to_e = jnp.where(here, turn(field[:, 128:], 16 * a - 112), to_e)
        to_w = jnp.where(here, turn(field[:, :128], 16 * a), to_w)
    for k in range(levels):
        to_e = jnp.where(lane == RAW + k, turn(u_s[k, :, 128:], RAW + k - 127), to_e)
    pack_e[0:32, :] = to_e
    pack_w[0:32, :] = to_w
    pack_e[32:48, :] = jnp.zeros((16, 128), F32)
    pack_w[32:48, :] = jnp.zeros((16, 128), F32)
    for k in range(levels):
        pack_e[32 + k : 33 + k, :] = v_s[k, 39:40, 128:256]
        pack_w[32 + k : 33 + k, :] = v_s[k, 39:40, 0:128]

    pl.semaphore_wait(barrier, 2 + 3 * number(1) + 3 * number(-1))

    def remote(i, src, dst, dx, dy):
        return pltpu.make_async_remote_copy(
            src_ref=src, dst_ref=dst, send_sem=send_sem.at[i], recv_sem=recv_sem.at[i],
            device_id=at(dx, dy), device_id_type=MESH_ID,
        )

    wide = pl.ds(128, 256)

    def parcels(first, entries):
        return [(first + i, *entry) for i, entry in enumerate(entries)]

    def start(group):
        for dy in (1, -1, 0):
            ours = [entry for entry in group if entry[4] == dy]
            if ours:
                given(exists(dy), lambda ours=ours: [remote(*e).start() for e in ours] and None)

    def finish(group):
        for dy in (1, -1, 0):
            ours = [entry for entry in group if entry[4] == dy]
            if ours:
                given(exists(-dy), lambda ours=ours: [remote(*e).wait_recv() for e in ours] and None)
                given(exists(dy), lambda ours=ours: [remote(*e).wait_send() for e in ours] and None)

    halo = parcels(0, [
        (pack_e.at[pl.ds(16, 32)], got_sw, 1, 1),
        (pack_w.at[pl.ds(16, 32)], got_se, -1, 1),
        (ext.at[:, pl.ds(40, 16), wide], ext.at[:, pl.ds(8, 16), wide], 0, 1),
        (pack_e.at[pl.ds(16, 16)], raw_s, 0, 1),
        (v_s.at[:, pl.ds(39, 1), :], v_s.at[:, pl.ds(7, 1), :], 0, 1),
        (pack_e.at[pl.ds(0, 16)], got_nw, 1, -1),
        (pack_w.at[pl.ds(0, 16)], got_ne, -1, -1),
        (ext.at[:, pl.ds(24, 16), wide], ext.at[:, pl.ds(56, 16), wide], 0, -1),
        (pack_e.at[pl.ds(0, 16)], raw_n, 0, -1),
        (pack_e, got_w, 1, 0),
        (pack_w, got_e, -1, 0),
    ])
    start(halo)
    greet(gx_greet.at[0], [(1, 0), (-1, 0)])
    greet(gy_greet.at[0], [(0, 1), (0, -1)])

    loads[6].wait()
    to_e = jnp.zeros((32, 128), F32)
    to_w = jnp.zeros((32, 128), F32)
    for tr in range(2):
        for k in range(levels):
            at_lane = 4 * (tr * levels + k)
            first = (at_lane - 2) % 128
            to_e = jnp.where((lane == first) | (lane == first + 1),
                             turn(t_s[tr, k, 16:48, 128:256], at_lane), to_e)
            to_w = jnp.where((lane == at_lane) | (lane == at_lane + 1),
                             turn(t_s[tr, k, 16:48, 0:128], at_lane), to_w)
    tr_e[...] = to_e
    tr_w[...] = to_w
    tracer_halo = parcels(11, [
        (t_s.at[:, :, pl.ds(46, 2), :], t_s.at[:, :, pl.ds(14, 2), :], 0, 1),
        (t_s.at[:, :, pl.ds(16, 2), :], t_s.at[:, :, pl.ds(48, 2), :], 0, -1),
        (tr_e, got_tw, 1, 0),
        (tr_w, got_te, -1, 0),
    ])
    start(tracer_halo)

    py = jnp.zeros_like(cw)
    sv = jnp.zeros_like(cw)
    for k in range(levels):
        py = py + (0.3 * t_s[1, k, 16:48, :] - 0.7 * t_s[0, k, 16:48, :])
        pp[k, 8:40, :] = py
        pp[k, 40:48, :] = jnp.zeros((8, 256), F32)
        vv = v_s[k, 8:40, :] - PRESS * (pp[k, 9:41, :] - py)
        tv[k, 8:40, :] = vv
        sv = sv + jnp.where(m_v > k, vv, 0.0)

    pl.semaphore_wait(gx_greet.at[0], 2)
    greet(gx_greet.at[1], [(2, 0), (-2, 0)])

    loads[7].wait()
    below_kappa = jnp.zeros_like(cw)
    below_ratio = jnp.zeros_like(cw)
    for k in range(levels - 1, -1, -1):
        above = jnp.where(cw > k, d_s[k - 1], 0.0) if k else jnp.zeros_like(cw)
        factor = 1.0 / (1.0 + above + below_kappa - below_kappa * below_ratio)
        below_ratio = above * factor
        inv[k] = factor
        ratio[k] = below_ratio
        below_kappa = above

    pl.semaphore_wait(gx_greet.at[1], 2)
    greet(gx_greet.at[2], [(4, 0), (-4, 0)])

    finish(halo)

    lane = lanes((64, 128))
    from_w = jnp.concatenate([got_sw[0:16], got_w[0:32], got_nw[...]], axis=0)
    from_e = jnp.concatenate([got_se[0:16], got_e[0:32], got_ne[...]], axis=0)
    for a in range(5):
        ext[a, 8:72, 0:128] = jnp.where(
            lane < 64, turn(from_e, -16 * a), turn(from_w, 112 - 16 * a)
        )
    cells = ext[CW, 8:72, :]
    ext[CW, 72:80, :] = jnp.zeros((8, 384), F32)
    mask_e = jnp.minimum(cells, east(cells))
    mask_n = jnp.minimum(cells, ext[CW, 9:73, :])
    me[...] = mask_e[16:48]
    mn[...] = mask_n[8:48, 128:384]
    deep = ext[DP, 8:72, :]
    half = 0.5 * WAVE
    ed[...] = jnp.where(mask_e > 0.0, half * (deep + east(deep)), 0.0)
    ew[...] = jnp.where(mask_e > 0.0, WAVE, 0.0)
    ext[DP, 72:80, :] = jnp.zeros((8, 384), F32)
    nd[...] = jnp.where(mask_n > 0.0, half * (deep + ext[DP, 9:73, :]), 0.0)
    nw[...] = jnp.where(mask_n > 0.0, WAVE, 0.0)

    def column_mean(raw, cut):
        hold = jnp.logical_and(lane >= RAW, (lane - RAW).astype(F32) < cut)
        return jnp.sum(jnp.where(hold, raw, 0.0), axis=1, keepdims=True) / levels

    raw_own = jnp.concatenate([raw_s[...], pack_e[0:32], raw_n[...]], axis=0)
    ext[FE, 8:72, 0:128] = jnp.where(
        lane == 127, column_mean(from_w, mask_e[:, 127:128]), ext[FE, 8:72, 0:128]
    )
    ext[FE, 8:72, 256:384] = jnp.where(
        lane == 127, column_mean(raw_own, mask_e[:, 383:384]), ext[FE, 8:72, 256:384]
    )
    for first, tile in ((16, 0), (48, 32)):
        cut = mask_n[first - 8 : first, 128:384]
        total = jnp.zeros_like(cut)
        for k in range(levels):
            total = total + jnp.where(cut > k, v_s[k, tile : tile + 8, :], 0.0)
        ext[FN, first : first + 8, 128:384] = jnp.where(
            rows((8, 256)) == 7, total / levels, ext[FN, first : first + 8, 128:384]
        )
    lane = lanes((16, 128))
    level = rows((16, 128)).astype(F32)
    for line, a, b in ((15, got_se[16:32], got_sw[16:32]), (47, got_e[32:48], got_w[32:48])):
        raw = jnp.where(lane < 64, a, b)
        hold = level < mask_n[line : line + 1, 0:128]
        mean = jnp.sum(jnp.where(hold, raw, 0.0), axis=0, keepdims=True) / levels
        ext[FN, 8 + line : 9 + line, 0:128] = mean

    te[...] = jnp.zeros_like(te)
    tn[...] = jnp.zeros_like(tn)
    gs[...] = jnp.zeros_like(gs)

    def substep(first, last):
        here = slice(8 + first, 8 + last)
        inner = slice(first, last)
        fe = ext[FE, here, :]
        fn = ext[FN, here, :]
        fx = ed[inner, :] * fe
        fy = nd[inner, :] * fn
        gs[here, :] = fy
        height = ext[HT, here, :] - (fx - west(fx) + fy - gs[7 + first : 7 + last, :])
        ext[HT, here, :] = height
        fe = fe - ew[inner, :] * (east(height) - height)
        fn = fn - nw[inner, :] * (ext[HT, 9 + first : 9 + last, :] - height)
        ext[FE, here, :] = fe
        ext[FN, here, :] = fn
        te[...] += fe[16 - first : 48 - first]
        tn[...] += fn[8 - first : 48 - first, 128:384]

    ext[HT, 72:80, :] = jnp.zeros((8, 384), F32)

    def wide_step(_, carry):
        substep(0, 64)
        return carry

    def narrow_step(_, carry):
        substep(8, 56)
        return carry

    lax.fori_loop(0, 5, wide_step, 0)
    pl.semaphore_wait(gx_greet.at[2], 2)
    greet(gx_greet.at[3], [(8, 0), (-8, 0)])
    pl.semaphore_wait(gy_greet.at[0], number(1) + number(-1))
    greet(gy_greet.at[1], [(0, 2), (0, -2)])
    lax.fori_loop(0, SUBSTEPS - 5, narrow_step, 0)

    finish(tracer_halo)
    m_n = mn[...]
    pn = jnp.zeros((8, 256), F32)
    ps = jnp.zeros((8, 256), F32)
    ends = [jnp.zeros((8, 256), F32)] * 2
    for k in range(levels):
        pn = pn + (0.3 * t_s[1, k, 48:56, :] - 0.7 * t_s[0, k, 48:56, :])
        ps = ps + (0.3 * t_s[1, k, 8:16, :] - 0.7 * t_s[0, k, 8:16, :])
        pp[k, 40:48, :] = pn
        pp[k, 0:8, :] = ps
        for i, first in enumerate((0, 32)):
            vv = v_s[k, first : first + 8, :] - PRESS * (
                pp[k, first + 1 : first + 9, :] - pp[k, first : first + 8, :])
            tv[k, first : first + 8, :] = vv
            ends[i] = ends[i] + jnp.where(m_n[first : first + 8] > k, vv, 0.0)
    sv = jnp.concatenate([ends[0], sv[0:24], ends[1]], axis=0)
    scale = levels / SUBSTEPS
    fix_v = (scale * tn[...] - sv) / jnp.maximum(m_n, 1.0)
    for k in range(levels):
        vv = jnp.where(m_n > k, tv[k] + fix_v, 0.0)
        tv[k] = vv
        fv_out[k] = vv[8:40]
        sums[k] = vv[8:40, 0:128] + vv[8:40, 128:256]
    sums[levels:12] = jnp.zeros((12 - levels, 32, 128), F32)

    part = jnp.zeros((8, 128), F32)
    for r in range(3):
        pick = (rows((8, 128)) == r).astype(F32)
        part = part + exact_dot(
            pick, sums[4 * r : 4 * r + 4].reshape(128, 128), ((1,), (1,))
        )
    own_r[...] = part[0:4]

    def share(src, dst, i, peer, send_to, recv_to):
        return pltpu.make_async_remote_copy(
            src_ref=src, dst_ref=dst.at[i], send_sem=send_to.at[i], recv_sem=recv_to.at[i],
            device_id=at(*peer), device_id_type=MESH_ID,
        )

    pl.semaphore_wait(gx_greet.at[3], 2)
    first_share = [share(own_r, peer_r, i, (i + 1, 0), gx_send, gx_recv) for i in range(nx - 1)]
    for copy in first_share:
        copy.start()
    pl.semaphore_wait(gy_greet.at[1], number(2) + number(-2))
    greet(gy_greet.at[2], [(0, -4)])

    h_out[...] = ext[HT, 24:56, 128:384]
    lane = lanes((32, 128))
    both = jnp.where(lane % 4 >= 2, got_tw[...], got_te[...])
    m_e = me[...]
    p0 = jnp.zeros((32, 128), F32)
    su = jnp.zeros((32, 384), F32)
    for k in range(levels):
        for tr in range(2):
            t0[tr, k] = turn(both, -4 * (tr * levels + k))
        p0 = p0 + (0.3 * t0[1, k] - 0.7 * t0[0, k])
        px = jnp.concatenate([p0, pp[k, 8:40, :]], axis=1)
        uu = jnp.concatenate([turn(got_w[0:32, :], 127 - RAW - k), u_s[k]], axis=1)
        uu = uu - PRESS * (east(px) - px)
        tu[k] = uu
        su = su + jnp.where(m_e > k, uu, 0.0)
    fix_u = (scale * te[...] - su) / jnp.maximum(m_e, 1.0)
    for k in range(levels):
        uu = jnp.where(m_e > k, tu[k] + fix_u, 0.0)
        tu[k] = uu
        fu_out[k] = uu[:, 128:384]

    def tracer_level(turn_index, carry):
        k = levels - 1 - turn_index
        up = jnp.maximum(k - 1, 0)
        level = k.astype(F32)
        w_below, wt, value = carry[0], carry[1:3], carry[3:5]
        fu = tu[k]
        fv = tv[k]
        div = (fu - west(fu))[:, 128:384] + fv[8:40] - tv[k, 7:39, :]
        w_top = w_below - div
        kappa = jnp.where(cw > level + 1.0, d_s[k], 0.0)
        new_wt, new_value = [], []
        for tr in range(2):
            own_t = t_s[tr, k, 16:48, :]
            tx = jnp.concatenate([t0[tr, k], own_t], axis=1)
            te1 = east(tx)
            face = (7.0 * (tx + te1) - (west(tx) + east(te1))) * (1.0 / 12.0)
            flux = fu * face
            out = (flux - west(flux))[:, 128:384]
            ty = t_s[tr, k, 8:48, :]
            face = (7.0 * (ty + t_s[tr, k, 9:49, :])
                    - (t_s[tr, k, 7:47, :] + t_s[tr, k, 10:50, :])) * (1.0 / 12.0)
            flux = fv * face
            fyb[...] = flux
            out = out + (flux[8:40] - fyb[7:39, :])
            top = jnp.where(k == 0, own_t, 0.5 * (own_t + t_s[tr, up, 16:48, :]))
            through = w_top * top
            source = jnp.where(cw > level, own_t - DT * (out + (through - wt[tr])), 0.0)
            val = (source + kappa * value[tr]) * inv[k]
            m_out[tr, k] = val
            new_wt.append(through)
            new_value.append(val)
        return (w_top, *new_wt, *new_value)

    zero = jnp.zeros((32, 256), F32)
    lax.fori_loop(0, levels, tracer_level, (zero,) * 5)

    def back(k, carry):
        out = []
        for tr in range(2):
            val = m_out[tr, k] + ratio[k] * carry[tr]
            m_out[tr, k] = val
            out.append(val)
        return tuple(out)

    lax.fori_loop(0, levels, back, (zero,) * 2)

    a, b = rows((128, 128)), lanes((128, 128))
    block = (a // 32) == (b // 32)
    upto = jnp.where(jnp.logical_and(block, a <= b), 1.0, 0.0)
    whole = jnp.where(block, 1.0, 0.0)
    for copy in first_share:
        copy.wait_recv()
    total = own_r[...]
    for i in range(nx - 1):
        total = total + peer_r[i]
    all_r[...] = total
    pl.when(exists(4))(lambda: pl.semaphore_wait(gy_greet.at[2], 1))
    second_share = [share(all_r, south_r, i, (0, i + 1), gy_send, gy_recv) for i in range(ny - 1)]
    for i, copy in enumerate(second_share):
        pl.when(exists(i + 1))(lambda copy=copy: copy.start())
    total = jnp.concatenate([total, jnp.zeros((4, 128), F32)], axis=0)
    running = exact_dot(total, upto, ((1,), (0,)))
    for copy in first_share:
        copy.wait_send()
    for i, copy in enumerate(second_share):
        pl.when(exists(-i - 1))(lambda copy=copy: copy.wait_recv())
    south = jnp.zeros((4, 128), F32)
    for i in range(ny - 1):
        south = south + jnp.where(gy >= i + 1, south_r[i], 0.0)
    south = jnp.concatenate([south, jnp.zeros((4, 128), F32)], axis=0)
    running = (running + exact_dot(south, whole, ((1,), (0,)))) * (nx * 256 * ny * 32) ** -0.5
    for k in range(levels):
        ov_out[k : k + 1, :] = running[k // 4 : k // 4 + 1, 32 * (k % 4) : 32 * (k % 4) + 32]
    for i, copy in enumerate(second_share):
        pl.when(exists(i + 1))(lambda copy=copy: copy.wait_send())


def store_kernel(*refs):
    held, results, sem = refs[:5], refs[5:10], refs[10]
    copies = [
        pltpu.make_async_copy(a, b, sem.at[i]) for i, (a, b) in enumerate(zip(held, results))
    ]
    for copy in copies:
        copy.start()
    for copy in copies:
        copy.wait()


def solution(mesh):
    nx, ny = mesh.shape["gx"], mesh.shape["gy"]
    vmem, anywhere = pltpu.VMEM, pl.ANY
    dma = pltpu.SemaphoreType.DMA

    def shape(*s):
        return jax.ShapeDtypeStruct(s, F32)

    def per_device(u, v, t, d, surface, depth, wet, count):
        operands = [
            pltpu.with_memory_space_constraint(a, pltpu.HBM)
            for a in (u, v, t, d, surface, depth, wet, count)
        ]

        def buf(*s):
            return vmem(s, F32)

        def ibuf(*s):
            return vmem(s, jnp.int32)

        scratch = [
            buf(5, 80, 384), buf(10, 32, 256), buf(10, 40, 256), buf(10, 32, 256),
            buf(2, 10, 56, 256), ibuf(32, 256), ibuf(32, 256),
            buf(48, 128), buf(48, 128), buf(48, 128), buf(48, 128),
            buf(32, 128), buf(16, 128), buf(32, 128), buf(16, 128), buf(16, 128), buf(16, 128),
            buf(32, 128), buf(32, 128), buf(32, 128), buf(32, 128),
            buf(64, 384), buf(64, 384), buf(64, 384), buf(64, 384),
            buf(32, 384), buf(40, 256), buf(80, 384), buf(32, 384), buf(40, 256),
            buf(10, 32, 384), buf(10, 40, 256), buf(2, 10, 32, 128), buf(10, 48, 256), buf(10, 32, 256), buf(10, 32, 256),
            buf(12, 32, 128), buf(4, 128), buf(nx - 1, 4, 128), buf(4, 128), buf(ny - 1, 4, 128),
            buf(40, 256),
            dma((8,)), dma((15,)), dma((15,)), dma((nx - 1,)), dma((nx - 1,)),
            dma((ny - 1,)), dma((ny - 1,)),
            pltpu.SemaphoreType.REGULAR((4,)), pltpu.SemaphoreType.REGULAR((3,)),
        ]
        sizes = [(10, 32, 256), (10, 32, 256), (2, 10, 32, 256), (32, 256), (10, 32)]

        def body(*refs):
            step_kernel(*refs, nx=nx, ny=ny)

        held = pl.pallas_call(
            body,
            name="ocean_step",
            out_shape=[pltpu.VMEM(s, F32) for s in sizes],
            in_specs=[pl.BlockSpec(memory_space=anywhere)] * 8,
            out_specs=[pl.BlockSpec(memory_space=vmem)] * 5,
            scratch_shapes=scratch,
            compiler_params=pltpu.CompilerParams(
                collective_id=0, has_side_effects=True, vmem_limit_bytes=32 << 20
            ),
        )(*operands)
        return pl.pallas_call(
            store_kernel,
            name="store_results",
            out_shape=[shape(10, 32, 256), shape(10, 32, 256), shape(2, 10, 32, 256),
                       shape(32, 256), shape(10, 32)],
            in_specs=[pl.BlockSpec(memory_space=anywhere)] * 5,
            out_specs=[pl.BlockSpec(memory_space=anywhere)] * 5,
            scratch_shapes=[dma((5,))],
            compiler_params=pltpu.CompilerParams(vmem_limit_bytes=4 << 20),
        )(*held)

    field, flat = P(None, "gy", "gx"), P("gy", "gx")
    tracer = P(None, None, "gy", "gx")
    return jax.shard_map(
        per_device,
        mesh=mesh,
        in_specs=(field, field, tracer, field, flat, flat, flat, flat),
        out_specs=(field, field, tracer, flat, P(None, "gy")),
        check_vma=False,
    )
```

```python
import jax
import jax.numpy as jnp
from jax import lax
from jax.experimental import pallas as pl
from jax.experimental.pallas import tpu as pltpu
from jax.sharding import PartitionSpec as P

SUBSTEPS = 12
WAVE = 0.5
PRESS = 0.05
DT = 0.5
MESH_ID = pl.DeviceIdType.MESH
F32 = jnp.float32
CW, DP, HT, FE, FN = range(5)
RAW = 80


def lanes(shape):
    return lax.broadcasted_iota(jnp.int32, shape, len(shape) - 1)


def rows(shape):
    return lax.broadcasted_iota(jnp.int32, shape, len(shape) - 2)


def turn(x, by):
    size = x.shape[-1]
    by = by % size if isinstance(by, int) else lax.rem(by + size, size)
    return x if isinstance(by, int) and by == 0 else pltpu.roll(x, by, x.ndim - 1)


def east(x):
    return turn(x, -1)


def west(x):
    return turn(x, 1)


def exact_dot(a, b, dims):
    return lax.dot_general(
        a, b, (dims, ((), ())), precision=lax.Precision.HIGHEST, preferred_element_type=F32
    )


def step_kernel(
    u_in, v_in, t_in, d_in, surface_in, depth_in, wet_in, count_in,
    fu_out, fv_out, m_out, h_out, ov_out,
    ext, u_s, v_s, d_s, t_s, wet_s, count_s,
    pack_e, pack_w, got_w, got_e, got_sw, got_nw, got_se, got_ne, raw_s, raw_n,
    tr_e, tr_w, got_tw, got_te,
    ed, nd, ew, nw, me, mn, gs, te, tn,
    tu, tv, t0, pp, inv, ratio, sums, own_r, peer_r, all_r, south_r, fyb,
    in_sem, send_sem, recv_sem, gx_send, gx_recv, gy_send, gy_recv, gx_greet, gy_greet,
    *, nx, ny,
):
    gx, gy = lax.axis_index("gx"), lax.axis_index("gy")
    levels = u_s.shape[0]

    def at(dx, dy):
        return (lax.rem(gx + dx + nx, nx), gy + dy)

    core, chip_y, chip_x = lax.rem(gx, 2), lax.rem(lax.div(gx, 2), 4), lax.div(gx, 8)

    def chip_at(dx, dy, other):
        x, y = lax.rem(chip_x + dx, 4), lax.rem(chip_y + dy, 4)
        return (8 * x + 2 * y + (1 - core if other else core), gy)

    beside = [(1, 0), (3, 0), (0, 1), (0, 3)]
    opposite = [(2, 0), (0, 2)]
    offsets = [(dx, dy, other) for dx in (2, 1, 3, 0) for dy in (2, 1, 3, 0) for other in (0, 1)]
    offsets = sorted(offsets[:-2], key=lambda o: -(min(o[0], 4 - o[0]) + min(o[1], 4 - o[1]))) + [(0, 0, 1)]

    def greet_chips(semaphore, chips, cores=(0,)):
        for dx, dy in chips:
            for other in cores:
                pl.semaphore_signal(
                    semaphore, inc=1, device_id=chip_at(dx, dy, other), device_id_type=MESH_ID)

    def exists(dy):
        if dy == 0:
            return None
        return gy + dy < ny if dy > 0 else gy + dy >= 0

    def given(condition, act):
        if condition is None:
            act()
        else:
            pl.when(condition)(act)

    def greet(semaphore, peers):
        for dx, dy in peers:
            given(exists(dy), lambda dx=dx, dy=dy: pl.semaphore_signal(
                semaphore, inc=1, device_id=at(dx, dy), device_id_type=MESH_ID))

    def number(dy):
        return jnp.where(exists(dy), 1, 0)

    south_r[...] = jnp.zeros_like(south_r)

    barrier = pltpu.get_barrier_semaphore()
    greet(barrier, [(dx, dy) for dy in (1, -1) for dx in (-1, 1, 0)] + [(1, 0), (-1, 0)])
    greet_chips(barrier, beside, (0, 1))

    own = (pl.ds(24, 32), pl.ds(128, 256))
    loads = [
        pltpu.make_async_copy(a, b, in_sem.at[i])
        for i, (a, b) in enumerate(
            [
                (wet_in, wet_s),
                (count_in, count_s),
                (depth_in, ext.at[(DP, *own)]),
                (surface_in, ext.at[(HT, *own)]),
                (u_in, u_s),
                (v_in, v_s.at[:, pl.ds(8, 32), :]),
                (t_in, t_s.at[:, :, pl.ds(16, 32), :]),
                (d_in, d_s),
            ]
        )
    ]
    for load in loads:
        load.start()

    @pl.when(gy == 0)
    def _():
        ext[:, 8:24, 128:384] = jnp.zeros((5, 16, 256), F32)
        v_s[:, 0:8, :] = jnp.zeros((levels, 8, 256), F32)
        t_s[:, :, 8:16, :] = jnp.zeros((2, levels, 8, 256), F32)
        got_sw[...] = jnp.zeros_like(got_sw)
        got_se[...] = jnp.zeros_like(got_se)
        raw_s[...] = jnp.zeros_like(raw_s)

    @pl.when(gy == ny - 1)
    def _():
        ext[:, 56:72, 128:384] = jnp.zeros((5, 16, 256), F32)
        t_s[:, :, 48:56, :] = jnp.zeros((2, levels, 8, 256), F32)
        got_nw[...] = jnp.zeros_like(got_nw)
        got_ne[...] = jnp.zeros_like(got_ne)
        raw_n[...] = jnp.zeros_like(raw_n)

    for load in loads[:4]:
        load.wait()
    cw = jnp.where(wet_s[...] > 0, count_s[...], 0).astype(F32)
    ext[CW, 24:56, 128:384] = cw
    m_u = jnp.minimum(cw, east(cw))
    gs[24:56, 128:384] = cw
    gs[56:64, 128:384] = jnp.zeros((8, 256), F32)
    m_v = jnp.minimum(cw, gs[25:57, 128:384])
    loads[4].wait()
    flow = jnp.zeros_like(cw)
    for k in range(levels):
        flow = flow + jnp.where(m_u > k, u_s[k], 0.0)
    flow_e = flow / levels
    ext[FE, 24:56, 128:384] = flow_e
    loads[5].wait()
    flow = jnp.zeros_like(cw)
    for k in range(levels):
        flow = flow + jnp.where(m_v > k, v_s[k, 8:40, :], 0.0)
    flow_n = flow / levels
    ext[FN, 24:56, 128:384] = flow_n

    lane = lanes((32, 128))
    fields = [cw, ext[DP, 24:56, 128:384], ext[HT, 24:56, 128:384], flow_e, flow_n]
    to_e = jnp.zeros((32, 128), F32)
    to_w = jnp.zeros((32, 128), F32)
    for a, field in enumerate(fields):
        here = jnp.logical_and(lane >= 16 * a, lane < 16 * a + 16)
        to_e = jnp.where(here, turn(field[:, 128:], 16 * a - 112), to_e)
        to_w = jnp.where(here, turn(field[:, :128], 16 * a), to_w)
    for k in range(levels):
        to_e = jnp.where(lane == RAW + k, turn(u_s[k, :, 128:], RAW + k - 127), to_e)
    pack_e[0:32, :] = to_e
    pack_w[0:32, :] = to_w
    pack_e[32:48, :] = jnp.zeros((16, 128), F32)
    pack_w[32:48, :] = jnp.zeros((16, 128), F32)
    for k in range(levels):
        pack_e[32 + k : 33 + k, :] = v_s[k, 39:40, 128:256]
        pack_w[32 + k : 33 + k, :] = v_s[k, 39:40, 0:128]

    pl.semaphore_wait(barrier, 10 + 3 * number(1) + 3 * number(-1))

    def remote(i, src, dst, dx, dy):
        return pltpu.make_async_remote_copy(
            src_ref=src, dst_ref=dst, send_sem=send_sem.at[i], recv_sem=recv_sem.at[i],
            device_id=at(dx, dy), device_id_type=MESH_ID,
        )

    wide = pl.ds(128, 256)

    def parcels(first, entries):
        return [(first + i, *entry) for i, entry in enumerate(entries)]

    def start(group):
        for dy in (1, -1, 0):
            ours = [entry for entry in group if entry[4] == dy]
            if ours:
                given(exists(dy), lambda ours=ours: [remote(*e).start() for e in ours] and None)

    def finish(group):
        for dy in (1, -1, 0):
            ours = [entry for entry in group if entry[4] == dy]
            if ours:
                given(exists(-dy), lambda ours=ours: [remote(*e).wait_recv() for e in ours] and None)
                given(exists(dy), lambda ours=ours: [remote(*e).wait_send() for e in ours] and None)

    halo = parcels(0, [
        (pack_e.at[pl.ds(16, 32)], got_sw, 1, 1),
        (pack_w.at[pl.ds(16, 32)], got_se, -1, 1),
        (ext.at[:, pl.ds(40, 16), wide], ext.at[:, pl.ds(8, 16), wide], 0, 1),
        (pack_e.at[pl.ds(16, 16)], raw_s, 0, 1),
        (v_s.at[:, pl.ds(39, 1), :], v_s.at[:, pl.ds(7, 1), :], 0, 1),
        (pack_e.at[pl.ds(0, 16)], got_nw, 1, -1),
        (pack_w.at[pl.ds(0, 16)], got_ne, -1, -1),
        (ext.at[:, pl.ds(24, 16), wide], ext.at[:, pl.ds(56, 16), wide], 0, -1),
        (pack_e.at[pl.ds(0, 16)], raw_n, 0, -1),
        (pack_e, got_w, 1, 0),
        (pack_w, got_e, -1, 0),
    ])
    start(halo)
    greet_chips(gx_greet.at[0], beside)
    greet(gy_greet.at[0], [(0, 1), (0, -1)])

    loads[6].wait()
    to_e = jnp.zeros((32, 128), F32)
    to_w = jnp.zeros((32, 128), F32)
    for tr in range(2):
        for k in range(levels):
            at_lane = 4 * (tr * levels + k)
            first = (at_lane - 2) % 128
            to_e = jnp.where((lane == first) | (lane == first + 1),
                             turn(t_s[tr, k, 16:48, 128:256], at_lane), to_e)
            to_w = jnp.where((lane == at_lane) | (lane == at_lane + 1),
                             turn(t_s[tr, k, 16:48, 0:128], at_lane), to_w)
    tr_e[...] = to_e
    tr_w[...] = to_w
    tracer_halo = parcels(11, [
        (t_s.at[:, :, pl.ds(46, 2), :], t_s.at[:, :, pl.ds(14, 2), :], 0, 1),
        (t_s.at[:, :, pl.ds(16, 2), :], t_s.at[:, :, pl.ds(48, 2), :], 0, -1),
        (tr_e, got_tw, 1, 0),
        (tr_w, got_te, -1, 0),
    ])
    start(tracer_halo)

    py = jnp.zeros_like(cw)
    sv = jnp.zeros_like(cw)
    for k in range(levels):
        py = py + (0.3 * t_s[1, k, 16:48, :] - 0.7 * t_s[0, k, 16:48, :])
        pp[k, 8:40, :] = py
        pp[k, 40:48, :] = jnp.zeros((8, 256), F32)
        vv = v_s[k, 8:40, :] - PRESS * (pp[k, 9:41, :] - py)
        tv[k, 8:40, :] = vv
        sv = sv + jnp.where(m_v > k, vv, 0.0)

    loads[7].wait()
    below_kappa = jnp.zeros_like(cw)
    below_ratio = jnp.zeros_like(cw)
    for k in range(levels - 1, -1, -1):
        above = jnp.where(cw > k, d_s[k - 1], 0.0) if k else jnp.zeros_like(cw)
        factor = 1.0 / (1.0 + above + below_kappa - below_kappa * below_ratio)
        below_ratio = above * factor
        inv[k] = factor
        ratio[k] = below_ratio
        below_kappa = above

    pl.semaphore_wait(gx_greet.at[0], 4)
    greet_chips(gx_greet.at[1], opposite)
    pl.semaphore_wait(gy_greet.at[0], number(1) + number(-1))
    greet(gy_greet.at[1], [(0, 2), (0, -2)])

    finish(halo)

    lane = lanes((64, 128))
    from_w = jnp.concatenate([got_sw[0:16], got_w[0:32], got_nw[...]], axis=0)
    from_e = jnp.concatenate([got_se[0:16], got_e[0:32], got_ne[...]], axis=0)
    for a in range(5):
        ext[a, 8:72, 0:128] = jnp.where(
            lane < 64, turn(from_e, -16 * a), turn(from_w, 112 - 16 * a)
        )
    cells = ext[CW, 8:72, :]
    ext[CW, 72:80, :] = jnp.zeros((8, 384), F32)
    mask_e = jnp.minimum(cells, east(cells))
    mask_n = jnp.minimum(cells, ext[CW, 9:73, :])
    me[...] = mask_e[16:48]
    mn[...] = mask_n[8:48, 128:384]
    deep = ext[DP, 8:72, :]
    half = 0.5 * WAVE
    ed[...] = jnp.where(mask_e > 0.0, half * (deep + east(deep)), 0.0)
    ew[...] = jnp.where(mask_e > 0.0, WAVE, 0.0)
    ext[DP, 72:80, :] = jnp.zeros((8, 384), F32)
    nd[...] = jnp.where(mask_n > 0.0, half * (deep + ext[DP, 9:73, :]), 0.0)
    nw[...] = jnp.where(mask_n > 0.0, WAVE, 0.0)

    def column_mean(raw, cut):
        hold = jnp.logical_and(lane >= RAW, (lane - RAW).astype(F32) < cut)
        return jnp.sum(jnp.where(hold, raw, 0.0), axis=1, keepdims=True) / levels

    raw_own = jnp.concatenate([raw_s[...], pack_e[0:32], raw_n[...]], axis=0)
    ext[FE, 8:72, 0:128] = jnp.where(
        lane == 127, column_mean(from_w, mask_e[:, 127:128]), ext[FE, 8:72, 0:128]
    )
    ext[FE, 8:72, 256:384] = jnp.where(
        lane == 127, column_mean(raw_own, mask_e[:, 383:384]), ext[FE, 8:72, 256:384]
    )
    for first, tile in ((16, 0), (48, 32)):
        cut = mask_n[first - 8 : first, 128:384]
        total = jnp.zeros_like(cut)
        for k in range(levels):
            total = total + jnp.where(cut > k, v_s[k, tile : tile + 8, :], 0.0)
        ext[FN, first : first + 8, 128:384] = jnp.where(
            rows((8, 256)) == 7, total / levels, ext[FN, first : first + 8, 128:384]
        )
    lane = lanes((16, 128))
    level = rows((16, 128)).astype(F32)
    for line, a, b in ((15, got_se[16:32], got_sw[16:32]), (47, got_e[32:48], got_w[32:48])):
        raw = jnp.where(lane < 64, a, b)
        hold = level < mask_n[line : line + 1, 0:128]
        mean = jnp.sum(jnp.where(hold, raw, 0.0), axis=0, keepdims=True) / levels
        ext[FN, 8 + line : 9 + line, 0:128] = mean

    te[...] = jnp.zeros_like(te)
    tn[...] = jnp.zeros_like(tn)
    gs[...] = jnp.zeros_like(gs)

    def substep(first, last):
        here = slice(8 + first, 8 + last)
        inner = slice(first, last)
        fe = ext[FE, here, :]
        fn = ext[FN, here, :]
        fx = ed[inner, :] * fe
        fy = nd[inner, :] * fn
        gs[here, :] = fy
        height = ext[HT, here, :] - (fx - west(fx) + fy - gs[7 + first : 7 + last, :])
        ext[HT, here, :] = height
        fe = fe - ew[inner, :] * (east(height) - height)
        fn = fn - nw[inner, :] * (ext[HT, 9 + first : 9 + last, :] - height)
        ext[FE, here, :] = fe
        ext[FN, here, :] = fn
        te[...] += fe[16 - first : 48 - first]
        tn[...] += fn[8 - first : 48 - first, 128:384]

    ext[HT, 72:80, :] = jnp.zeros((8, 384), F32)

    def wide_step(_, carry):
        substep(0, 64)
        return carry

    def narrow_step(_, carry):
        substep(8, 56)
        return carry

    lax.fori_loop(0, 5, wide_step, 0)
    pl.semaphore_wait(gy_greet.at[1], number(2) + number(-2))
    greet(gy_greet.at[2], [(0, -4)])
    lax.fori_loop(0, SUBSTEPS - 5, narrow_step, 0)

    finish(tracer_halo)
    m_n = mn[...]
    pn = jnp.zeros((8, 256), F32)
    ps = jnp.zeros((8, 256), F32)
    ends = [jnp.zeros((8, 256), F32)] * 2
    for k in range(levels):
        pn = pn + (0.3 * t_s[1, k, 48:56, :] - 0.7 * t_s[0, k, 48:56, :])
        ps = ps + (0.3 * t_s[1, k, 8:16, :] - 0.7 * t_s[0, k, 8:16, :])
        pp[k, 40:48, :] = pn
        pp[k, 0:8, :] = ps
        for i, first in enumerate((0, 32)):
            vv = v_s[k, first : first + 8, :] - PRESS * (
                pp[k, first + 1 : first + 9, :] - pp[k, first : first + 8, :])
            tv[k, first : first + 8, :] = vv
            ends[i] = ends[i] + jnp.where(m_n[first : first + 8] > k, vv, 0.0)
    sv = jnp.concatenate([ends[0], sv[0:24], ends[1]], axis=0)
    scale = levels / SUBSTEPS
    fix_v = (scale * tn[...] - sv) / jnp.maximum(m_n, 1.0)
    for k in range(levels):
        vv = jnp.where(m_n > k, tv[k] + fix_v, 0.0)
        tv[k] = vv
        fv_out[k] = vv[8:40]
        sums[k] = vv[8:40, 0:128] + vv[8:40, 128:256]
    sums[levels:12] = jnp.zeros((12 - levels, 32, 128), F32)

    part = jnp.zeros((8, 128), F32)
    for r in range(3):
        pick = (rows((8, 128)) == r).astype(F32)
        part = part + exact_dot(
            pick, sums[4 * r : 4 * r + 4].reshape(128, 128), ((1,), (1,))
        )
    own_r[...] = part[0:4]

    def share(src, dst, i, peer, send_to, recv_to):
        return pltpu.make_async_remote_copy(
            src_ref=src, dst_ref=dst.at[i], send_sem=send_to.at[i], recv_sem=recv_to.at[i],
            device_id=peer, device_id_type=MESH_ID,
        )

    pl.semaphore_wait(gx_greet.at[1], 2)
    first_share = [
        share(own_r, peer_r, i, chip_at(*offset), gx_send, gx_recv)
        for i, offset in enumerate(offsets)
    ]
    for copy in first_share:
        copy.start()

    h_out[...] = ext[HT, 24:56, 128:384]
    lane = lanes((32, 128))
    both = jnp.where(lane % 4 >= 2, got_tw[...], got_te[...])
    m_e = me[...]
    p0 = jnp.zeros((32, 128), F32)
    su = jnp.zeros((32, 384), F32)
    for k in range(levels):
        for tr in range(2):
            t0[tr, k] = turn(both, -4 * (tr * levels + k))
        p0 = p0 + (0.3 * t0[1, k] - 0.7 * t0[0, k])
        px = jnp.concatenate([p0, pp[k, 8:40, :]], axis=1)
        uu = jnp.concatenate([turn(got_w[0:32, :], 127 - RAW - k), u_s[k]], axis=1)
        uu = uu - PRESS * (east(px) - px)
        tu[k] = uu
        su = su + jnp.where(m_e > k, uu, 0.0)
    fix_u = (scale * te[...] - su) / jnp.maximum(m_e, 1.0)
    for k in range(levels):
        uu = jnp.where(m_e > k, tu[k] + fix_u, 0.0)
        tu[k] = uu
        fu_out[k] = uu[:, 128:384]

    def tracer_level(turn_index, carry):
        k = levels - 1 - turn_index
        up = jnp.maximum(k - 1, 0)
        level = k.astype(F32)
        w_below, wt, value = carry[0], carry[1:3], carry[3:5]
        fu = tu[k]
        fv = tv[k]
        div = (fu - west(fu))[:, 128:384] + fv[8:40] - tv[k, 7:39, :]
        w_top = w_below - div
        kappa = jnp.where(cw > level + 1.0, d_s[k], 0.0)
        new_wt, new_value = [], []
        for tr in range(2):
            own_t = t_s[tr, k, 16:48, :]
            tx = jnp.concatenate([t0[tr, k], own_t], axis=1)
            te1 = east(tx)
            face = (7.0 * (tx + te1) - (west(tx) + east(te1))) * (1.0 / 12.0)
            flux = fu * face
            out = (flux - west(flux))[:, 128:384]
            ty = t_s[tr, k, 8:48, :]
            face = (7.0 * (ty + t_s[tr, k, 9:49, :])
                    - (t_s[tr, k, 7:47, :] + t_s[tr, k, 10:50, :])) * (1.0 / 12.0)
            flux = fv * face
            fyb[...] = flux
            out = out + (flux[8:40] - fyb[7:39, :])
            top = jnp.where(k == 0, own_t, 0.5 * (own_t + t_s[tr, up, 16:48, :]))
            through = w_top * top
            source = jnp.where(cw > level, own_t - DT * (out + (through - wt[tr])), 0.0)
            val = (source + kappa * value[tr]) * inv[k]
            m_out[tr, k] = val
            new_wt.append(through)
            new_value.append(val)
        return (w_top, *new_wt, *new_value)

    zero = jnp.zeros((32, 256), F32)
    lax.fori_loop(0, levels, tracer_level, (zero,) * 5)

    def back(k, carry):
        out = []
        for tr in range(2):
            val = m_out[tr, k] + ratio[k] * carry[tr]
            m_out[tr, k] = val
            out.append(val)
        return tuple(out)

    lax.fori_loop(0, levels, back, (zero,) * 2)

    a, b = rows((128, 128)), lanes((128, 128))
    block = (a // 32) == (b // 32)
    upto = jnp.where(jnp.logical_and(block, a <= b), 1.0, 0.0)
    whole = jnp.where(block, 1.0, 0.0)
    for copy in first_share:
        copy.wait_recv()
    total = own_r[...]
    for i in range(nx - 1):
        total = total + peer_r[i]
    all_r[...] = total
    pl.when(exists(4))(lambda: pl.semaphore_wait(gy_greet.at[2], 1))
    second_share = [
        share(all_r, south_r, i, at(0, i + 1), gy_send, gy_recv) for i in range(ny - 1)
    ]
    for i, copy in enumerate(second_share):
        pl.when(exists(i + 1))(lambda copy=copy: copy.start())
    total = jnp.concatenate([total, jnp.zeros((4, 128), F32)], axis=0)
    running = exact_dot(total, upto, ((1,), (0,)))
    for copy in first_share:
        copy.wait_send()
    for i, copy in enumerate(second_share):
        pl.when(exists(-i - 1))(lambda copy=copy: copy.wait_recv())
    south = jnp.zeros((4, 128), F32)
    for i in range(ny - 1):
        south = south + jnp.where(gy >= i + 1, south_r[i], 0.0)
    south = jnp.concatenate([south, jnp.zeros((4, 128), F32)], axis=0)
    running = (running + exact_dot(south, whole, ((1,), (0,)))) * (nx * 256 * ny * 32) ** -0.5
    for k in range(levels):
        ov_out[k : k + 1, :] = running[k // 4 : k // 4 + 1, 32 * (k % 4) : 32 * (k % 4) + 32]
    for i, copy in enumerate(second_share):
        pl.when(exists(i + 1))(lambda copy=copy: copy.wait_send())


def store_kernel(*refs):
    held, results, sem = refs[:5], refs[5:10], refs[10]
    copies = [
        pltpu.make_async_copy(a, b, sem.at[i]) for i, (a, b) in enumerate(zip(held, results))
    ]
    for copy in copies:
        copy.start()
    for copy in copies:
        copy.wait()


def solution(mesh):
    nx, ny = mesh.shape["gx"], mesh.shape["gy"]
    vmem, anywhere = pltpu.VMEM, pl.ANY
    dma = pltpu.SemaphoreType.DMA

    def shape(*s):
        return jax.ShapeDtypeStruct(s, F32)

    def per_device(u, v, t, d, surface, depth, wet, count):
        operands = [
            pltpu.with_memory_space_constraint(a, pltpu.HBM)
            for a in (u, v, t, d, surface, depth, wet, count)
        ]

        def buf(*s):
            return vmem(s, F32)

        def ibuf(*s):
            return vmem(s, jnp.int32)

        scratch = [
            buf(5, 80, 384), buf(10, 32, 256), buf(10, 40, 256), buf(10, 32, 256),
            buf(2, 10, 56, 256), ibuf(32, 256), ibuf(32, 256),
            buf(48, 128), buf(48, 128), buf(48, 128), buf(48, 128),
            buf(32, 128), buf(16, 128), buf(32, 128), buf(16, 128), buf(16, 128), buf(16, 128),
            buf(32, 128), buf(32, 128), buf(32, 128), buf(32, 128),
            buf(64, 384), buf(64, 384), buf(64, 384), buf(64, 384),
            buf(32, 384), buf(40, 256), buf(80, 384), buf(32, 384), buf(40, 256),
            buf(10, 32, 384), buf(10, 40, 256), buf(2, 10, 32, 128), buf(10, 48, 256), buf(10, 32, 256), buf(10, 32, 256),
            buf(12, 32, 128), buf(4, 128), buf(nx - 1, 4, 128), buf(4, 128), buf(ny - 1, 4, 128),
            buf(40, 256),
            dma((8,)), dma((15,)), dma((15,)), dma((nx - 1,)), dma((nx - 1,)),
            dma((ny - 1,)), dma((ny - 1,)),
            pltpu.SemaphoreType.REGULAR((2,)), pltpu.SemaphoreType.REGULAR((3,)),
        ]
        sizes = [(10, 32, 256), (10, 32, 256), (2, 10, 32, 256), (32, 256), (10, 32)]

        def body(*refs):
            step_kernel(*refs, nx=nx, ny=ny)

        held = pl.pallas_call(
            body,
            name="ocean_step",
            out_shape=[pltpu.VMEM(s, F32) for s in sizes],
            in_specs=[pl.BlockSpec(memory_space=anywhere)] * 8,
            out_specs=[pl.BlockSpec(memory_space=vmem)] * 5,
            scratch_shapes=scratch,
            compiler_params=pltpu.CompilerParams(
                collective_id=0, has_side_effects=True, vmem_limit_bytes=32 << 20
            ),
        )(*operands)
        return pl.pallas_call(
            store_kernel,
            name="store_results",
            out_shape=[shape(10, 32, 256), shape(10, 32, 256), shape(2, 10, 32, 256),
                       shape(32, 256), shape(10, 32)],
            in_specs=[pl.BlockSpec(memory_space=anywhere)] * 5,
            out_specs=[pl.BlockSpec(memory_space=anywhere)] * 5,
            scratch_shapes=[dma((5,))],
            compiler_params=pltpu.CompilerParams(vmem_limit_bytes=4 << 20),
        )(*held)

    field, flat = P(None, "gy", "gx"), P("gy", "gx")
    tracer = P(None, None, "gy", "gx")
    return jax.shard_map(
        per_device,
        mesh=mesh,
        in_specs=(field, field, tracer, field, flat, flat, flat, flat),
        out_specs=(field, field, tracer, flat, P(None, "gy")),
        check_vma=False,
    )
```

```python
import jax
import jax.numpy as jnp
from jax import lax
from jax.experimental import pallas as pl
from jax.experimental.pallas import tpu as pltpu
from jax.sharding import PartitionSpec as P

SUBSTEPS = 12
WAVE = 0.5
PRESS = 0.05
DT = 0.5
MESH_ID = pl.DeviceIdType.MESH
F32 = jnp.float32
CW, DP, HT, FE, FN = range(5)
RAW = 80


def lanes(shape):
    return lax.broadcasted_iota(jnp.int32, shape, len(shape) - 1)


def rows(shape):
    return lax.broadcasted_iota(jnp.int32, shape, len(shape) - 2)


def turn(x, by):
    size = x.shape[-1]
    by = by % size if isinstance(by, int) else lax.rem(by + size, size)
    return x if isinstance(by, int) and by == 0 else pltpu.roll(x, by, x.ndim - 1)


def east(x):
    return turn(x, -1)


def west(x):
    return turn(x, 1)


def exact_dot(a, b, dims):
    return lax.dot_general(
        a, b, (dims, ((), ())), precision=lax.Precision.HIGHEST, preferred_element_type=F32
    )


def step_kernel(
    u_in, v_in, t_in, d_in, surface_in, depth_in, wet_in, count_in,
    fu_out, fv_out, m_out, h_out, ov_out,
    ext, u_s, v_s, d_s, t_s, wet_s, count_s,
    pack_e, pack_w, got_w, got_e, got_sw, got_nw, got_se, got_ne, raw_s, raw_n,
    tr_e, tr_w, got_tw, got_te,
    ed, nd, ew, nw, me, mn, gs, hb, coef, hw,
    tu, tv, t0, pp, inv, ratio, sums, own_r, peer_r, all_r, south_r, fyb,
    in_sem, send_sem, recv_sem, gx_send, gx_recv, gy_send, gy_recv, gx_greet, gy_greet,
    *, nx, ny,
):
    gx, gy = lax.axis_index("gx"), lax.axis_index("gy")
    levels = u_s.shape[0]

    def at(dx, dy):
        return (lax.rem(gx + dx + nx, nx), gy + dy)

    core, chip_y, chip_x = lax.rem(gx, 2), lax.rem(lax.div(gx, 2), 4), lax.div(gx, 8)

    def chip_at(dx, dy, other):
        x, y = lax.rem(chip_x + dx, 4), lax.rem(chip_y + dy, 4)
        return (8 * x + 2 * y + (1 - core if other else core), gy)

    beside = [(1, 0), (3, 0), (0, 1), (0, 3)]
    opposite = [(2, 0), (0, 2)]
    offsets = [(dx, dy, other) for dx in (2, 1, 3, 0) for dy in (2, 1, 3, 0) for other in (0, 1)]
    offsets = sorted(offsets[:-2], key=lambda o: -(min(o[0], 4 - o[0]) + min(o[1], 4 - o[1]))) + [(0, 0, 1)]

    def greet_chips(semaphore, chips, cores=(0,)):
        for dx, dy in chips:
            for other in cores:
                pl.semaphore_signal(
                    semaphore, inc=1, device_id=chip_at(dx, dy, other), device_id_type=MESH_ID)

    def exists(dy):
        if dy == 0:
            return None
        return gy + dy < ny if dy > 0 else gy + dy >= 0

    def given(condition, act):
        if condition is None:
            act()
        else:
            pl.when(condition)(act)

    def greet(semaphore, peers):
        for dx, dy in peers:
            given(exists(dy), lambda dx=dx, dy=dy: pl.semaphore_signal(
                semaphore, inc=1, device_id=at(dx, dy), device_id_type=MESH_ID))

    def number(dy):
        return jnp.where(exists(dy), 1, 0)

    south_r[...] = jnp.zeros_like(south_r)

    barrier = pltpu.get_barrier_semaphore()
    greet(barrier, [(dx, dy) for dy in (1, -1) for dx in (-1, 1, 0)] + [(1, 0), (-1, 0)])
    greet_chips(barrier, beside, (0, 1))

    own = (pl.ds(24, 32), pl.ds(128, 256))
    loads = [
        pltpu.make_async_copy(a, b, in_sem.at[i])
        for i, (a, b) in enumerate(
            [
                (wet_in, wet_s),
                (count_in, count_s),
                (depth_in, ext.at[(DP, *own)]),
                (surface_in, ext.at[(HT, *own)]),
                (u_in, u_s),
                (v_in, v_s.at[:, pl.ds(8, 32), :]),
                (t_in, t_s.at[:, :, pl.ds(16, 32), :]),
                (d_in, d_s),
            ]
        )
    ]
    for load in loads:
        load.start()

    @pl.when(gy == 0)
    def _():
        ext[:, 8:24, 128:384] = jnp.zeros((5, 16, 256), F32)
        v_s[:, 0:8, :] = jnp.zeros((levels, 8, 256), F32)
        t_s[:, :, 8:16, :] = jnp.zeros((2, levels, 8, 256), F32)
        got_sw[...] = jnp.zeros_like(got_sw)
        got_se[...] = jnp.zeros_like(got_se)
        raw_s[...] = jnp.zeros_like(raw_s)

    @pl.when(gy == ny - 1)
    def _():
        ext[:, 56:72, 128:384] = jnp.zeros((5, 16, 256), F32)
        t_s[:, :, 48:56, :] = jnp.zeros((2, levels, 8, 256), F32)
        got_nw[...] = jnp.zeros_like(got_nw)
        got_ne[...] = jnp.zeros_like(got_ne)
        raw_n[...] = jnp.zeros_like(raw_n)

    for load in loads[:4]:
        load.wait()
    cw = jnp.where(wet_s[...] > 0, count_s[...], 0).astype(F32)
    ext[CW, 24:56, 128:384] = cw
    m_u = jnp.minimum(cw, east(cw))
    gs[24:56, 128:384] = cw
    gs[56:64, 128:384] = jnp.zeros((8, 256), F32)
    m_v = jnp.minimum(cw, gs[25:57, 128:384])
    loads[4].wait()
    flow = jnp.zeros_like(cw)
    for k in range(levels):
        flow = flow + jnp.where(m_u > k, u_s[k], 0.0)
    flow_e = flow / levels
    ext[FE, 24:56, 128:384] = flow_e
    loads[5].wait()
    flow = jnp.zeros_like(cw)
    for k in range(levels):
        flow = flow + jnp.where(m_v > k, v_s[k, 8:40, :], 0.0)
    flow_n = flow / levels
    ext[FN, 24:56, 128:384] = flow_n

    lane = lanes((32, 128))
    fields = [cw, ext[DP, 24:56, 128:384], ext[HT, 24:56, 128:384], flow_e, flow_n]
    to_e = jnp.zeros((32, 128), F32)
    to_w = jnp.zeros((32, 128), F32)
    for a, field in enumerate(fields):
        here = jnp.logical_and(lane >= 16 * a, lane < 16 * a + 16)
        to_e = jnp.where(here, turn(field[:, 128:], 16 * a - 112), to_e)
        to_w = jnp.where(here, turn(field[:, :128], 16 * a), to_w)
    for k in range(levels):
        to_e = jnp.where(lane == RAW + k, turn(u_s[k, :, 128:], RAW + k - 127), to_e)
    pack_e[0:32, :] = to_e
    pack_w[0:32, :] = to_w
    pack_e[32:48, :] = jnp.zeros((16, 128), F32)
    pack_w[32:48, :] = jnp.zeros((16, 128), F32)
    for k in range(levels):
        pack_e[32 + k : 33 + k, :] = v_s[k, 39:40, 128:256]
        pack_w[32 + k : 33 + k, :] = v_s[k, 39:40, 0:128]

    pl.semaphore_wait(barrier, 10 + 3 * number(1) + 3 * number(-1))

    def remote(i, src, dst, dx, dy):
        return pltpu.make_async_remote_copy(
            src_ref=src, dst_ref=dst, send_sem=send_sem.at[i], recv_sem=recv_sem.at[i],
            device_id=at(dx, dy), device_id_type=MESH_ID,
        )

    wide = pl.ds(128, 256)

    def parcels(first, entries):
        return [(first + i, *entry) for i, entry in enumerate(entries)]

    def start(group):
        for dy in (1, -1, 0):
            ours = [entry for entry in group if entry[4] == dy]
            if ours:
                given(exists(dy), lambda ours=ours: [remote(*e).start() for e in ours] and None)

    def finish(group):
        for dy in (1, -1, 0):
            ours = [entry for entry in group if entry[4] == dy]
            if ours:
                given(exists(-dy), lambda ours=ours: [remote(*e).wait_recv() for e in ours] and None)
                given(exists(dy), lambda ours=ours: [remote(*e).wait_send() for e in ours] and None)

    halo = parcels(0, [
        (pack_e.at[pl.ds(16, 32)], got_sw, 1, 1),
        (pack_w.at[pl.ds(16, 32)], got_se, -1, 1),
        (ext.at[:, pl.ds(40, 16), wide], ext.at[:, pl.ds(8, 16), wide], 0, 1),
        (pack_e.at[pl.ds(16, 16)], raw_s, 0, 1),
        (v_s.at[:, pl.ds(39, 1), :], v_s.at[:, pl.ds(7, 1), :], 0, 1),
        (pack_e.at[pl.ds(0, 16)], got_nw, 1, -1),
        (pack_w.at[pl.ds(0, 16)], got_ne, -1, -1),
        (ext.at[:, pl.ds(24, 16), wide], ext.at[:, pl.ds(56, 16), wide], 0, -1),
        (pack_e.at[pl.ds(0, 16)], raw_n, 0, -1),
        (pack_e, got_w, 1, 0),
        (pack_w, got_e, -1, 0),
    ])
    start(halo)
    greet_chips(gx_greet.at[0], beside)
    greet(gy_greet.at[0], [(0, 1), (0, -1)])

    loads[6].wait()
    to_e = jnp.zeros((32, 128), F32)
    to_w = jnp.zeros((32, 128), F32)
    for tr in range(2):
        for k in range(levels):
            at_lane = 4 * (tr * levels + k)
            first = (at_lane - 2) % 128
            to_e = jnp.where((lane == first) | (lane == first + 1),
                             turn(t_s[tr, k, 16:48, 128:256], at_lane), to_e)
            to_w = jnp.where((lane == at_lane) | (lane == at_lane + 1),
                             turn(t_s[tr, k, 16:48, 0:128], at_lane), to_w)
    tr_e[...] = to_e
    tr_w[...] = to_w
    tracer_halo = parcels(11, [
        (t_s.at[:, :, pl.ds(46, 2), :], t_s.at[:, :, pl.ds(14, 2), :], 0, 1),
        (t_s.at[:, :, pl.ds(16, 2), :], t_s.at[:, :, pl.ds(48, 2), :], 0, -1),
        (tr_e, got_tw, 1, 0),
        (tr_w, got_te, -1, 0),
    ])
    start(tracer_halo)

    py = jnp.zeros_like(cw)
    sv = jnp.zeros_like(cw)
    for k in range(levels):
        py = py + (0.3 * t_s[1, k, 16:48, :] - 0.7 * t_s[0, k, 16:48, :])
        pp[k, 8:40, :] = py
        pp[k, 40:48, :] = jnp.zeros((8, 256), F32)
        vv = v_s[k, 8:40, :] - PRESS * (pp[k, 9:41, :] - py)
        tv[k, 8:40, :] = vv
        sv = sv + jnp.where(m_v > k, vv, 0.0)

    loads[7].wait()
    below_kappa = jnp.zeros_like(cw)
    below_ratio = jnp.zeros_like(cw)
    for k in range(levels - 1, -1, -1):
        above = jnp.where(cw > k, d_s[k - 1], 0.0) if k else jnp.zeros_like(cw)
        factor = 1.0 / (1.0 + above + below_kappa - below_kappa * below_ratio)
        below_ratio = above * factor
        inv[k] = factor
        ratio[k] = below_ratio
        below_kappa = above

    pl.semaphore_wait(gx_greet.at[0], 4)
    greet_chips(gx_greet.at[1], opposite)
    pl.semaphore_wait(gy_greet.at[0], number(1) + number(-1))
    greet(gy_greet.at[1], [(0, 2), (0, -2)])

    finish(halo)

    lane = lanes((64, 128))
    from_w = jnp.concatenate([got_sw[0:16], got_w[0:32], got_nw[...]], axis=0)
    from_e = jnp.concatenate([got_se[0:16], got_e[0:32], got_ne[...]], axis=0)
    for a in range(5):
        ext[a, 8:72, 0:128] = jnp.where(
            lane < 64, turn(from_e, -16 * a), turn(from_w, 112 - 16 * a)
        )
    cells = ext[CW, 8:72, :]
    ext[CW, 72:80, :] = jnp.zeros((8, 384), F32)
    mask_e = jnp.minimum(cells, east(cells))
    mask_n = jnp.minimum(cells, ext[CW, 9:73, :])
    me[...] = mask_e[16:48]
    mn[...] = mask_n[8:48, 128:384]
    deep = ext[DP, 8:72, :]
    half = 0.5 * WAVE
    ed[...] = jnp.where(mask_e > 0.0, half * (deep + east(deep)), 0.0)
    ew[...] = jnp.where(mask_e > 0.0, WAVE, 0.0)
    ext[DP, 72:80, :] = jnp.zeros((8, 384), F32)
    nd[...] = jnp.where(mask_n > 0.0, half * (deep + ext[DP, 9:73, :]), 0.0)
    nw[...] = jnp.where(mask_n > 0.0, WAVE, 0.0)

    def column_mean(raw, cut):
        hold = jnp.logical_and(lane >= RAW, (lane - RAW).astype(F32) < cut)
        return jnp.sum(jnp.where(hold, raw, 0.0), axis=1, keepdims=True) / levels

    raw_own = jnp.concatenate([raw_s[...], pack_e[0:32], raw_n[...]], axis=0)
    ext[FE, 8:72, 0:128] = jnp.where(
        lane == 127, column_mean(from_w, mask_e[:, 127:128]), ext[FE, 8:72, 0:128]
    )
    ext[FE, 8:72, 256:384] = jnp.where(
        lane == 127, column_mean(raw_own, mask_e[:, 383:384]), ext[FE, 8:72, 256:384]
    )
    for first, tile in ((16, 0), (48, 32)):
        cut = mask_n[first - 8 : first, 128:384]
        total = jnp.zeros_like(cut)
        for k in range(levels):
            total = total + jnp.where(cut > k, v_s[k, tile : tile + 8, :], 0.0)
        ext[FN, first : first + 8, 128:384] = jnp.where(
            rows((8, 256)) == 7, total / levels, ext[FN, first : first + 8, 128:384]
        )
    lane = lanes((16, 128))
    level = rows((16, 128)).astype(F32)
    for line, a, b in ((15, got_se[16:32], got_sw[16:32]), (47, got_e[32:48], got_w[32:48])):
        raw = jnp.where(lane < 64, a, b)
        hold = level < mask_n[line : line + 1, 0:128]
        mean = jnp.sum(jnp.where(hold, raw, 0.0), axis=0, keepdims=True) / levels
        ext[FN, 8 + line : 9 + line, 0:128] = mean

    tiles = [slice(128 * t, 128 * t + 128) for t in range(3)]
    fx = ed[...] * ext[FE, 8:72, :]
    fy = nd[...] * ext[FN, 8:72, :]
    gs[0:8, :] = jnp.zeros((8, 384), F32)
    gs[8:72, :] = fy
    divergence = fx - west(fx) + fy - gs[7:71, :]
    height = ext[HT, 8:72, :] - divergence
    a_e = WAVE * ed[...]
    a_n = WAVE * nd[...]
    a_w = west(a_e)
    gs[8:72, :] = a_n
    a_s = gs[7:71, :]
    a_0 = a_e + a_w + a_n + a_s
    for t, tile in enumerate(tiles):
        for i, value in enumerate((divergence, a_e, a_w, a_n, a_s, a_0)):
            coef[i, t] = value[:, tile]
        for b in range(2):
            hb[b, t, 0:8, :] = jnp.zeros((8, 128), F32)
            hb[b, t, 72:80, :] = jnp.zeros((8, 128), F32)
        hb[0, t, 8:72, :] = height[:, tile]
        hw[t, 0:48, :] = (SUBSTEPS * 1.0) * height[8:56, tile]
        hw[t, 48:56, :] = jnp.zeros((8, 128), F32)
    lane = lanes((8, 128))

    def substep(old, weight, first, last, final=False):
        new = 1 - old
        for at_row in range(first, last, 8):
            here, inner = slice(8 + at_row, 16 + at_row), slice(at_row, at_row + 8)
            north, south = slice(9 + at_row, 17 + at_row), slice(7 + at_row, 15 + at_row)
            h = [hb[old, t, here, :] for t in range(3)]
            to_w = [pltpu.roll(x, 127, 1) for x in h]
            to_e = [pltpu.roll(x, 1, 1) for x in h]
            for t in range(3):
                h_e = jnp.where(lane == 127, to_w[(t + 1) % 3], to_w[t])
                h_w = jnp.where(lane == 0, to_e[(t + 2) % 3], to_e[t])
                change = (
                    (coef[1, t, inner, :] * h_e + coef[2, t, inner, :] * h_w)
                    + (coef[3, t, inner, :] * hb[old, t, north, :]
                       + coef[4, t, inner, :] * hb[old, t, south, :])
                    - coef[5, t, inner, :] * h[t]
                )
                div = coef[0, t, inner, :] - change
                value = h[t] - div
                if not final:
                    coef[0, t, inner, :] = div
                hb[new, t, here, :] = value
                if 8 <= at_row < 56:
                    hw[t, at_row - 8 : at_row, :] += weight * value

    for step in range(2, 6):
        substep(step % 2, SUBSTEPS + 1.0 - step, 0, 64)
    pl.semaphore_wait(gy_greet.at[1], number(2) + number(-2))
    greet(gy_greet.at[2], [(0, -4)])
    for step in range(6, SUBSTEPS + 1):
        substep(step % 2, SUBSTEPS + 1.0 - step, 8, 56, step == SUBSTEPS)

    finish(tracer_halo)
    m_n = mn[...]
    pn = jnp.zeros((8, 256), F32)
    ps = jnp.zeros((8, 256), F32)
    ends = [jnp.zeros((8, 256), F32)] * 2
    for k in range(levels):
        pn = pn + (0.3 * t_s[1, k, 48:56, :] - 0.7 * t_s[0, k, 48:56, :])
        ps = ps + (0.3 * t_s[1, k, 8:16, :] - 0.7 * t_s[0, k, 8:16, :])
        pp[k, 40:48, :] = pn
        pp[k, 0:8, :] = ps
        for i, first in enumerate((0, 32)):
            vv = v_s[k, first : first + 8, :] - PRESS * (
                pp[k, first + 1 : first + 9, :] - pp[k, first : first + 8, :])
            tv[k, first : first + 8, :] = vv
            ends[i] = ends[i] + jnp.where(m_n[first : first + 8] > k, vv, 0.0)
    sv = jnp.concatenate([ends[0], sv[0:24], ends[1]], axis=0)
    scale = levels / SUBSTEPS
    wide_n = [hw[t, 0:40, :] for t in (1, 2)]
    next_n = [hw[t, 1:41, :] for t in (1, 2)]
    step_n = jnp.concatenate([b - a for a, b in zip(wide_n, next_n)], axis=1)
    sum_n = SUBSTEPS * ext[FN, 16:56, 128:384] - nw[8:48, 128:384] * step_n
    fix_v = (scale * sum_n - sv) / jnp.maximum(m_n, 1.0)
    for k in range(levels):
        vv = jnp.where(m_n > k, tv[k] + fix_v, 0.0)
        tv[k] = vv
        fv_out[k] = vv[8:40]
        sums[k] = vv[8:40, 0:128] + vv[8:40, 128:256]
    sums[levels:12] = jnp.zeros((12 - levels, 32, 128), F32)

    part = jnp.zeros((8, 128), F32)
    for r in range(3):
        pick = (rows((8, 128)) == r).astype(F32)
        part = part + exact_dot(
            pick, sums[4 * r : 4 * r + 4].reshape(128, 128), ((1,), (1,))
        )
    own_r[...] = part[0:4]

    def share(src, dst, i, peer, send_to, recv_to):
        return pltpu.make_async_remote_copy(
            src_ref=src, dst_ref=dst.at[i], send_sem=send_to.at[i], recv_sem=recv_to.at[i],
            device_id=peer, device_id_type=MESH_ID,
        )

    pl.semaphore_wait(gx_greet.at[1], 2)
    first_share = [
        share(own_r, peer_r, i, chip_at(*offset), gx_send, gx_recv)
        for i, offset in enumerate(offsets)
    ]
    for copy in first_share:
        copy.start()

    h_out[:, 0:128] = hb[1, 1, 24:56, :]
    h_out[:, 128:256] = hb[1, 2, 24:56, :]
    weighted = jnp.concatenate([hw[t, 8:40, :] for t in range(3)], axis=1)
    sum_e = SUBSTEPS * ext[FE, 24:56, :] - ew[16:48, :] * (east(weighted) - weighted)
    lane = lanes((32, 128))
    both = jnp.where(lane % 4 >= 2, got_tw[...], got_te[...])
    m_e = me[...]
    p0 = jnp.zeros((32, 128), F32)
    su = jnp.zeros((32, 384), F32)
    for k in range(levels):
        for tr in range(2):
            t0[tr, k] = turn(both, -4 * (tr * levels + k))
        p0 = p0 + (0.3 * t0[1, k] - 0.7 * t0[0, k])
        px = jnp.concatenate([p0, pp[k, 8:40, :]], axis=1)
        uu = jnp.concatenate([turn(got_w[0:32, :], 127 - RAW - k), u_s[k]], axis=1)
        uu = uu - PRESS * (east(px) - px)
        tu[k] = uu
        su = su + jnp.where(m_e > k, uu, 0.0)
    fix_u = (scale * sum_e - su) / jnp.maximum(m_e, 1.0)
    for k in range(levels):
        uu = jnp.where(m_e > k, tu[k] + fix_u, 0.0)
        tu[k] = uu
        fu_out[k] = uu[:, 128:384]

    def tracer_level(turn_index, carry):
        k = levels - 1 - turn_index
        up = jnp.maximum(k - 1, 0)
        level = k.astype(F32)
        w_below, wt, value = carry[0], carry[1:3], carry[3:5]
        fu = tu[k]
        fv = tv[k]
        div = (fu - west(fu))[:, 128:384] + fv[8:40] - tv[k, 7:39, :]
        w_top = w_below - div
        kappa = jnp.where(cw > level + 1.0, d_s[k], 0.0)
        new_wt, new_value = [], []
        for tr in range(2):
            own_t = t_s[tr, k, 16:48, :]
            tx = jnp.concatenate([t0[tr, k], own_t], axis=1)
            te1 = east(tx)
            face = (7.0 * (tx + te1) - (west(tx) + east(te1))) * (1.0 / 12.0)
            flux = fu * face
            out = (flux - west(flux))[:, 128:384]
            ty = t_s[tr, k, 8:48, :]
            face = (7.0 * (ty + t_s[tr, k, 9:49, :])
                    - (t_s[tr, k, 7:47, :] + t_s[tr, k, 10:50, :])) * (1.0 / 12.0)
            flux = fv * face
            fyb[...] = flux
            out = out + (flux[8:40] - fyb[7:39, :])
            top = jnp.where(k == 0, own_t, 0.5 * (own_t + t_s[tr, up, 16:48, :]))
            through = w_top * top
            source = jnp.where(cw > level, own_t - DT * (out + (through - wt[tr])), 0.0)
            val = (source + kappa * value[tr]) * inv[k]
            m_out[tr, k] = val
            new_wt.append(through)
            new_value.append(val)
        return (w_top, *new_wt, *new_value)

    zero = jnp.zeros((32, 256), F32)
    lax.fori_loop(0, levels, tracer_level, (zero,) * 5)

    def back(k, carry):
        out = []
        for tr in range(2):
            val = m_out[tr, k] + ratio[k] * carry[tr]
            m_out[tr, k] = val
            out.append(val)
        return tuple(out)

    lax.fori_loop(0, levels, back, (zero,) * 2)

    a, b = rows((128, 128)), lanes((128, 128))
    block = (a // 32) == (b // 32)
    upto = jnp.where(jnp.logical_and(block, a <= b), 1.0, 0.0)
    whole = jnp.where(block, 1.0, 0.0)
    for copy in first_share:
        copy.wait_recv()
    total = own_r[...]
    for i in range(nx - 1):
        total = total + peer_r[i]
    all_r[...] = total
    pl.when(exists(4))(lambda: pl.semaphore_wait(gy_greet.at[2], 1))
    second_share = [
        share(all_r, south_r, i, at(0, i + 1), gy_send, gy_recv) for i in range(ny - 1)
    ]
    for i, copy in enumerate(second_share):
        pl.when(exists(i + 1))(lambda copy=copy: copy.start())
    total = jnp.concatenate([total, jnp.zeros((4, 128), F32)], axis=0)
    running = exact_dot(total, upto, ((1,), (0,)))
    for copy in first_share:
        copy.wait_send()
    for i, copy in enumerate(second_share):
        pl.when(exists(-i - 1))(lambda copy=copy: copy.wait_recv())
    south = jnp.zeros((4, 128), F32)
    for i in range(ny - 1):
        south = south + jnp.where(gy >= i + 1, south_r[i], 0.0)
    south = jnp.concatenate([south, jnp.zeros((4, 128), F32)], axis=0)
    running = (running + exact_dot(south, whole, ((1,), (0,)))) * (nx * 256 * ny * 32) ** -0.5
    for k in range(levels):
        ov_out[k : k + 1, :] = running[k // 4 : k // 4 + 1, 32 * (k % 4) : 32 * (k % 4) + 32]
    for i, copy in enumerate(second_share):
        pl.when(exists(i + 1))(lambda copy=copy: copy.wait_send())


def store_kernel(*refs):
    held, results, sem = refs[:5], refs[5:10], refs[10]
    copies = [
        pltpu.make_async_copy(a, b, sem.at[i]) for i, (a, b) in enumerate(zip(held, results))
    ]
    for copy in copies:
        copy.start()
    for copy in copies:
        copy.wait()


def solution(mesh):
    nx, ny = mesh.shape["gx"], mesh.shape["gy"]
    vmem, anywhere = pltpu.VMEM, pl.ANY
    dma = pltpu.SemaphoreType.DMA

    def shape(*s):
        return jax.ShapeDtypeStruct(s, F32)

    def per_device(u, v, t, d, surface, depth, wet, count):
        operands = [
            pltpu.with_memory_space_constraint(a, pltpu.HBM)
            for a in (u, v, t, d, surface, depth, wet, count)
        ]

        def buf(*s):
            return vmem(s, F32)

        def ibuf(*s):
            return vmem(s, jnp.int32)

        scratch = [
            buf(5, 80, 384), buf(10, 32, 256), buf(10, 40, 256), buf(10, 32, 256),
            buf(2, 10, 56, 256), ibuf(32, 256), ibuf(32, 256),
            buf(48, 128), buf(48, 128), buf(48, 128), buf(48, 128),
            buf(32, 128), buf(16, 128), buf(32, 128), buf(16, 128), buf(16, 128), buf(16, 128),
            buf(32, 128), buf(32, 128), buf(32, 128), buf(32, 128),
            buf(64, 384), buf(64, 384), buf(64, 384), buf(64, 384),
            buf(32, 384), buf(40, 256), buf(80, 384), buf(2, 3, 80, 128), buf(6, 3, 64, 128), buf(3, 56, 128),
            buf(10, 32, 384), buf(10, 40, 256), buf(2, 10, 32, 128), buf(10, 48, 256), buf(10, 32, 256), buf(10, 32, 256),
            buf(12, 32, 128), buf(4, 128), buf(nx - 1, 4, 128), buf(4, 128), buf(ny - 1, 4, 128),
            buf(40, 256),
            dma((8,)), dma((15,)), dma((15,)), dma((nx - 1,)), dma((nx - 1,)),
            dma((ny - 1,)), dma((ny - 1,)),
            pltpu.SemaphoreType.REGULAR((2,)), pltpu.SemaphoreType.REGULAR((3,)),
        ]
        sizes = [(10, 32, 256), (10, 32, 256), (2, 10, 32, 256), (32, 256), (10, 32)]

        def body(*refs):
            step_kernel(*refs, nx=nx, ny=ny)

        held = pl.pallas_call(
            body,
            name="ocean_step",
            out_shape=[pltpu.VMEM(s, F32) for s in sizes],
            in_specs=[pl.BlockSpec(memory_space=anywhere)] * 8,
            out_specs=[pl.BlockSpec(memory_space=vmem)] * 5,
            scratch_shapes=scratch,
            compiler_params=pltpu.CompilerParams(
                collective_id=0, has_side_effects=True, vmem_limit_bytes=32 << 20
            ),
        )(*operands)
        return pl.pallas_call(
            store_kernel,
            name="store_results",
            out_shape=[shape(10, 32, 256), shape(10, 32, 256), shape(2, 10, 32, 256),
                       shape(32, 256), shape(10, 32)],
            in_specs=[pl.BlockSpec(memory_space=anywhere)] * 5,
            out_specs=[pl.BlockSpec(memory_space=anywhere)] * 5,
            scratch_shapes=[dma((5,))],
            compiler_params=pltpu.CompilerParams(vmem_limit_bytes=4 << 20),
        )(*held)

    field, flat = P(None, "gy", "gx"), P("gy", "gx")
    tracer = P(None, None, "gy", "gx")
    return jax.shard_map(
        per_device,
        mesh=mesh,
        in_specs=(field, field, tracer, field, flat, flat, flat, flat),
        out_specs=(field, field, tracer, flat, P(None, "gy")),
        check_vma=False,
    )
```

```python
import jax
import jax.numpy as jnp
from jax import lax
from jax.experimental import pallas as pl
from jax.experimental.pallas import tpu as pltpu
from jax.sharding import PartitionSpec as P

SUBSTEPS = 12
WAVE = 0.5
PRESS = 0.05
DT = 0.5
MESH_ID = pl.DeviceIdType.MESH
F32 = jnp.float32
CW, DP, HT, FE, FN = range(5)
RAW = 80


def lanes(shape):
    return lax.broadcasted_iota(jnp.int32, shape, len(shape) - 1)


def rows(shape):
    return lax.broadcasted_iota(jnp.int32, shape, len(shape) - 2)


def turn(x, by):
    size = x.shape[-1]
    by = by % size if isinstance(by, int) else lax.rem(by + size, size)
    return x if isinstance(by, int) and by == 0 else pltpu.roll(x, by, x.ndim - 1)


def east(x):
    return turn(x, -1)


def west(x):
    return turn(x, 1)


def exact_dot(a, b, dims, split_first):
    whole, parts = (b, a) if split_first else (a, b)
    whole = whole.astype(jnp.bfloat16)
    total = None
    for _ in range(3):
        piece = parts.astype(jnp.bfloat16)
        parts = parts - piece.astype(F32)
        pair = (piece, whole) if split_first else (whole, piece)
        term = lax.dot_general(*pair, (dims, ((), ())), preferred_element_type=F32)
        total = term if total is None else total + term
    return total


def step_kernel(
    u_in, v_in, t_in, d_in, surface_in, depth_in, wet_in, count_in,
    fu_out, fv_out, m_out, h_out, ov_out,
    ext, u_s, v_s, d_s, t_s, wet_s, count_s,
    pack_e, pack_w, got_w, got_e, got_sw, got_nw, got_se, got_ne, raw_s, raw_n,
    tr_e, tr_w, got_tw, got_te,
    ed, nd, ew, nw, me, mn, gs, hb, coef, hw,
    tu, tv, t0, pp, inv, ratio, sums, own_r, peer_r, all_r, south_r, fyb,
    in_sem, send_sem, recv_sem, gx_send, gx_recv, gy_send, gy_recv, gx_greet, gy_greet,
    *, nx, ny,
):
    gx, gy = lax.axis_index("gx"), lax.axis_index("gy")
    levels = u_s.shape[0]

    def at(dx, dy):
        return (lax.rem(gx + dx + nx, nx), gy + dy)

    core, chip_y, chip_x = lax.rem(gx, 2), lax.rem(lax.div(gx, 2), 4), lax.div(gx, 8)

    def chip_at(dx, dy, other):
        x, y = lax.rem(chip_x + dx, 4), lax.rem(chip_y + dy, 4)
        return (8 * x + 2 * y + (1 - core if other else core), gy)

    beside = [(1, 0), (3, 0), (0, 1), (0, 3)]
    opposite = [(2, 0), (0, 2)]
    offsets = [(dx, dy, other) for dx in (2, 1, 3, 0) for dy in (2, 1, 3, 0) for other in (0, 1)]
    offsets = sorted(offsets[:-2], key=lambda o: -(min(o[0], 4 - o[0]) + min(o[1], 4 - o[1]))) + [(0, 0, 1)]

    def greet_chips(semaphore, chips, cores=(0,)):
        for dx, dy in chips:
            for other in cores:
                pl.semaphore_signal(
                    semaphore, inc=1, device_id=chip_at(dx, dy, other), device_id_type=MESH_ID)

    def exists(dy):
        if dy == 0:
            return None
        return gy + dy < ny if dy > 0 else gy + dy >= 0

    def given(condition, act):
        if condition is None:
            act()
        else:
            pl.when(condition)(act)

    def greet(semaphore, peers):
        for dx, dy in peers:
            given(exists(dy), lambda dx=dx, dy=dy: pl.semaphore_signal(
                semaphore, inc=1, device_id=at(dx, dy), device_id_type=MESH_ID))

    def number(dy):
        return jnp.where(exists(dy), 1, 0)

    south_r[...] = jnp.zeros_like(south_r)

    barrier = pltpu.get_barrier_semaphore()
    greet(barrier, [(dx, dy) for dy in (1, -1) for dx in (-1, 1, 0)] + [(1, 0), (-1, 0)])
    greet_chips(barrier, beside, (0, 1))

    own = (pl.ds(24, 32), pl.ds(128, 256))
    loads = [
        pltpu.make_async_copy(a, b, in_sem.at[i])
        for i, (a, b) in enumerate(
            [
                (wet_in, wet_s),
                (count_in, count_s),
                (depth_in, ext.at[(DP, *own)]),
                (surface_in, ext.at[(HT, *own)]),
                (u_in, u_s),
                (v_in, v_s.at[:, pl.ds(8, 32), :]),
                (t_in, t_s.at[:, :, pl.ds(16, 32), :]),
                (d_in, d_s),
            ]
        )
    ]
    for load in loads:
        load.start()

    @pl.when(gy == 0)
    def _():
        ext[:, 8:24, 128:384] = jnp.zeros((5, 16, 256), F32)
        v_s[:, 0:8, :] = jnp.zeros((levels, 8, 256), F32)
        t_s[:, :, 8:16, :] = jnp.zeros((2, levels, 8, 256), F32)
        got_sw[...] = jnp.zeros_like(got_sw)
        got_se[...] = jnp.zeros_like(got_se)
        raw_s[...] = jnp.zeros_like(raw_s)

    @pl.when(gy == ny - 1)
    def _():
        ext[:, 56:72, 128:384] = jnp.zeros((5, 16, 256), F32)
        t_s[:, :, 48:56, :] = jnp.zeros((2, levels, 8, 256), F32)
        got_nw[...] = jnp.zeros_like(got_nw)
        got_ne[...] = jnp.zeros_like(got_ne)
        raw_n[...] = jnp.zeros_like(raw_n)

    for load in loads[:4]:
        load.wait()
    cw = jnp.where(wet_s[...] > 0, count_s[...], 0).astype(F32)
    ext[CW, 24:56, 128:384] = cw
    m_u = jnp.minimum(cw, east(cw))
    gs[24:56, 128:384] = cw
    gs[56:64, 128:384] = jnp.zeros((8, 256), F32)
    m_v = jnp.minimum(cw, gs[25:57, 128:384])
    loads[4].wait()
    flow = jnp.zeros_like(cw)
    for k in range(levels):
        flow = flow + jnp.where(m_u > k, u_s[k], 0.0)
    flow_e = flow / levels
    ext[FE, 24:56, 128:384] = flow_e
    loads[5].wait()
    flow = jnp.zeros_like(cw)
    for k in range(levels):
        flow = flow + jnp.where(m_v > k, v_s[k, 8:40, :], 0.0)
    flow_n = flow / levels
    ext[FN, 24:56, 128:384] = flow_n

    lane = lanes((32, 128))
    fields = [cw, ext[DP, 24:56, 128:384], ext[HT, 24:56, 128:384], flow_e, flow_n]
    to_e = jnp.zeros((32, 128), F32)
    to_w = jnp.zeros((32, 128), F32)
    for a, field in enumerate(fields):
        here = jnp.logical_and(lane >= 16 * a, lane < 16 * a + 16)
        to_e = jnp.where(here, turn(field[:, 128:], 16 * a - 112), to_e)
        to_w = jnp.where(here, turn(field[:, :128], 16 * a), to_w)
    for k in range(levels):
        to_e = jnp.where(lane == RAW + k, turn(u_s[k, :, 128:], RAW + k - 127), to_e)
    pack_e[0:32, :] = to_e
    pack_w[0:32, :] = to_w
    pack_e[32:48, :] = jnp.zeros((16, 128), F32)
    pack_w[32:48, :] = jnp.zeros((16, 128), F32)
    for k in range(levels):
        pack_e[32 + k : 33 + k, :] = v_s[k, 39:40, 128:256]
        pack_w[32 + k : 33 + k, :] = v_s[k, 39:40, 0:128]

    pl.semaphore_wait(barrier, 10 + 3 * number(1) + 3 * number(-1))

    def remote(i, src, dst, dx, dy):
        return pltpu.make_async_remote_copy(
            src_ref=src, dst_ref=dst, send_sem=send_sem.at[i], recv_sem=recv_sem.at[i],
            device_id=at(dx, dy), device_id_type=MESH_ID,
        )

    wide = pl.ds(128, 256)

    def parcels(first, entries):
        return [(first + i, *entry) for i, entry in enumerate(entries)]

    def start(group):
        for dy in (1, -1, 0):
            ours = [entry for entry in group if entry[4] == dy]
            if ours:
                given(exists(dy), lambda ours=ours: [remote(*e).start() for e in ours] and None)

    def finish(group):
        for dy in (1, -1, 0):
            ours = [entry for entry in group if entry[4] == dy]
            if ours:
                given(exists(-dy), lambda ours=ours: [remote(*e).wait_recv() for e in ours] and None)
                given(exists(dy), lambda ours=ours: [remote(*e).wait_send() for e in ours] and None)

    halo = parcels(0, [
        (pack_e.at[pl.ds(16, 32)], got_sw, 1, 1),
        (pack_w.at[pl.ds(16, 32)], got_se, -1, 1),
        (ext.at[:, pl.ds(40, 16), wide], ext.at[:, pl.ds(8, 16), wide], 0, 1),
        (pack_e.at[pl.ds(16, 16)], raw_s, 0, 1),
        (v_s.at[:, pl.ds(39, 1), :], v_s.at[:, pl.ds(7, 1), :], 0, 1),
        (pack_e.at[pl.ds(0, 16)], got_nw, 1, -1),
        (pack_w.at[pl.ds(0, 16)], got_ne, -1, -1),
        (ext.at[:, pl.ds(24, 16), wide], ext.at[:, pl.ds(56, 16), wide], 0, -1),
        (pack_e.at[pl.ds(0, 16)], raw_n, 0, -1),
        (pack_e, got_w, 1, 0),
        (pack_w, got_e, -1, 0),
    ])
    start(halo)
    greet_chips(gx_greet.at[0], beside)
    greet(gy_greet.at[0], [(0, 1), (0, -1)])

    loads[6].wait()
    to_e = jnp.zeros((32, 128), F32)
    to_w = jnp.zeros((32, 128), F32)
    for tr in range(2):
        for k in range(levels):
            at_lane = 4 * (tr * levels + k)
            first = (at_lane - 2) % 128
            to_e = jnp.where((lane == first) | (lane == first + 1),
                             turn(t_s[tr, k, 16:48, 128:256], at_lane), to_e)
            to_w = jnp.where((lane == at_lane) | (lane == at_lane + 1),
                             turn(t_s[tr, k, 16:48, 0:128], at_lane), to_w)
    tr_e[...] = to_e
    tr_w[...] = to_w
    tracer_halo = parcels(11, [
        (t_s.at[:, :, pl.ds(46, 2), :], t_s.at[:, :, pl.ds(14, 2), :], 0, 1),
        (t_s.at[:, :, pl.ds(16, 2), :], t_s.at[:, :, pl.ds(48, 2), :], 0, -1),
        (tr_e, got_tw, 1, 0),
        (tr_w, got_te, -1, 0),
    ])
    start(tracer_halo)

    py = jnp.zeros_like(cw)
    sv = jnp.zeros_like(cw)
    for k in range(levels):
        py = py + (0.3 * t_s[1, k, 16:48, :] - 0.7 * t_s[0, k, 16:48, :])
        pp[k, 8:40, :] = py
        pp[k, 40:48, :] = jnp.zeros((8, 256), F32)
        vv = v_s[k, 8:40, :] - PRESS * (pp[k, 9:41, :] - py)
        tv[k, 8:40, :] = vv
        sv = sv + jnp.where(m_v > k, vv, 0.0)

    loads[7].wait()
    below_kappa = jnp.zeros_like(cw)
    below_ratio = jnp.zeros_like(cw)
    for k in range(levels - 1, -1, -1):
        above = jnp.where(cw > k, d_s[k - 1], 0.0) if k else jnp.zeros_like(cw)
        factor = 1.0 / (1.0 + above + below_kappa - below_kappa * below_ratio)
        below_ratio = above * factor
        inv[k] = factor
        ratio[k] = below_ratio
        below_kappa = above

    pl.semaphore_wait(gx_greet.at[0], 4)
    greet_chips(gx_greet.at[1], opposite)
    pl.semaphore_wait(gy_greet.at[0], number(1) + number(-1))
    greet(gy_greet.at[1], [(0, 2), (0, -2)])

    finish(halo)

    lane = lanes((64, 128))
    from_w = jnp.concatenate([got_sw[0:16], got_w[0:32], got_nw[...]], axis=0)
    from_e = jnp.concatenate([got_se[0:16], got_e[0:32], got_ne[...]], axis=0)
    for a in range(5):
        ext[a, 8:72, 0:128] = jnp.where(
            lane < 64, turn(from_e, -16 * a), turn(from_w, 112 - 16 * a)
        )
    cells = ext[CW, 8:72, :]
    ext[CW, 72:80, :] = jnp.zeros((8, 384), F32)
    mask_e = jnp.minimum(cells, east(cells))
    mask_n = jnp.minimum(cells, ext[CW, 9:73, :])
    me[...] = mask_e[16:48]
    mn[...] = mask_n[8:48, 128:384]
    deep = ext[DP, 8:72, :]
    half = 0.5 * WAVE
    ed[...] = jnp.where(mask_e > 0.0, half * (deep + east(deep)), 0.0)
    ew[...] = jnp.where(mask_e > 0.0, WAVE, 0.0)
    ext[DP, 72:80, :] = jnp.zeros((8, 384), F32)
    nd[...] = jnp.where(mask_n > 0.0, half * (deep + ext[DP, 9:73, :]), 0.0)
    nw[...] = jnp.where(mask_n > 0.0, WAVE, 0.0)

    def column_mean(raw, cut):
        hold = jnp.logical_and(lane >= RAW, (lane - RAW).astype(F32) < cut)
        return jnp.sum(jnp.where(hold, raw, 0.0), axis=1, keepdims=True) / levels

    raw_own = jnp.concatenate([raw_s[...], pack_e[0:32], raw_n[...]], axis=0)
    ext[FE, 8:72, 0:128] = jnp.where(
        lane == 127, column_mean(from_w, mask_e[:, 127:128]), ext[FE, 8:72, 0:128]
    )
    ext[FE, 8:72, 256:384] = jnp.where(
        lane == 127, column_mean(raw_own, mask_e[:, 383:384]), ext[FE, 8:72, 256:384]
    )
    for first, tile in ((16, 0), (48, 32)):
        cut = mask_n[first - 8 : first, 128:384]
        total = jnp.zeros_like(cut)
        for k in range(levels):
            total = total + jnp.where(cut > k, v_s[k, tile : tile + 8, :], 0.0)
        ext[FN, first : first + 8, 128:384] = jnp.where(
            rows((8, 256)) == 7, total / levels, ext[FN, first : first + 8, 128:384]
        )
    lane = lanes((16, 128))
    level = rows((16, 128)).astype(F32)
    for line, a, b in ((15, got_se[16:32], got_sw[16:32]), (47, got_e[32:48], got_w[32:48])):
        raw = jnp.where(lane < 64, a, b)
        hold = level < mask_n[line : line + 1, 0:128]
        mean = jnp.sum(jnp.where(hold, raw, 0.0), axis=0, keepdims=True) / levels
        ext[FN, 8 + line : 9 + line, 0:128] = mean

    tiles = [slice(128 * t, 128 * t + 128) for t in range(3)]
    fx = ed[...] * ext[FE, 8:72, :]
    fy = nd[...] * ext[FN, 8:72, :]
    gs[0:8, :] = jnp.zeros((8, 384), F32)
    gs[8:72, :] = fy
    divergence = fx - west(fx) + fy - gs[7:71, :]
    height = ext[HT, 8:72, :] - divergence
    a_e = WAVE * ed[...]
    a_n = WAVE * nd[...]
    a_w = west(a_e)
    gs[8:72, :] = a_n
    a_s = gs[7:71, :]
    a_0 = a_e + a_w + a_n + a_s
    for t, tile in enumerate(tiles):
        for i, value in enumerate((divergence, a_e, a_w, a_n, a_s, a_0)):
            coef[i, t] = value[:, tile]
        for b in range(2):
            hb[b, t, 0:8, :] = jnp.zeros((8, 128), F32)
            hb[b, t, 72:80, :] = jnp.zeros((8, 128), F32)
        hb[0, t, 8:72, :] = height[:, tile]
        hw[t, 0:48, :] = (SUBSTEPS * 1.0) * height[8:56, tile]
        hw[t, 48:56, :] = jnp.zeros((8, 128), F32)
    lane = lanes((8, 128))

    def substep(old, weight, first, last, final=False):
        new = 1 - old
        for at_row in range(first, last, 8):
            here, inner = slice(8 + at_row, 16 + at_row), slice(at_row, at_row + 8)
            north, south = slice(9 + at_row, 17 + at_row), slice(7 + at_row, 15 + at_row)
            h = [hb[old, t, here, :] for t in range(3)]
            to_w = [pltpu.roll(x, 127, 1) for x in h]
            to_e = [pltpu.roll(x, 1, 1) for x in h]
            for t in range(3):
                h_e = jnp.where(lane == 127, to_w[(t + 1) % 3], to_w[t])
                h_w = jnp.where(lane == 0, to_e[(t + 2) % 3], to_e[t])
                change = (
                    (coef[1, t, inner, :] * h_e + coef[2, t, inner, :] * h_w)
                    + (coef[3, t, inner, :] * hb[old, t, north, :]
                       + coef[4, t, inner, :] * hb[old, t, south, :])
                    - coef[5, t, inner, :] * h[t]
                )
                div = coef[0, t, inner, :] - change
                value = h[t] - div
                if not final:
                    coef[0, t, inner, :] = div
                hb[new, t, here, :] = value
                if 8 <= at_row < 56:
                    hw[t, at_row - 8 : at_row, :] += weight * value

    for step in range(2, 6):
        substep(step % 2, SUBSTEPS + 1.0 - step, 0, 64)
    pl.semaphore_wait(gy_greet.at[1], number(2) + number(-2))
    greet(gy_greet.at[2], [(0, -4)])
    for step in range(6, SUBSTEPS + 1):
        substep(step % 2, SUBSTEPS + 1.0 - step, 8, 56, step == SUBSTEPS)

    finish(tracer_halo)
    m_n = mn[...]
    pn = jnp.zeros((8, 256), F32)
    ps = jnp.zeros((8, 256), F32)
    ends = [jnp.zeros((8, 256), F32)] * 2
    for k in range(levels):
        pn = pn + (0.3 * t_s[1, k, 48:56, :] - 0.7 * t_s[0, k, 48:56, :])
        ps = ps + (0.3 * t_s[1, k, 8:16, :] - 0.7 * t_s[0, k, 8:16, :])
        pp[k, 40:48, :] = pn
        pp[k, 0:8, :] = ps
        for i, first in enumerate((0, 32)):
            vv = v_s[k, first : first + 8, :] - PRESS * (
                pp[k, first + 1 : first + 9, :] - pp[k, first : first + 8, :])
            tv[k, first : first + 8, :] = vv
            ends[i] = ends[i] + jnp.where(m_n[first : first + 8] > k, vv, 0.0)
    sv = jnp.concatenate([ends[0], sv[0:24], ends[1]], axis=0)
    scale = levels / SUBSTEPS
    wide_n = [hw[t, 0:40, :] for t in (1, 2)]
    next_n = [hw[t, 1:41, :] for t in (1, 2)]
    step_n = jnp.concatenate([b - a for a, b in zip(wide_n, next_n)], axis=1)
    sum_n = SUBSTEPS * ext[FN, 16:56, 128:384] - nw[8:48, 128:384] * step_n
    fix_v = (scale * sum_n - sv) / jnp.maximum(m_n, 1.0)
    for k in range(levels):
        vv = jnp.where(m_n > k, tv[k] + fix_v, 0.0)
        tv[k] = vv
        fv_out[k] = vv[8:40]
        sums[k] = vv[8:40, 0:128] + vv[8:40, 128:256]
    sums[levels:12] = jnp.zeros((12 - levels, 32, 128), F32)

    part = jnp.zeros((8, 128), F32)
    for r in range(3):
        pick = (rows((8, 128)) == r).astype(F32)
        part = part + exact_dot(
            pick, sums[4 * r : 4 * r + 4].reshape(128, 128), ((1,), (1,)), False
        )
    own_r[...] = part[0:3]

    def share(src, dst, i, peer, send_to, recv_to):
        return pltpu.make_async_remote_copy(
            src_ref=src, dst_ref=dst.at[i], send_sem=send_to.at[i], recv_sem=recv_to.at[i],
            device_id=peer, device_id_type=MESH_ID,
        )

    pl.semaphore_wait(gx_greet.at[1], 2)
    def first_copy(i):
        to = jnp.where(i >= gx, i + 1, i)
        return pltpu.make_async_remote_copy(
            src_ref=own_r, dst_ref=peer_r.at[jnp.where(gx > to, gx - 1, gx)],
            send_sem=gx_send.at[0], recv_sem=gx_recv.at[0], device_id=(to, gy), device_id_type=MESH_ID,
        )

    def all_shares():
        return pltpu.make_async_remote_copy(
            src_ref=peer_r, dst_ref=peer_r, send_sem=gx_send.at[0], recv_sem=gx_recv.at[0],
            device_id=chip_at(0, 0, 1), device_id_type=MESH_ID,
        )

    first_share = [first_copy(i) for i in range(nx - 1)]
    for copy in first_share:
        copy.start()

    h_out[:, 0:128] = hb[1, 1, 24:56, :]
    h_out[:, 128:256] = hb[1, 2, 24:56, :]
    weighted = jnp.concatenate([hw[t, 8:40, :] for t in range(3)], axis=1)
    sum_e = SUBSTEPS * ext[FE, 24:56, :] - ew[16:48, :] * (east(weighted) - weighted)
    lane = lanes((32, 128))
    both = jnp.where(lane % 4 >= 2, got_tw[...], got_te[...])
    m_e = me[...]
    p0 = jnp.zeros((32, 128), F32)
    su = jnp.zeros((32, 384), F32)
    for k in range(levels):
        for tr in range(2):
            t0[tr, k] = turn(both, -4 * (tr * levels + k))
        p0 = p0 + (0.3 * t0[1, k] - 0.7 * t0[0, k])
        px = jnp.concatenate([p0, pp[k, 8:40, :]], axis=1)
        uu = jnp.concatenate([turn(got_w[0:32, :], 127 - RAW - k), u_s[k]], axis=1)
        uu = uu - PRESS * (east(px) - px)
        tu[k] = uu
        su = su + jnp.where(m_e > k, uu, 0.0)
    fix_u = (scale * sum_e - su) / jnp.maximum(m_e, 1.0)
    for k in range(levels):
        uu = jnp.where(m_e > k, tu[k] + fix_u, 0.0)
        tu[k] = uu
        fu_out[k] = uu[:, 128:384]

    def tracer_level(turn_index, carry):
        k = levels - 1 - turn_index
        up = jnp.maximum(k - 1, 0)
        level = k.astype(F32)
        w_below, wt, value = carry[0], carry[1:3], carry[3:5]
        fu = tu[k]
        fv = tv[k]
        div = (fu - west(fu))[:, 128:384] + fv[8:40] - tv[k, 7:39, :]
        w_top = w_below - div
        kappa = jnp.where(cw > level + 1.0, d_s[k], 0.0)
        new_wt, new_value = [], []
        for tr in range(2):
            own_t = t_s[tr, k, 16:48, :]
            tx = jnp.concatenate([t0[tr, k], own_t], axis=1)
            te1 = east(tx)
            face = (7.0 * (tx + te1) - (west(tx) + east(te1))) * (1.0 / 12.0)
            flux = fu * face
            out = (flux - west(flux))[:, 128:384]
            ty = t_s[tr, k, 8:48, :]
            face = (7.0 * (ty + t_s[tr, k, 9:49, :])
                    - (t_s[tr, k, 7:47, :] + t_s[tr, k, 10:50, :])) * (1.0 / 12.0)
            flux = fv * face
            fyb[...] = flux
            out = out + (flux[8:40] - fyb[7:39, :])
            top = jnp.where(k == 0, own_t, 0.5 * (own_t + t_s[tr, up, 16:48, :]))
            through = w_top * top
            source = jnp.where(cw > level, own_t - DT * (out + (through - wt[tr])), 0.0)
            val = (source + kappa * value[tr]) * inv[k]
            m_out[tr, k] = val
            new_wt.append(through)
            new_value.append(val)
        return (w_top, *new_wt, *new_value)

    zero = jnp.zeros((32, 256), F32)
    lax.fori_loop(0, levels, tracer_level, (zero,) * 5)

    def back(k, carry):
        out = []
        for tr in range(2):
            val = m_out[tr, k] + ratio[k] * carry[tr]
            m_out[tr, k] = val
            out.append(val)
        return tuple(out)

    lax.fori_loop(0, levels, back, (zero,) * 2)

    a, b = rows((128, 128)), lanes((128, 128))
    block = (a // 32) == (b // 32)
    upto = jnp.where(jnp.logical_and(block, a <= b), 1.0, 0.0)
    whole = jnp.where(block, 1.0, 0.0)
    all_shares().wait_recv()
    total = own_r[...]
    for i in range(nx - 1):
        total = total + peer_r[i]
    all_r[...] = total
    pl.when(exists(4))(lambda: pl.semaphore_wait(gy_greet.at[2], 1))
    second_share = [
        share(all_r, south_r, i, at(0, i + 1), gy_send, gy_recv) for i in range(ny - 1)
    ]
    for i, copy in enumerate(second_share):
        pl.when(exists(i + 1))(lambda copy=copy: copy.start())
    total = jnp.concatenate([total, jnp.zeros((5, 128), F32)], axis=0)
    running = exact_dot(total, upto, ((1,), (0,)), True)
    all_shares().wait_send()
    for i, copy in enumerate(second_share):
        pl.when(exists(-i - 1))(lambda copy=copy: copy.wait_recv())
    south = jnp.zeros((3, 128), F32)
    for i in range(ny - 1):
        south = south + jnp.where(gy >= i + 1, south_r[i], 0.0)
    south = jnp.concatenate([south, jnp.zeros((5, 128), F32)], axis=0)
    running = (running + exact_dot(south, whole, ((1,), (0,)), True)) * (nx * 256 * ny * 32) ** -0.5
    for k in range(levels):
        ov_out[k : k + 1, :] = running[k // 4 : k // 4 + 1, 32 * (k % 4) : 32 * (k % 4) + 32]
    for i, copy in enumerate(second_share):
        pl.when(exists(i + 1))(lambda copy=copy: copy.wait_send())


def store_kernel(*refs):
    held, results, sem = refs[:5], refs[5:10], refs[10]
    copies = [
        pltpu.make_async_copy(a, b, sem.at[i]) for i, (a, b) in enumerate(zip(held, results))
    ]
    for copy in copies:
        copy.start()
    for copy in copies:
        copy.wait()


def solution(mesh):
    nx, ny = mesh.shape["gx"], mesh.shape["gy"]
    vmem, anywhere = pltpu.VMEM, pl.ANY
    dma = pltpu.SemaphoreType.DMA

    def shape(*s):
        return jax.ShapeDtypeStruct(s, F32)

    def per_device(u, v, t, d, surface, depth, wet, count):
        operands = [
            pltpu.with_memory_space_constraint(a, pltpu.HBM)
            for a in (u, v, t, d, surface, depth, wet, count)
        ]

        def buf(*s):
            return vmem(s, F32)

        def ibuf(*s):
            return vmem(s, jnp.int32)

        scratch = [
            buf(5, 80, 384), buf(10, 32, 256), buf(10, 40, 256), buf(10, 32, 256),
            buf(2, 10, 56, 256), ibuf(32, 256), ibuf(32, 256),
            buf(48, 128), buf(48, 128), buf(48, 128), buf(48, 128),
            buf(32, 128), buf(16, 128), buf(32, 128), buf(16, 128), buf(16, 128), buf(16, 128),
            buf(32, 128), buf(32, 128), buf(32, 128), buf(32, 128),
            buf(64, 384), buf(64, 384), buf(64, 384), buf(64, 384),
            buf(32, 384), buf(40, 256), buf(80, 384), buf(2, 3, 80, 128), buf(6, 3, 64, 128), buf(3, 56, 128),
            buf(10, 32, 384), buf(10, 40, 256), buf(2, 10, 32, 128), buf(10, 48, 256), buf(10, 32, 256), buf(10, 32, 256),
            buf(12, 32, 128), buf(3, 128), buf(nx - 1, 3, 128), buf(3, 128), buf(ny - 1, 3, 128),
            buf(40, 256),
            dma((8,)), dma((15,)), dma((15,)), dma((1,)), dma((1,)),
            dma((ny - 1,)), dma((ny - 1,)),
            pltpu.SemaphoreType.REGULAR((2,)), pltpu.SemaphoreType.REGULAR((3,)),
        ]
        sizes = [(10, 32, 256), (10, 32, 256), (2, 10, 32, 256), (32, 256), (10, 32)]

        def body(*refs):
            step_kernel(*refs, nx=nx, ny=ny)

        held = pl.pallas_call(
            body,
            name="ocean_step",
            out_shape=[pltpu.VMEM(s, F32) for s in sizes],
            in_specs=[pl.BlockSpec(memory_space=anywhere)] * 8,
            out_specs=[pl.BlockSpec(memory_space=vmem)] * 5,
            scratch_shapes=scratch,
            compiler_params=pltpu.CompilerParams(
                collective_id=0, has_side_effects=True, vmem_limit_bytes=32 << 20
            ),
        )(*operands)
        return pl.pallas_call(
            store_kernel,
            name="store_results",
            out_shape=[shape(10, 32, 256), shape(10, 32, 256), shape(2, 10, 32, 256),
                       shape(32, 256), shape(10, 32)],
            in_specs=[pl.BlockSpec(memory_space=anywhere)] * 5,
            out_specs=[pl.BlockSpec(memory_space=anywhere)] * 5,
            scratch_shapes=[dma((5,))],
            compiler_params=pltpu.CompilerParams(vmem_limit_bytes=4 << 20),
        )(*held)

    field, flat = P(None, "gy", "gx"), P("gy", "gx")
    tracer = P(None, None, "gy", "gx")
    return jax.shard_map(
        per_device,
        mesh=mesh,
        in_specs=(field, field, tracer, field, flat, flat, flat, flat),
        out_specs=(field, field, tracer, flat, P(None, "gy")),
        check_vma=False,
    )
```

```python
import jax
import jax.numpy as jnp
from jax import lax
from jax.experimental import pallas as pl
from jax.experimental.pallas import tpu as pltpu
from jax.sharding import PartitionSpec as P

SUBSTEPS = 12
WAVE = 0.5
PRESS = 0.05
DT = 0.5
MESH_ID = pl.DeviceIdType.MESH
F32 = jnp.float32
CW, DP, HT, FE, FN = range(5)
RAW = 80


def lanes(shape):
    return lax.broadcasted_iota(jnp.int32, shape, len(shape) - 1)


def rows(shape):
    return lax.broadcasted_iota(jnp.int32, shape, len(shape) - 2)


def turn(x, by):
    size = x.shape[-1]
    by = by % size if isinstance(by, int) else lax.rem(by + size, size)
    return x if isinstance(by, int) and by == 0 else pltpu.roll(x, by, x.ndim - 1)


def east(x):
    return turn(x, -1)


def west(x):
    return turn(x, 1)


def exact_dot(a, b, dims, split_first):
    whole, parts = (b, a) if split_first else (a, b)
    whole = whole.astype(jnp.bfloat16)
    total = None
    for _ in range(3):
        piece = parts.astype(jnp.bfloat16)
        parts = parts - piece.astype(F32)
        pair = (piece, whole) if split_first else (whole, piece)
        term = lax.dot_general(*pair, (dims, ((), ())), preferred_element_type=F32)
        total = term if total is None else total + term
    return total


def step_kernel(
    u_in, v_in, t_in, d_in, surface_in, depth_in, wet_in, count_in,
    fu_out, fv_out, m_out, h_out, ov_out,
    ext, u_s, v_s, d_s, t_s, cell_s, fe_x, fn_x, fu_b, fv_b, m_b, h_b, tally,
    pack_e, pack_w, got_w, got_e, got_sw, got_nw, got_se, got_ne, raw_s, raw_n,
    tr_e, tr_w, got_tw, got_te,
    ed, nd, ew, nw, me, mn, gs, hb, coef, hw,
    tu, tv, t0, pp, inv, ratio, sums, own_r, peer_r, all_r, south_r, fyb,
    in_sem, send_sem, recv_sem, gx_send, gx_recv, gy_send, gy_recv, gx_greet, gy_greet,
    *, nx, ny,
):
    gx, gy = lax.axis_index("gx"), lax.axis_index("gy")
    levels = u_s.shape[0]

    def at(dx, dy):
        return (lax.rem(gx + dx + nx, nx), gy + dy)

    core, chip_y, chip_x = lax.rem(gx, 2), lax.rem(lax.div(gx, 2), 4), lax.div(gx, 8)

    def chip_at(dx, dy, other):
        x, y = lax.rem(chip_x + dx, 4), lax.rem(chip_y + dy, 4)
        return (8 * x + 2 * y + (1 - core if other else core), gy)

    beside = [(1, 0), (3, 0), (0, 1), (0, 3)]
    opposite = [(2, 0), (0, 2)]
    offsets = [(dx, dy, other) for dx in (2, 1, 3, 0) for dy in (2, 1, 3, 0) for other in (0, 1)]
    offsets = sorted(offsets[:-2], key=lambda o: -(min(o[0], 4 - o[0]) + min(o[1], 4 - o[1]))) + [(0, 0, 1)]

    def greet_chips(semaphore, chips, cores=(0,)):
        for dx, dy in chips:
            for other in cores:
                pl.semaphore_signal(
                    semaphore, inc=1, device_id=chip_at(dx, dy, other), device_id_type=MESH_ID)

    def exists(dy):
        if dy == 0:
            return None
        return gy + dy < ny if dy > 0 else gy + dy >= 0

    def given(condition, act):
        if condition is None:
            act()
        else:
            pl.when(condition)(act)

    def greet(semaphore, peers):
        for dx, dy in peers:
            given(exists(dy), lambda dx=dx, dy=dy: pl.semaphore_signal(
                semaphore, inc=1, device_id=at(dx, dy), device_id_type=MESH_ID))

    def number(dy):
        return jnp.where(exists(dy), 1, 0)

    south_r[...] = jnp.zeros_like(south_r)

    barrier = pltpu.get_barrier_semaphore()
    greet(barrier, [(dx, dy) for dy in (1, -1) for dx in (-1, 1, 0)] + [(1, 0), (-1, 0)])
    greet_chips(barrier, beside, (0, 1))

    own = (pl.ds(24, 32), pl.ds(128, 256))
    loads = [
        pltpu.make_async_copy(a, b, in_sem.at[i])
        for i, a, b in [
            (0, wet_in, cell_s.at[0]),
            (0, count_in, cell_s.at[1]),
            (1, depth_in, ext.at[(DP, *own)]),
            (1, surface_in, ext.at[(HT, *own)]),
            (2, u_in, u_s),
            (3, v_in, v_s.at[:, pl.ds(8, 32), :]),
            (4, t_in, t_s.at[:, :, pl.ds(16, 32), :]),
            (5, d_in, d_s),
        ]
    ]
    for load in loads:
        load.start()

    def arrived(ref, semaphore):
        pltpu.make_async_copy(ref, ref, semaphore).wait()

    @pl.when(gy == 0)
    def _():
        ext[:, 8:24, 128:384] = jnp.zeros((5, 16, 256), F32)
        v_s[:, 0:8, :] = jnp.zeros((levels, 8, 256), F32)
        t_s[:, :, 8:16, :] = jnp.zeros((2, levels, 8, 256), F32)
        got_sw[...] = jnp.zeros_like(got_sw)
        got_se[...] = jnp.zeros_like(got_se)
        raw_s[...] = jnp.zeros_like(raw_s)

    @pl.when(gy == ny - 1)
    def _():
        ext[:, 56:72, 128:384] = jnp.zeros((5, 16, 256), F32)
        t_s[:, :, 48:56, :] = jnp.zeros((2, levels, 8, 256), F32)
        got_nw[...] = jnp.zeros_like(got_nw)
        got_ne[...] = jnp.zeros_like(got_ne)
        raw_n[...] = jnp.zeros_like(raw_n)

    arrived(cell_s, in_sem.at[0])
    arrived(ext.at[(pl.ds(DP, 2), *own)], in_sem.at[1])
    cw = jnp.where(cell_s[0] > 0, cell_s[1], 0).astype(F32)
    ext[CW, 24:56, 128:384] = cw
    m_u = jnp.minimum(cw, east(cw))
    gs[24:56, 128:384] = cw
    gs[56:64, 128:384] = jnp.zeros((8, 256), F32)
    m_v = jnp.minimum(cw, gs[25:57, 128:384])
    loads[4].wait()
    flow = jnp.zeros_like(cw)
    for k in range(levels):
        flow = flow + jnp.where(m_u > k, u_s[k], 0.0)
    flow_e = flow / levels
    ext[FE, 24:56, 128:384] = flow_e
    loads[5].wait()
    flow = jnp.zeros_like(cw)
    for k in range(levels):
        flow = flow + jnp.where(m_v > k, v_s[k, 8:40, :], 0.0)
    flow_n = flow / levels
    ext[FN, 24:56, 128:384] = flow_n

    lane = lanes((32, 128))
    fields = [cw, ext[DP, 24:56, 128:384], ext[HT, 24:56, 128:384], flow_e, flow_n]
    to_e = jnp.zeros((32, 128), F32)
    to_w = jnp.zeros((32, 128), F32)
    for a, field in enumerate(fields):
        here = jnp.logical_and(lane >= 16 * a, lane < 16 * a + 16)
        to_e = jnp.where(here, turn(field[:, 128:], 16 * a - 112), to_e)
        to_w = jnp.where(here, turn(field[:, :128], 16 * a), to_w)
    for k in range(levels):
        to_e = jnp.where(lane == RAW + k, turn(u_s[k, :, 128:], RAW + k - 127), to_e)
    pack_e[0:32, :] = to_e
    pack_w[0:32, :] = to_w
    pack_e[32:48, :] = jnp.zeros((16, 128), F32)
    pack_w[32:48, :] = jnp.zeros((16, 128), F32)
    for k in range(levels):
        pack_e[32 + k : 33 + k, :] = v_s[k, 39:40, 128:256]
        pack_w[32 + k : 33 + k, :] = v_s[k, 39:40, 0:128]

    pl.semaphore_wait(barrier, 10 + 3 * number(1) + 3 * number(-1))

    X, NORTH, SOUTH, LATER = 0, 1, 2, 3
    side = {0: X, 1: NORTH, -1: SOUTH}

    def start(group, later=0):
        def send(src, dst, dx, dy):
            pltpu.make_async_remote_copy(
                src_ref=src, dst_ref=dst,
                send_sem=send_sem.at[side[dy]], recv_sem=recv_sem.at[later + side[-dy]],
                device_id=at(dx, dy), device_id_type=MESH_ID,
            ).start()

        for dy in (1, -1, 0):
            ours = [entry for entry in group if entry[3] == dy]
            given(exists(dy), lambda ours=ours: [send(*e) for e in ours] and None)

    def wait_for(semaphore, count):
        ref = tally.at[pl.ds(0, count // 128), :]
        return lambda: pltpu.make_async_remote_copy(
            src_ref=ref, dst_ref=ref, send_sem=semaphore, recv_sem=semaphore,
            device_id=chip_at(0, 0, 1), device_id_type=MESH_ID,
        ).wait_recv()

    def size(ref):
        total = 1
        for extent in ref.shape:
            total *= extent
        return total

    def finish(group, later=0):
        for dy in (0, 1, -1):
            total = sum(size(entry[0]) for entry in group if entry[3] == dy)
            given(exists(-dy), wait_for(recv_sem.at[later + side[-dy]], total))

    def finish_sends(group):
        for dy in (0, 1, -1):
            total = sum(size(entry[0]) for entry in group if entry[3] == dy)
            given(exists(dy), wait_for(send_sem.at[side[dy]], total))

    wide = pl.ds(128, 256)
    halo = [
        (pack_e.at[pl.ds(16, 32)], got_sw, 1, 1),
        (pack_w.at[pl.ds(16, 32)], got_se, -1, 1),
        (ext.at[:, pl.ds(40, 16), wide], ext.at[:, pl.ds(8, 16), wide], 0, 1),
        (pack_e.at[pl.ds(16, 16)], raw_s, 0, 1),
        (pack_e.at[pl.ds(0, 16)], got_nw, 1, -1),
        (pack_w.at[pl.ds(0, 16)], got_ne, -1, -1),
        (ext.at[:, pl.ds(24, 16), wide], ext.at[:, pl.ds(56, 16), wide], 0, -1),
        (pack_e.at[pl.ds(0, 16)], raw_n, 0, -1),
        (pack_e, got_w, 1, 0),
        (pack_w, got_e, -1, 0),
    ]
    start(halo)
    v_row = pltpu.make_async_remote_copy(
        src_ref=v_s.at[:, pl.ds(39, 1), :], dst_ref=v_s.at[:, pl.ds(7, 1), :],
        send_sem=send_sem.at[3], recv_sem=recv_sem.at[6],
        device_id=at(0, 1), device_id_type=MESH_ID,
    )
    pl.when(exists(1))(v_row.start)
    greet_chips(gx_greet.at[0], beside)
    greet(gy_greet.at[0], [(0, 1), (0, -1)])

    loads[6].wait()
    to_e = jnp.zeros((32, 128), F32)
    to_w = jnp.zeros((32, 128), F32)
    for tr in range(2):
        for k in range(levels):
            at_lane = 4 * (tr * levels + k)
            first = (at_lane - 2) % 128
            to_e = jnp.where((lane == first) | (lane == first + 1),
                             turn(t_s[tr, k, 16:48, 128:256], at_lane), to_e)
            to_w = jnp.where((lane == at_lane) | (lane == at_lane + 1),
                             turn(t_s[tr, k, 16:48, 0:128], at_lane), to_w)
    tr_e[...] = to_e
    tr_w[...] = to_w
    tracer_halo = [
        (t_s.at[:, :, pl.ds(46, 2), :], t_s.at[:, :, pl.ds(14, 2), :], 0, 1),
        (t_s.at[:, :, pl.ds(16, 2), :], t_s.at[:, :, pl.ds(48, 2), :], 0, -1),
        (tr_e, got_tw, 1, 0),
        (tr_w, got_te, -1, 0),
    ]
    start(tracer_halo, LATER)

    py = jnp.zeros_like(cw)
    sv = jnp.zeros_like(cw)
    for k in range(levels):
        py = py + (0.3 * t_s[1, k, 16:48, :] - 0.7 * t_s[0, k, 16:48, :])
        pp[k, 8:40, :] = py
        pp[k, 40:48, :] = jnp.zeros((8, 256), F32)
        vv = v_s[k, 8:40, :] - PRESS * (pp[k, 9:41, :] - py)
        tv[k, 8:40, :] = vv
        sv = sv + jnp.where(m_v > k, vv, 0.0)

    loads[7].wait()
    below_kappa = jnp.zeros_like(cw)
    below_ratio = jnp.zeros_like(cw)
    for k in range(levels - 1, -1, -1):
        above = jnp.where(cw > k, d_s[k - 1], 0.0) if k else jnp.zeros_like(cw)
        factor = 1.0 / (1.0 + above + below_kappa - below_kappa * below_ratio)
        below_ratio = above * factor
        inv[k] = factor
        ratio[k] = below_ratio
        below_kappa = above

    pl.semaphore_wait(gx_greet.at[0], 4)
    greet_chips(gx_greet.at[1], opposite)
    pl.semaphore_wait(gy_greet.at[0], number(1) + number(-1))
    greet(gy_greet.at[1], [(0, 2), (0, -2)])

    finish(halo)
    pl.when(exists(-1))(v_row.wait_recv)

    lane = lanes((64, 128))
    from_w = jnp.concatenate([got_sw[0:16], got_w[0:32], got_nw[...]], axis=0)
    from_e = jnp.concatenate([got_se[0:16], got_e[0:32], got_ne[...]], axis=0)
    edge = [
        jnp.where(lane < 64, turn(from_e, -16 * a), turn(from_w, 112 - 16 * a)) for a in range(5)
    ]
    for a in range(3):
        ext[a, 8:72, 0:128] = edge[a]
    cells = ext[CW, 8:72, :]
    ext[CW, 72:80, :] = jnp.zeros((8, 384), F32)
    mask_e = jnp.minimum(cells, east(cells))
    mask_n = jnp.minimum(cells, ext[CW, 9:73, :])
    me[...] = mask_e[16:48]
    mn[...] = mask_n[8:48, 128:384]
    deep = ext[DP, 8:72, :]
    half = 0.5 * WAVE
    ed[...] = jnp.where(mask_e > 0.0, half * (deep + east(deep)), 0.0)
    ew[...] = jnp.where(mask_e > 0.0, WAVE, 0.0)
    ext[DP, 72:80, :] = jnp.zeros((8, 384), F32)
    nd[...] = jnp.where(mask_n > 0.0, half * (deep + ext[DP, 9:73, :]), 0.0)
    nw[...] = jnp.where(mask_n > 0.0, WAVE, 0.0)

    def column_mean(raw, cut):
        hold = jnp.logical_and(lane >= RAW, (lane - RAW).astype(F32) < cut)
        return jnp.sum(jnp.where(hold, raw, 0.0), axis=1, keepdims=True) / levels

    raw_own = jnp.concatenate([raw_s[...], pack_e[0:32], raw_n[...]], axis=0)
    fe_x[:, 0:128] = jnp.where(lane == 127, column_mean(from_w, mask_e[:, 127:128]), edge[FE])
    fe_x[:, 128:256] = ext[FE, 8:72, 128:256]
    fe_x[:, 256:384] = jnp.where(
        lane == 127, column_mean(raw_own, mask_e[:, 383:384]), ext[FE, 8:72, 256:384]
    )
    fn_x[:, 0:128] = edge[FN]
    fn_x[:, 128:384] = ext[FN, 8:72, 128:384]
    for first, tile in ((8, 0), (40, 32)):
        cut = mask_n[first : first + 8, 128:384]
        total = jnp.zeros_like(cut)
        for k in range(levels):
            total = total + jnp.where(cut > k, v_s[k, tile : tile + 8, :], 0.0)
        fn_x[first : first + 8, 128:384] = jnp.where(
            rows((8, 256)) == 7, total / levels, ext[FN, 8 + first : 16 + first, 128:384]
        )
    lane = lanes((16, 128))
    level = rows((16, 128)).astype(F32)
    for line, a, b in ((15, got_se[16:32], got_sw[16:32]), (47, got_e[32:48], got_w[32:48])):
        raw = jnp.where(lane < 64, a, b)
        hold = level < mask_n[line : line + 1, 0:128]
        mean = jnp.sum(jnp.where(hold, raw, 0.0), axis=0, keepdims=True) / levels
        fn_x[line : line + 1, 0:128] = mean

    tiles = [slice(128 * t, 128 * t + 128) for t in range(3)]
    fx = ed[...] * fe_x[...]
    fy = nd[...] * fn_x[...]
    gs[0:8, :] = jnp.zeros((8, 384), F32)
    gs[8:72, :] = fy
    divergence = fx - west(fx) + fy - gs[7:71, :]
    height = ext[HT, 8:72, :] - divergence
    a_e = WAVE * ed[...]
    a_n = WAVE * nd[...]
    a_w = west(a_e)
    gs[8:72, :] = a_n
    a_s = gs[7:71, :]
    a_0 = a_e + a_w + a_n + a_s
    for t, tile in enumerate(tiles):
        for i, value in enumerate((divergence, a_e, a_w, a_n, a_s, a_0)):
            coef[i, t] = value[:, tile]
        for b in range(2):
            hb[b, t, 0:8, :] = jnp.zeros((8, 128), F32)
            hb[b, t, 72:80, :] = jnp.zeros((8, 128), F32)
        hb[0, t, 8:72, :] = height[:, tile]
        hw[t, 0:48, :] = (SUBSTEPS * 1.0) * height[8:56, tile]
        hw[t, 48:56, :] = jnp.zeros((8, 128), F32)
    lane = lanes((8, 128))

    def substep(old, weight, first, last, final=False):
        new = 1 - old
        for at_row in range(first, last, 8):
            here, inner = slice(8 + at_row, 16 + at_row), slice(at_row, at_row + 8)
            north, south = slice(9 + at_row, 17 + at_row), slice(7 + at_row, 15 + at_row)
            h = [hb[old, t, here, :] for t in range(3)]
            to_w = [pltpu.roll(x, 127, 1) for x in h]
            to_e = [pltpu.roll(x, 1, 1) for x in h]
            for t in range(3):
                h_e = jnp.where(lane == 127, to_w[(t + 1) % 3], to_w[t])
                h_w = jnp.where(lane == 0, to_e[(t + 2) % 3], to_e[t])
                change = (
                    (coef[1, t, inner, :] * h_e + coef[2, t, inner, :] * h_w)
                    + (coef[3, t, inner, :] * hb[old, t, north, :]
                       + coef[4, t, inner, :] * hb[old, t, south, :])
                    - coef[5, t, inner, :] * h[t]
                )
                div = coef[0, t, inner, :] - change
                value = h[t] - div
                if not final:
                    coef[0, t, inner, :] = div
                hb[new, t, here, :] = value
                if 8 <= at_row < 56:
                    hw[t, at_row - 8 : at_row, :] += weight * value

    for step in range(2, 6):
        substep(step % 2, SUBSTEPS + 1.0 - step, 0, 64)
    pl.semaphore_wait(gy_greet.at[1], number(2) + number(-2))
    greet(gy_greet.at[2], [(0, -4)])
    for step in range(6, SUBSTEPS + 1):
        substep(step % 2, SUBSTEPS + 1.0 - step, 8, 56, step == SUBSTEPS)

    finish(tracer_halo, LATER)
    m_n = mn[...]
    pn = jnp.zeros((8, 256), F32)
    ps = jnp.zeros((8, 256), F32)
    ends = [jnp.zeros((8, 256), F32)] * 2
    for k in range(levels):
        pn = pn + (0.3 * t_s[1, k, 48:56, :] - 0.7 * t_s[0, k, 48:56, :])
        ps = ps + (0.3 * t_s[1, k, 8:16, :] - 0.7 * t_s[0, k, 8:16, :])
        pp[k, 40:48, :] = pn
        pp[k, 0:8, :] = ps
        for i, first in enumerate((0, 32)):
            vv = v_s[k, first : first + 8, :] - PRESS * (
                pp[k, first + 1 : first + 9, :] - pp[k, first : first + 8, :])
            tv[k, first : first + 8, :] = vv
            ends[i] = ends[i] + jnp.where(m_n[first : first + 8] > k, vv, 0.0)
    sv = jnp.concatenate([ends[0], sv[0:24], ends[1]], axis=0)
    scale = levels / SUBSTEPS
    wide_n = [hw[t, 0:40, :] for t in (1, 2)]
    next_n = [hw[t, 1:41, :] for t in (1, 2)]
    step_n = jnp.concatenate([b - a for a, b in zip(wide_n, next_n)], axis=1)
    sum_n = SUBSTEPS * fn_x[8:48, 128:384] - nw[8:48, 128:384] * step_n
    fix_v = (scale * sum_n - sv) / jnp.maximum(m_n, 1.0)
    for k in range(levels):
        vv = jnp.where(m_n > k, tv[k] + fix_v, 0.0)
        tv[k] = vv
        fv_b[k] = vv[8:40]
        sums[k] = vv[8:40, 0:128] + vv[8:40, 128:256]
    sums[levels:12] = jnp.zeros((12 - levels, 32, 128), F32)

    part = jnp.zeros((8, 128), F32)
    for r in range(3):
        pick = (rows((8, 128)) == r).astype(F32)
        part = part + exact_dot(
            pick, sums[4 * r : 4 * r + 4].reshape(128, 128), ((1,), (1,)), False
        )
    own_r[...] = part[0:3]

    def share(src, dst, i, peer, send_to, recv_to):
        return pltpu.make_async_remote_copy(
            src_ref=src, dst_ref=dst.at[i], send_sem=send_to.at[i], recv_sem=recv_to.at[i],
            device_id=peer, device_id_type=MESH_ID,
        )

    pl.semaphore_wait(gx_greet.at[1], 2)
    def first_copy(i):
        to = jnp.where(i >= gx, i + 1, i)
        return pltpu.make_async_remote_copy(
            src_ref=own_r, dst_ref=peer_r.at[jnp.where(gx > to, gx - 1, gx)],
            send_sem=gx_send.at[0], recv_sem=gx_recv.at[0], device_id=(to, gy), device_id_type=MESH_ID,
        )

    def all_shares():
        return pltpu.make_async_remote_copy(
            src_ref=peer_r, dst_ref=peer_r, send_sem=gx_send.at[0], recv_sem=gx_recv.at[0],
            device_id=chip_at(0, 0, 1), device_id_type=MESH_ID,
        )

    first_share = [first_copy(i) for i in range(nx - 1)]
    for copy in first_share:
        copy.start()

    h_b[:, 0:128] = hb[1, 1, 24:56, :]
    h_b[:, 128:256] = hb[1, 2, 24:56, :]
    stores = [
        pltpu.make_async_copy(a, b, in_sem.at[i])
        for i, (a, b) in enumerate([(h_b, h_out), (fv_b, fv_out), (fu_b, fu_out), (m_b, m_out)])
    ]
    stores[0].start()
    stores[1].start()
    weighted = jnp.concatenate([hw[t, 8:40, :] for t in range(3)], axis=1)
    sum_e = SUBSTEPS * fe_x[16:48, :] - ew[16:48, :] * (east(weighted) - weighted)
    lane = lanes((32, 128))
    both = jnp.where(lane % 4 >= 2, got_tw[...], got_te[...])
    m_e = me[...]
    p0 = jnp.zeros((32, 128), F32)
    su = jnp.zeros((32, 384), F32)
    for k in range(levels):
        for tr in range(2):
            t0[tr, k] = turn(both, -4 * (tr * levels + k))
        p0 = p0 + (0.3 * t0[1, k] - 0.7 * t0[0, k])
        px = jnp.concatenate([p0, pp[k, 8:40, :]], axis=1)
        uu = jnp.concatenate([turn(got_w[0:32, :], 127 - RAW - k), u_s[k]], axis=1)
        uu = uu - PRESS * (east(px) - px)
        tu[k] = uu
        su = su + jnp.where(m_e > k, uu, 0.0)
    fix_u = (scale * sum_e - su) / jnp.maximum(m_e, 1.0)
    for k in range(levels):
        uu = jnp.where(m_e > k, tu[k] + fix_u, 0.0)
        tu[k] = uu
        fu_b[k] = uu[:, 128:384]
    stores[2].start()

    def tracer_level(turn_index, carry):
        k = levels - 1 - turn_index
        up = jnp.maximum(k - 1, 0)
        level = k.astype(F32)
        w_below, wt, value = carry[0], carry[1:3], carry[3:5]
        fu = tu[k]
        fv = tv[k]
        div = (fu - west(fu))[:, 128:384] + fv[8:40] - tv[k, 7:39, :]
        w_top = w_below - div
        kappa = jnp.where(cw > level + 1.0, d_s[k], 0.0)
        new_wt, new_value = [], []
        for tr in range(2):
            own_t = t_s[tr, k, 16:48, :]
            tx = jnp.concatenate([t0[tr, k], own_t], axis=1)
            te1 = east(tx)
            face = (7.0 * (tx + te1) - (west(tx) + east(te1))) * (1.0 / 12.0)
            flux = fu * face
            out = (flux - west(flux))[:, 128:384]
            ty = t_s[tr, k, 8:48, :]
            face = (7.0 * (ty + t_s[tr, k, 9:49, :])
                    - (t_s[tr, k, 7:47, :] + t_s[tr, k, 10:50, :])) * (1.0 / 12.0)
            flux = fv * face
            fyb[...] = flux
            out = out + (flux[8:40] - fyb[7:39, :])
            top = jnp.where(k == 0, own_t, 0.5 * (own_t + t_s[tr, up, 16:48, :]))
            through = w_top * top
            source = jnp.where(cw > level, own_t - DT * (out + (through - wt[tr])), 0.0)
            val = (source + kappa * value[tr]) * inv[k]
            m_b[tr, k] = val
            new_wt.append(through)
            new_value.append(val)
        return (w_top, *new_wt, *new_value)

    zero = jnp.zeros((32, 256), F32)
    lax.fori_loop(0, levels, tracer_level, (zero,) * 5)

    def back(k, carry):
        out = []
        for tr in range(2):
            val = m_b[tr, k] + ratio[k] * carry[tr]
            m_b[tr, k] = val
            out.append(val)
        return tuple(out)

    lax.fori_loop(0, levels, back, (zero,) * 2)
    stores[3].start()

    a, b = rows((128, 128)), lanes((128, 128))
    block = (a // 32) == (b // 32)
    upto = jnp.where(jnp.logical_and(block, a <= b), 1.0, 0.0)
    whole = jnp.where(block, 1.0, 0.0)
    all_shares().wait_recv()
    total = own_r[...]
    for i in range(nx - 1):
        total = total + peer_r[i]
    all_r[...] = total
    pl.when(exists(4))(lambda: pl.semaphore_wait(gy_greet.at[2], 1))
    second_share = [
        share(all_r, south_r, i, at(0, i + 1), gy_send, gy_recv) for i in range(ny - 1)
    ]
    for i, copy in enumerate(second_share):
        pl.when(exists(i + 1))(lambda copy=copy: copy.start())
    total = jnp.concatenate([total, jnp.zeros((5, 128), F32)], axis=0)
    running = exact_dot(total, upto, ((1,), (0,)), True)
    all_shares().wait_send()
    finish_sends(halo + tracer_halo)
    pl.when(exists(1))(v_row.wait_send)
    for store in stores:
        store.wait()
    for i, copy in enumerate(second_share):
        pl.when(exists(-i - 1))(lambda copy=copy: copy.wait_recv())
    south = jnp.zeros((3, 128), F32)
    for i in range(ny - 1):
        south = south + jnp.where(gy >= i + 1, south_r[i], 0.0)
    south = jnp.concatenate([south, jnp.zeros((5, 128), F32)], axis=0)
    running = (running + exact_dot(south, whole, ((1,), (0,)), True)) * (nx * 256 * ny * 32) ** -0.5
    for k in range(levels):
        ov_out[k : k + 1, :] = running[k // 4 : k // 4 + 1, 32 * (k % 4) : 32 * (k % 4) + 32]
    for i, copy in enumerate(second_share):
        pl.when(exists(i + 1))(lambda copy=copy: copy.wait_send())


def store_kernel(*refs):
    held, results, sem = refs[:5], refs[5:10], refs[10]
    copies = [
        pltpu.make_async_copy(a, b, sem.at[i]) for i, (a, b) in enumerate(zip(held, results))
    ]
    for copy in copies:
        copy.start()
    for copy in copies:
        copy.wait()


def solution(mesh):
    nx, ny = mesh.shape["gx"], mesh.shape["gy"]
    vmem, anywhere = pltpu.VMEM, pl.ANY
    dma = pltpu.SemaphoreType.DMA

    def shape(*s):
        return jax.ShapeDtypeStruct(s, F32)

    def per_device(u, v, t, d, surface, depth, wet, count):
        operands = [
            pltpu.with_memory_space_constraint(a, pltpu.HBM)
            for a in (u, v, t, d, surface, depth, wet, count)
        ]

        def buf(*s):
            return vmem(s, F32)

        def ibuf(*s):
            return vmem(s, jnp.int32)

        scratch = [
            buf(5, 80, 384), buf(10, 32, 256), buf(10, 40, 256), buf(10, 32, 256),
            buf(2, 10, 56, 256), ibuf(2, 32, 256), buf(64, 384), buf(64, 384),
            buf(10, 32, 256), buf(10, 32, 256), buf(2, 10, 32, 256), buf(32, 256), buf(320, 128),
            buf(48, 128), buf(48, 128), buf(48, 128), buf(48, 128),
            buf(32, 128), buf(16, 128), buf(32, 128), buf(16, 128), buf(16, 128), buf(16, 128),
            buf(32, 128), buf(32, 128), buf(32, 128), buf(32, 128),
            buf(64, 384), buf(64, 384), buf(64, 384), buf(64, 384),
            buf(32, 384), buf(40, 256), buf(80, 384), buf(2, 3, 80, 128), buf(6, 3, 64, 128), buf(3, 56, 128),
            buf(10, 32, 384), buf(10, 40, 256), buf(2, 10, 32, 128), buf(10, 48, 256), buf(10, 32, 256), buf(10, 32, 256),
            buf(12, 32, 128), buf(3, 128), buf(nx - 1, 3, 128), buf(3, 128), buf(ny - 1, 3, 128),
            buf(40, 256),
            dma((6,)), dma((4,)), dma((7,)), dma((1,)), dma((1,)),
            dma((ny - 1,)), dma((ny - 1,)),
            pltpu.SemaphoreType.REGULAR((2,)), pltpu.SemaphoreType.REGULAR((3,)),
        ]
        sizes = [(10, 32, 256), (10, 32, 256), (2, 10, 32, 256), (32, 256), (10, 32)]

        def body(*refs):
            step_kernel(*refs, nx=nx, ny=ny)

        held = pl.pallas_call(
            body,
            name="ocean_step",
            out_shape=[pltpu.VMEM(s, F32) for s in sizes],
            in_specs=[pl.BlockSpec(memory_space=anywhere)] * 8,
            out_specs=[pl.BlockSpec(memory_space=anywhere)] * 4 + [pl.BlockSpec(memory_space=vmem)],
            scratch_shapes=scratch,
            compiler_params=pltpu.CompilerParams(
                collective_id=0, has_side_effects=True, vmem_limit_bytes=32 << 20
            ),
        )(*operands)
        return pl.pallas_call(
            store_kernel,
            name="store_results",
            out_shape=[shape(10, 32, 256), shape(10, 32, 256), shape(2, 10, 32, 256),
                       shape(32, 256), shape(10, 32)],
            in_specs=[pl.BlockSpec(memory_space=anywhere)] * 5,
            out_specs=[pl.BlockSpec(memory_space=anywhere)] * 5,
            scratch_shapes=[dma((5,))],
            compiler_params=pltpu.CompilerParams(vmem_limit_bytes=4 << 20),
        )(*held)

    field, flat = P(None, "gy", "gx"), P("gy", "gx")
    tracer = P(None, None, "gy", "gx")
    return jax.shard_map(
        per_device,
        mesh=mesh,
        in_specs=(field, field, tracer, field, flat, flat, flat, flat),
        out_specs=(field, field, tracer, flat, P(None, "gy")),
        check_vma=False,
    )
```

```python
import jax
import jax.numpy as jnp
from jax import lax
from jax.experimental import pallas as pl
from jax.experimental.pallas import tpu as pltpu
from jax.sharding import PartitionSpec as P

SUBSTEPS = 12
WAVE = 0.5
PRESS = 0.05
DT = 0.5
MESH_ID = pl.DeviceIdType.MESH
F32 = jnp.float32
CW, DP, HT, FE, FN = range(5)
RAW = 80


def lanes(shape):
    return lax.broadcasted_iota(jnp.int32, shape, len(shape) - 1)


def rows(shape):
    return lax.broadcasted_iota(jnp.int32, shape, len(shape) - 2)


def turn(x, by):
    size = x.shape[-1]
    by = by % size if isinstance(by, int) else lax.rem(by + size, size)
    return x if isinstance(by, int) and by == 0 else pltpu.roll(x, by, x.ndim - 1)


def east(x):
    return turn(x, -1)


def west(x):
    return turn(x, 1)


def exact_dot(a, b, dims, split_first):
    whole, parts = (b, a) if split_first else (a, b)
    whole = whole.astype(jnp.bfloat16)
    total = None
    for _ in range(3):
        piece = parts.astype(jnp.bfloat16)
        parts = parts - piece.astype(F32)
        pair = (piece, whole) if split_first else (whole, piece)
        term = lax.dot_general(*pair, (dims, ((), ())), preferred_element_type=F32)
        total = term if total is None else total + term
    return total


def step_kernel(
    u_in, v_in, t_in, d_in, surface_in, depth_in, wet_in, count_in,
    fu_out, fv_out, m_out, h_out, ov_out,
    ext, u_s, v_s, d_s, t_s, cell_s, fe_x, fn_x, fu_b, fv_b, m_b, h_b, tally,
    pack_e, pack_w, got_w, got_e, got_sw, got_nw, got_se, got_ne, raw_s, raw_n,
    tr_e, tr_w, got_tw, got_te,
    ed, nd, ew, nw, me, mn, gs, hb, coef, hw,
    tu, tv, t0, pp, inv, ratio, sums, own_r, peer_r, all_r, south_r, fyb,
    in_sem, send_sem, recv_sem, gx_send, gx_recv, gy_send, gy_recv, gx_greet, gy_greet,
    *, nx, ny,
):
    gx, gy = lax.axis_index("gx"), lax.axis_index("gy")
    levels = u_s.shape[0]

    def at(dx, dy):
        return (lax.rem(gx + dx + nx, nx), gy + dy)

    core, chip_y, chip_x = lax.rem(gx, 2), lax.rem(lax.div(gx, 2), 4), lax.div(gx, 8)

    def chip_at(dx, dy, other):
        x, y = lax.rem(chip_x + dx, 4), lax.rem(chip_y + dy, 4)
        return (8 * x + 2 * y + (1 - core if other else core), gy)

    beside = [(1, 0), (3, 0), (0, 1), (0, 3)]
    opposite = [(2, 0), (0, 2)]
    offsets = [(dx, dy, other) for dx in (2, 1, 3, 0) for dy in (2, 1, 3, 0) for other in (0, 1)]
    offsets = sorted(offsets[:-2], key=lambda o: -(min(o[0], 4 - o[0]) + min(o[1], 4 - o[1]))) + [(0, 0, 1)]

    def greet_chips(semaphore, chips, cores=(0,)):
        for dx, dy in chips:
            for other in cores:
                pl.semaphore_signal(
                    semaphore, inc=1, device_id=chip_at(dx, dy, other), device_id_type=MESH_ID)

    def exists(dy):
        if dy == 0:
            return None
        return gy + dy < ny if dy > 0 else gy + dy >= 0

    def given(condition, act):
        if condition is None:
            act()
        else:
            pl.when(condition)(act)

    def greet(semaphore, peers):
        for dx, dy in peers:
            given(exists(dy), lambda dx=dx, dy=dy: pl.semaphore_signal(
                semaphore, inc=1, device_id=at(dx, dy), device_id_type=MESH_ID))

    def number(dy):
        return jnp.where(exists(dy), 1, 0)

    south_r[...] = jnp.zeros_like(south_r)

    barrier = pltpu.get_barrier_semaphore()
    greet(barrier, [(dx, dy) for dy in (1, -1) for dx in (-1, 1, 0)] + [(1, 0), (-1, 0)])
    greet_chips(barrier, beside, (0, 1))

    own = (pl.ds(24, 32), pl.ds(128, 256))
    loads = [
        pltpu.make_async_copy(a, b, in_sem.at[i])
        for i, a, b in [
            (0, wet_in, cell_s.at[0]),
            (0, count_in, cell_s.at[1]),
            (1, depth_in, ext.at[(DP, *own)]),
            (1, surface_in, ext.at[(HT, *own)]),
            (2, u_in, u_s),
            (3, v_in, v_s.at[:, pl.ds(8, 32), :]),
            (4, t_in, t_s.at[:, :, pl.ds(16, 32), :]),
            (5, d_in, d_s),
        ]
    ]
    for load in loads[4:6] + loads[:4]:
        load.start()

    def arrived(ref, semaphore):
        pltpu.make_async_copy(ref, ref, semaphore).wait()

    @pl.when(gy == 0)
    def _():
        ext[:, 8:24, 128:384] = jnp.zeros((5, 16, 256), F32)
        v_s[:, 0:8, :] = jnp.zeros((levels, 8, 256), F32)
        t_s[:, :, 8:16, :] = jnp.zeros((2, levels, 8, 256), F32)
        got_sw[...] = jnp.zeros_like(got_sw)
        got_se[...] = jnp.zeros_like(got_se)
        raw_s[...] = jnp.zeros_like(raw_s)

    @pl.when(gy == ny - 1)
    def _():
        ext[:, 56:72, 128:384] = jnp.zeros((5, 16, 256), F32)
        t_s[:, :, 48:56, :] = jnp.zeros((2, levels, 8, 256), F32)
        got_nw[...] = jnp.zeros_like(got_nw)
        got_ne[...] = jnp.zeros_like(got_ne)
        raw_n[...] = jnp.zeros_like(raw_n)

    arrived(cell_s, in_sem.at[0])
    arrived(ext.at[(pl.ds(DP, 2), *own)], in_sem.at[1])
    cw = jnp.where(cell_s[0] > 0, cell_s[1], 0).astype(F32)
    ext[CW, 24:56, 128:384] = cw
    m_u = jnp.minimum(cw, east(cw))
    gs[24:56, 128:384] = cw
    gs[56:64, 128:384] = jnp.zeros((8, 256), F32)
    m_v = jnp.minimum(cw, gs[25:57, 128:384])
    loads[4].wait()
    flow = jnp.zeros_like(cw)
    for k in range(levels):
        flow = flow + jnp.where(m_u > k, u_s[k], 0.0)
    flow_e = flow / levels
    ext[FE, 24:56, 128:384] = flow_e
    loads[5].wait()
    loads[6].start()
    loads[7].start()
    flow = jnp.zeros_like(cw)
    for k in range(levels):
        flow = flow + jnp.where(m_v > k, v_s[k, 8:40, :], 0.0)
    flow_n = flow / levels
    ext[FN, 24:56, 128:384] = flow_n

    lane = lanes((32, 128))
    fields = [cw, ext[DP, 24:56, 128:384], ext[HT, 24:56, 128:384], flow_e, flow_n]
    to_e = jnp.zeros((32, 128), F32)
    to_w = jnp.zeros((32, 128), F32)
    for a, field in enumerate(fields):
        here = jnp.logical_and(lane >= 16 * a, lane < 16 * a + 16)
        to_e = jnp.where(here, turn(field[:, 128:], 16 * a - 112), to_e)
        to_w = jnp.where(here, turn(field[:, :128], 16 * a), to_w)
    for k in range(levels):
        to_e = jnp.where(lane == RAW + k, turn(u_s[k, :, 128:], RAW + k - 127), to_e)
    pack_e[0:32, :] = to_e
    pack_w[0:32, :] = to_w
    pack_e[32:48, :] = jnp.zeros((16, 128), F32)
    pack_w[32:48, :] = jnp.zeros((16, 128), F32)
    for k in range(levels):
        pack_e[32 + k : 33 + k, :] = v_s[k, 39:40, 128:256]
        pack_w[32 + k : 33 + k, :] = v_s[k, 39:40, 0:128]

    pl.semaphore_wait(barrier, 10 + 3 * number(1) + 3 * number(-1))

    X, NORTH, SOUTH, LATER = 0, 1, 2, 3
    side = {0: X, 1: NORTH, -1: SOUTH}

    def start(group, later=0):
        def send(src, dst, dx, dy):
            pltpu.make_async_remote_copy(
                src_ref=src, dst_ref=dst,
                send_sem=send_sem.at[side[dy]], recv_sem=recv_sem.at[later + side[-dy]],
                device_id=at(dx, dy), device_id_type=MESH_ID,
            ).start()

        for dy in (1, -1, 0):
            ours = [entry for entry in group if entry[3] == dy]
            if ours:
                given(exists(dy), lambda ours=ours: [send(*e) for e in ours] and None)

    def wait_for(semaphore, count):
        ref = tally.at[pl.ds(0, count // 128), :]
        return lambda: pltpu.make_async_remote_copy(
            src_ref=ref, dst_ref=ref, send_sem=semaphore, recv_sem=semaphore,
            device_id=chip_at(0, 0, 1), device_id_type=MESH_ID,
        ).wait_recv()

    def size(ref):
        total = 1
        for extent in ref.shape:
            total *= extent
        return total

    def finish(group, later=0):
        for dy in (0, 1, -1):
            total = sum(size(entry[0]) for entry in group if entry[3] == dy)
            if total:
                given(exists(-dy), wait_for(recv_sem.at[later + side[-dy]], total))

    def finish_sends(group):
        for dy in (0, 1, -1):
            total = sum(size(entry[0]) for entry in group if entry[3] == dy)
            given(exists(dy), wait_for(send_sem.at[side[dy]], total))

    wide = pl.ds(128, 256)
    halo = [
        (pack_e.at[pl.ds(16, 32)], got_sw, 1, 1),
        (pack_w.at[pl.ds(16, 32)], got_se, -1, 1),
        (ext.at[:, pl.ds(48, 8), wide], ext.at[:, pl.ds(16, 8), wide], 0, 1),
        (ext.at[:, pl.ds(44, 4), wide], ext.at[:, pl.ds(12, 4), wide], 0, 1),
        (pack_e.at[pl.ds(16, 16)], raw_s, 0, 1),
        (pack_e.at[pl.ds(0, 16)], got_nw, 1, -1),
        (pack_w.at[pl.ds(0, 16)], got_ne, -1, -1),
        (ext.at[:, pl.ds(24, 8), wide], ext.at[:, pl.ds(56, 8), wide], 0, -1),
        (ext.at[:, pl.ds(32, 4), wide], ext.at[:, pl.ds(64, 4), wide], 0, -1),
        (pack_e.at[pl.ds(0, 16)], raw_n, 0, -1),
        (pack_e, got_w, 1, 0),
        (pack_w, got_e, -1, 0),
    ]
    start(halo)
    row_copies = [
        (pltpu.make_async_remote_copy(
            src_ref=src, dst_ref=dst, send_sem=send_sem.at[3 + i], recv_sem=recv_sem.at[6 + i],
            device_id=at(0, dy), device_id_type=MESH_ID), dy)
        for i, (src, dst, dy) in enumerate([
            (v_s.at[:, pl.ds(39, 1), :], v_s.at[:, pl.ds(7, 1), :], 1),
            (ext.at[:, pl.ds(43, 1), wide], ext.at[:, pl.ds(11, 1), wide], 1),
            (ext.at[:, pl.ds(36, 1), wide], ext.at[:, pl.ds(68, 1), wide], -1),
        ])
    ]
    for copy, dy in row_copies:
        pl.when(exists(dy))(copy.start)
    greet_chips(gx_greet.at[0], beside)
    greet(gy_greet.at[0], [(0, 1), (0, -1)])

    loads[6].wait()
    tracer_y = [
        (t_s.at[:, :, pl.ds(46, 2), :], t_s.at[:, :, pl.ds(14, 2), :], 0, 1),
        (t_s.at[:, :, pl.ds(16, 2), :], t_s.at[:, :, pl.ds(48, 2), :], 0, -1),
    ]
    start(tracer_y, LATER)
    to_e = jnp.zeros((32, 128), F32)
    to_w = jnp.zeros((32, 128), F32)
    for tr in range(2):
        for k in range(levels):
            at_lane = 4 * (tr * levels + k)
            first = (at_lane - 2) % 128
            to_e = jnp.where((lane == first) | (lane == first + 1),
                             turn(t_s[tr, k, 16:48, 128:256], at_lane), to_e)
            to_w = jnp.where((lane == at_lane) | (lane == at_lane + 1),
                             turn(t_s[tr, k, 16:48, 0:128], at_lane), to_w)
    tr_e[...] = to_e
    tr_w[...] = to_w
    tracer_x = [(tr_e, got_tw, 1, 0), (tr_w, got_te, -1, 0)]
    start(tracer_x, LATER)

    py = jnp.zeros_like(cw)
    sv = jnp.zeros_like(cw)
    for k in range(levels):
        py = py + (0.3 * t_s[1, k, 16:48, :] - 0.7 * t_s[0, k, 16:48, :])
        pp[k, 8:40, :] = py
        pp[k, 40:48, :] = jnp.zeros((8, 256), F32)
        vv = v_s[k, 8:40, :] - PRESS * (pp[k, 9:41, :] - py)
        tv[k, 8:40, :] = vv
        sv = sv + jnp.where(m_v > k, vv, 0.0)

    loads[7].wait()
    below_kappa = jnp.zeros_like(cw)
    below_ratio = jnp.zeros_like(cw)
    for k in range(levels - 1, -1, -1):
        above = jnp.where(cw > k, d_s[k - 1], 0.0) if k else jnp.zeros_like(cw)
        factor = 1.0 / (1.0 + above + below_kappa - below_kappa * below_ratio)
        below_ratio = above * factor
        inv[k] = factor
        ratio[k] = below_ratio
        below_kappa = above

    pl.semaphore_wait(gx_greet.at[0], 4)
    greet_chips(gx_greet.at[1], opposite)
    pl.semaphore_wait(gy_greet.at[0], number(1) + number(-1))
    greet(gy_greet.at[1], [(0, 2), (0, -2)])

    finish(halo)
    for copy, dy in row_copies:
        pl.when(exists(-dy))(copy.wait_recv)

    lane = lanes((64, 128))
    from_w = jnp.concatenate([got_sw[0:16], got_w[0:32], got_nw[...]], axis=0)
    from_e = jnp.concatenate([got_se[0:16], got_e[0:32], got_ne[...]], axis=0)
    edge = [
        jnp.where(lane < 64, turn(from_e, -16 * a), turn(from_w, 112 - 16 * a)) for a in range(5)
    ]
    for a in range(3):
        ext[a, 8:72, 0:128] = edge[a]
    cells = ext[CW, 8:72, :]
    ext[CW, 72:80, :] = jnp.zeros((8, 384), F32)
    mask_e = jnp.minimum(cells, east(cells))
    mask_n = jnp.minimum(cells, ext[CW, 9:73, :])
    me[...] = mask_e[16:48]
    mn[...] = mask_n[8:48, 128:384]
    deep = ext[DP, 8:72, :]
    half = 0.5 * WAVE
    ed[...] = jnp.where(mask_e > 0.0, half * (deep + east(deep)), 0.0)
    ew[...] = jnp.where(mask_e > 0.0, WAVE, 0.0)
    ext[DP, 72:80, :] = jnp.zeros((8, 384), F32)
    nd[...] = jnp.where(mask_n > 0.0, half * (deep + ext[DP, 9:73, :]), 0.0)
    nw[...] = jnp.where(mask_n > 0.0, WAVE, 0.0)

    def column_mean(raw, cut):
        hold = jnp.logical_and(lane >= RAW, (lane - RAW).astype(F32) < cut)
        return jnp.sum(jnp.where(hold, raw, 0.0), axis=1, keepdims=True) / levels

    raw_own = jnp.concatenate([raw_s[...], pack_e[0:32], raw_n[...]], axis=0)
    fe_x[:, 0:128] = jnp.where(lane == 127, column_mean(from_w, mask_e[:, 127:128]), edge[FE])
    fe_x[:, 128:256] = ext[FE, 8:72, 128:256]
    fe_x[:, 256:384] = jnp.where(
        lane == 127, column_mean(raw_own, mask_e[:, 383:384]), ext[FE, 8:72, 256:384]
    )
    fn_x[:, 0:128] = edge[FN]
    fn_x[:, 128:384] = ext[FN, 8:72, 128:384]
    for first, tile in ((8, 0), (40, 32)):
        cut = mask_n[first : first + 8, 128:384]
        total = jnp.zeros_like(cut)
        for k in range(levels):
            total = total + jnp.where(cut > k, v_s[k, tile : tile + 8, :], 0.0)
        fn_x[first : first + 8, 128:384] = jnp.where(
            rows((8, 256)) == 7, total / levels, ext[FN, 8 + first : 16 + first, 128:384]
        )
    lane = lanes((16, 128))
    level = rows((16, 128)).astype(F32)
    for line, a, b in ((15, got_se[16:32], got_sw[16:32]), (47, got_e[32:48], got_w[32:48])):
        raw = jnp.where(lane < 64, a, b)
        hold = level < mask_n[line : line + 1, 0:128]
        mean = jnp.sum(jnp.where(hold, raw, 0.0), axis=0, keepdims=True) / levels
        fn_x[line : line + 1, 0:128] = mean

    tiles = [slice(128 * t, 128 * t + 128) for t in range(3)]
    fx = ed[...] * fe_x[...]
    fy = nd[...] * fn_x[...]
    gs[0:8, :] = jnp.zeros((8, 384), F32)
    gs[8:72, :] = fy
    divergence = fx - west(fx) + fy - gs[7:71, :]
    height = ext[HT, 8:72, :] - divergence
    a_e = WAVE * ed[...]
    a_n = WAVE * nd[...]
    a_w = west(a_e)
    gs[8:72, :] = a_n
    a_s = gs[7:71, :]
    a_0 = a_e + a_w + a_n + a_s
    for t, tile in enumerate(tiles):
        for i, value in enumerate((divergence, a_e, a_w, a_n, a_s, a_0)):
            coef[i, t] = value[:, tile]
        for b in range(2):
            hb[b, t, 0:8, :] = jnp.zeros((8, 128), F32)
            hb[b, t, 72:80, :] = jnp.zeros((8, 128), F32)
        hb[0, t, 8:72, :] = height[:, tile]
        hw[t, 0:48, :] = (SUBSTEPS * 1.0) * height[8:56, tile]
        hw[t, 48:56, :] = jnp.zeros((8, 128), F32)
    lane = lanes((8, 128))

    def substep(old, weight, first, last, final=False):
        new = 1 - old
        for at_row in range(first, last, 8):
            here, inner = slice(8 + at_row, 16 + at_row), slice(at_row, at_row + 8)
            north, south = slice(9 + at_row, 17 + at_row), slice(7 + at_row, 15 + at_row)
            h = [hb[old, t, here, :] for t in range(3)]
            to_w = [pltpu.roll(x, 127, 1) for x in h]
            to_e = [pltpu.roll(x, 1, 1) for x in h]
            for t in range(3):
                h_e = jnp.where(lane == 127, to_w[(t + 1) % 3], to_w[t])
                h_w = jnp.where(lane == 0, to_e[(t + 2) % 3], to_e[t])
                change = (
                    (coef[1, t, inner, :] * h_e + coef[2, t, inner, :] * h_w)
                    + (coef[3, t, inner, :] * hb[old, t, north, :]
                       + coef[4, t, inner, :] * hb[old, t, south, :])
                    - coef[5, t, inner, :] * h[t]
                )
                div = coef[0, t, inner, :] - change
                value = h[t] - div
                if not final:
                    coef[0, t, inner, :] = div
                hb[new, t, here, :] = value
                if 8 <= at_row < 56:
                    hw[t, at_row - 8 : at_row, :] += weight * value

    for step in range(2, 6):
        substep(step % 2, SUBSTEPS + 1.0 - step, 0, 64)
    pl.semaphore_wait(gy_greet.at[1], number(2) + number(-2))
    greet(gy_greet.at[2], [(0, -4)])
    for step in range(6, SUBSTEPS + 1):
        substep(step % 2, SUBSTEPS + 1.0 - step, 8, 56, step == SUBSTEPS)

    finish(tracer_y, LATER)
    m_n = mn[...]
    pn = jnp.zeros((8, 256), F32)
    ps = jnp.zeros((8, 256), F32)
    ends = [jnp.zeros((8, 256), F32)] * 2
    for k in range(levels):
        pn = pn + (0.3 * t_s[1, k, 48:56, :] - 0.7 * t_s[0, k, 48:56, :])
        ps = ps + (0.3 * t_s[1, k, 8:16, :] - 0.7 * t_s[0, k, 8:16, :])
        pp[k, 40:48, :] = pn
        pp[k, 0:8, :] = ps
        for i, first in enumerate((0, 32)):
            vv = v_s[k, first : first + 8, :] - PRESS * (
                pp[k, first + 1 : first + 9, :] - pp[k, first : first + 8, :])
            tv[k, first : first + 8, :] = vv
            ends[i] = ends[i] + jnp.where(m_n[first : first + 8] > k, vv, 0.0)
    sv = jnp.concatenate([ends[0], sv[0:24], ends[1]], axis=0)
    scale = levels / SUBSTEPS
    wide_n = [hw[t, 0:40, :] for t in (1, 2)]
    next_n = [hw[t, 1:41, :] for t in (1, 2)]
    step_n = jnp.concatenate([b - a for a, b in zip(wide_n, next_n)], axis=1)
    sum_n = SUBSTEPS * fn_x[8:48, 128:384] - nw[8:48, 128:384] * step_n
    fix_v = (scale * sum_n - sv) / jnp.maximum(m_n, 1.0)
    for k in range(levels):
        vv = jnp.where(m_n > k, tv[k] + fix_v, 0.0)
        tv[k] = vv
        fv_b[k] = vv[8:40]
        sums[k] = vv[8:40, 0:128] + vv[8:40, 128:256]
    sums[levels:12] = jnp.zeros((12 - levels, 32, 128), F32)

    part = jnp.zeros((8, 128), F32)
    for r in range(3):
        pick = (rows((8, 128)) == r).astype(F32)
        part = part + exact_dot(
            pick, sums[4 * r : 4 * r + 4].reshape(128, 128), ((1,), (1,)), False
        )
    own_r[...] = part[0:3]

    def share(src, dst, i, peer, send_to, recv_to):
        return pltpu.make_async_remote_copy(
            src_ref=src, dst_ref=dst.at[i], send_sem=send_to.at[i], recv_sem=recv_to.at[i],
            device_id=peer, device_id_type=MESH_ID,
        )

    pl.semaphore_wait(gx_greet.at[1], 2)
    def first_copy(i):
        to = jnp.where(i >= gx, i + 1, i)
        return pltpu.make_async_remote_copy(
            src_ref=own_r, dst_ref=peer_r.at[jnp.where(gx > to, gx - 1, gx)],
            send_sem=gx_send.at[0], recv_sem=gx_recv.at[0], device_id=(to, gy), device_id_type=MESH_ID,
        )

    def all_shares():
        return pltpu.make_async_remote_copy(
            src_ref=peer_r, dst_ref=peer_r, send_sem=gx_send.at[0], recv_sem=gx_recv.at[0],
            device_id=chip_at(0, 0, 1), device_id_type=MESH_ID,
        )

    first_share = [first_copy(i) for i in range(nx - 1)]
    for copy in first_share:
        copy.start()

    h_b[:, 0:128] = hb[1, 1, 24:56, :]
    h_b[:, 128:256] = hb[1, 2, 24:56, :]
    stores = [
        pltpu.make_async_copy(a, b, in_sem.at[i])
        for i, (a, b) in enumerate([(h_b, h_out), (fv_b, fv_out), (fu_b, fu_out), (m_b, m_out)])
    ]
    stores[0].start()
    stores[1].start()
    weighted = jnp.concatenate([hw[t, 8:40, :] for t in range(3)], axis=1)
    sum_e = SUBSTEPS * fe_x[16:48, :] - ew[16:48, :] * (east(weighted) - weighted)
    finish(tracer_x, LATER)
    lane = lanes((32, 128))
    both = jnp.where(lane % 4 >= 2, got_tw[...], got_te[...])
    m_e = me[...]
    p0 = jnp.zeros((32, 128), F32)
    su = jnp.zeros((32, 384), F32)
    for k in range(levels):
        for tr in range(2):
            t0[tr, k] = turn(both, -4 * (tr * levels + k))
        p0 = p0 + (0.3 * t0[1, k] - 0.7 * t0[0, k])
        px = jnp.concatenate([p0, pp[k, 8:40, :]], axis=1)
        uu = jnp.concatenate([turn(got_w[0:32, :], 127 - RAW - k), u_s[k]], axis=1)
        uu = uu - PRESS * (east(px) - px)
        tu[k] = uu
        su = su + jnp.where(m_e > k, uu, 0.0)
    fix_u = (scale * sum_e - su) / jnp.maximum(m_e, 1.0)
    for k in range(levels):
        uu = jnp.where(m_e > k, tu[k] + fix_u, 0.0)
        tu[k] = uu
        fu_b[k] = uu[:, 128:384]
    stores[2].start()

    def tracer_level(turn_index, carry):
        k = levels - 1 - turn_index
        up = jnp.maximum(k - 1, 0)
        level = k.astype(F32)
        w_below, wt, value = carry[0], carry[1:3], carry[3:5]
        fu = tu[k]
        fv = tv[k]
        div = (fu - west(fu))[:, 128:384] + fv[8:40] - tv[k, 7:39, :]
        w_top = w_below - div
        kappa = jnp.where(cw > level + 1.0, d_s[k], 0.0)
        new_wt, new_value = [], []
        for tr in range(2):
            own_t = t_s[tr, k, 16:48, :]
            tx = jnp.concatenate([t0[tr, k], own_t], axis=1)
            te1 = east(tx)
            face = (7.0 * (tx + te1) - (west(tx) + east(te1))) * (1.0 / 12.0)
            flux = fu * face
            out = (flux - west(flux))[:, 128:384]
            ty = t_s[tr, k, 8:48, :]
            face = (7.0 * (ty + t_s[tr, k, 9:49, :])
                    - (t_s[tr, k, 7:47, :] + t_s[tr, k, 10:50, :])) * (1.0 / 12.0)
            flux = fv * face
            fyb[...] = flux
            out = out + (flux[8:40] - fyb[7:39, :])
            top = jnp.where(k == 0, own_t, 0.5 * (own_t + t_s[tr, up, 16:48, :]))
            through = w_top * top
            source = jnp.where(cw > level, own_t - DT * (out + (through - wt[tr])), 0.0)
            val = (source + kappa * value[tr]) * inv[k]
            m_b[tr, k] = val
            new_wt.append(through)
            new_value.append(val)
        return (w_top, *new_wt, *new_value)

    zero = jnp.zeros((32, 256), F32)
    lax.fori_loop(0, levels, tracer_level, (zero,) * 5)

    def back(k, carry):
        out = []
        for tr in range(2):
            val = m_b[tr, k] + ratio[k] * carry[tr]
            m_b[tr, k] = val
            out.append(val)
        return tuple(out)

    lax.fori_loop(0, levels, back, (zero,) * 2)
    stores[3].start()

    a, b = rows((128, 128)), lanes((128, 128))
    block = (a // 32) == (b // 32)
    upto = jnp.where(jnp.logical_and(block, a <= b), 1.0, 0.0)
    whole = jnp.where(block, 1.0, 0.0)
    all_shares().wait_recv()
    total = own_r[...]
    for i in range(nx - 1):
        total = total + peer_r[i]
    all_r[...] = total
    pl.when(exists(4))(lambda: pl.semaphore_wait(gy_greet.at[2], 1))
    second_share = [
        share(all_r, south_r, i, at(0, i + 1), gy_send, gy_recv) for i in range(ny - 1)
    ]
    for i, copy in enumerate(second_share):
        pl.when(exists(i + 1))(lambda copy=copy: copy.start())
    total = jnp.concatenate([total, jnp.zeros((5, 128), F32)], axis=0)
    running = exact_dot(total, upto, ((1,), (0,)), True)
    all_shares().wait_send()
    finish_sends(halo + tracer_x + tracer_y)
    for copy, dy in row_copies:
        pl.when(exists(dy))(copy.wait_send)
    for store in stores:
        store.wait()
    for i, copy in enumerate(second_share):
        pl.when(exists(-i - 1))(lambda copy=copy: copy.wait_recv())
    south = jnp.zeros((3, 128), F32)
    for i in range(ny - 1):
        south = south + jnp.where(gy >= i + 1, south_r[i], 0.0)
    south = jnp.concatenate([south, jnp.zeros((5, 128), F32)], axis=0)
    running = (running + exact_dot(south, whole, ((1,), (0,)), True)) * (nx * 256 * ny * 32) ** -0.5
    for k in range(levels):
        ov_out[k : k + 1, :] = running[k // 4 : k // 4 + 1, 32 * (k % 4) : 32 * (k % 4) + 32]
    for i, copy in enumerate(second_share):
        pl.when(exists(i + 1))(lambda copy=copy: copy.wait_send())


def store_kernel(*refs):
    held, results, sem = refs[:5], refs[5:10], refs[10]
    copies = [
        pltpu.make_async_copy(a, b, sem.at[i]) for i, (a, b) in enumerate(zip(held, results))
    ]
    for copy in copies:
        copy.start()
    for copy in copies:
        copy.wait()


def solution(mesh):
    nx, ny = mesh.shape["gx"], mesh.shape["gy"]
    vmem, anywhere = pltpu.VMEM, pl.ANY
    dma = pltpu.SemaphoreType.DMA

    def shape(*s):
        return jax.ShapeDtypeStruct(s, F32)

    def per_device(u, v, t, d, surface, depth, wet, count):
        operands = [
            pltpu.with_memory_space_constraint(a, pltpu.HBM)
            for a in (u, v, t, d, surface, depth, wet, count)
        ]

        def buf(*s):
            return vmem(s, F32)

        def ibuf(*s):
            return vmem(s, jnp.int32)

        scratch = [
            buf(5, 80, 384), buf(10, 32, 256), buf(10, 40, 256), buf(10, 32, 256),
            buf(2, 10, 56, 256), ibuf(2, 32, 256), buf(64, 384), buf(64, 384),
            buf(10, 32, 256), buf(10, 32, 256), buf(2, 10, 32, 256), buf(32, 256), buf(320, 128),
            buf(48, 128), buf(48, 128), buf(48, 128), buf(48, 128),
            buf(32, 128), buf(16, 128), buf(32, 128), buf(16, 128), buf(16, 128), buf(16, 128),
            buf(32, 128), buf(32, 128), buf(32, 128), buf(32, 128),
            buf(64, 384), buf(64, 384), buf(64, 384), buf(64, 384),
            buf(32, 384), buf(40, 256), buf(80, 384), buf(2, 3, 80, 128), buf(6, 3, 64, 128), buf(3, 56, 128),
            buf(10, 32, 384), buf(10, 40, 256), buf(2, 10, 32, 128), buf(10, 48, 256), buf(10, 32, 256), buf(10, 32, 256),
            buf(12, 32, 128), buf(3, 128), buf(nx - 1, 3, 128), buf(3, 128), buf(ny - 1, 3, 128),
            buf(40, 256),
            dma((6,)), dma((6,)), dma((9,)), dma((1,)), dma((1,)),
            dma((ny - 1,)), dma((ny - 1,)),
            pltpu.SemaphoreType.REGULAR((2,)), pltpu.SemaphoreType.REGULAR((3,)),
        ]
        sizes = [(10, 32, 256), (10, 32, 256), (2, 10, 32, 256), (32, 256), (10, 32)]

        def body(*refs):
            step_kernel(*refs, nx=nx, ny=ny)

        held = pl.pallas_call(
            body,
            name="ocean_step",
            out_shape=[pltpu.VMEM(s, F32) for s in sizes],
            in_specs=[pl.BlockSpec(memory_space=anywhere)] * 8,
            out_specs=[pl.BlockSpec(memory_space=anywhere)] * 4 + [pl.BlockSpec(memory_space=vmem)],
            scratch_shapes=scratch,
            compiler_params=pltpu.CompilerParams(
                collective_id=0, has_side_effects=True, vmem_limit_bytes=32 << 20
            ),
        )(*operands)
        return pl.pallas_call(
            store_kernel,
            name="store_results",
            out_shape=[shape(10, 32, 256), shape(10, 32, 256), shape(2, 10, 32, 256),
                       shape(32, 256), shape(10, 32)],
            in_specs=[pl.BlockSpec(memory_space=anywhere)] * 5,
            out_specs=[pl.BlockSpec(memory_space=anywhere)] * 5,
            scratch_shapes=[dma((5,))],
            compiler_params=pltpu.CompilerParams(vmem_limit_bytes=4 << 20),
        )(*held)

    field, flat = P(None, "gy", "gx"), P("gy", "gx")
    tracer = P(None, None, "gy", "gx")
    return jax.shard_map(
        per_device,
        mesh=mesh,
        in_specs=(field, field, tracer, field, flat, flat, flat, flat),
        out_specs=(field, field, tracer, flat, P(None, "gy")),
        check_vma=False,
    )
```

```python
import jax
import jax.numpy as jnp
from jax import lax
from jax.experimental import pallas as pl
from jax.experimental.pallas import tpu as pltpu
from jax.sharding import PartitionSpec as P

SUBSTEPS = 12
WAVE = 0.5
PRESS = 0.05
DT = 0.5
MESH_ID = pl.DeviceIdType.MESH
F32 = jnp.float32
CW, DP, HT, FE, FN = range(5)
RAW = 80


def lanes(shape):
    return lax.broadcasted_iota(jnp.int32, shape, len(shape) - 1)


def rows(shape):
    return lax.broadcasted_iota(jnp.int32, shape, len(shape) - 2)


def turn(x, by):
    size = x.shape[-1]
    by = by % size if isinstance(by, int) else lax.rem(by + size, size)
    return x if isinstance(by, int) and by == 0 else pltpu.roll(x, by, x.ndim - 1)


def east(x):
    return turn(x, -1)


def west(x):
    return turn(x, 1)


def exact_dot(a, b, dims, split_first):
    whole, parts = (b, a) if split_first else (a, b)
    whole = whole.astype(jnp.bfloat16)
    total = None
    for _ in range(3):
        piece = parts.astype(jnp.bfloat16)
        parts = parts - piece.astype(F32)
        pair = (piece, whole) if split_first else (whole, piece)
        term = lax.dot_general(*pair, (dims, ((), ())), preferred_element_type=F32)
        total = term if total is None else total + term
    return total


def step_kernel(
    u_in, v_in, t_in, d_in, surface_in, depth_in, wet_in, count_in,
    fu_out, fv_out, m_out, h_out, ov_out,
    ext, u_s, v_s, d_s, t_s, cell_s, fe_x, fn_x, fu_b, fv_b, m_b, h_b, tally,
    pack_e, pack_w, got_w, got_e, got_sw, got_nw, got_se, got_ne, raw_s, raw_n,
    tr_e, tr_w, got_tw, got_te,
    ed, nd, ew, nw, me, mn, gs, hb, coef, hw,
    tu, tv, t0, pp, inv, ratio, sums, own_r, peer_r, all_r, south_r, fyb,
    in_sem, send_sem, recv_sem, gx_send, gx_recv, gy_send, gy_recv, gx_greet, gy_greet,
    *, nx, ny,
):
    gx, gy = lax.axis_index("gx"), lax.axis_index("gy")
    levels = u_s.shape[0]

    def at(dx, dy):
        return (lax.rem(gx + dx + nx, nx), gy + dy)

    core, chip_y, chip_x = lax.rem(gx, 2), lax.rem(lax.div(gx, 2), 4), lax.div(gx, 8)

    def chip_at(dx, dy, other):
        x, y = lax.rem(chip_x + dx, 4), lax.rem(chip_y + dy, 4)
        return (8 * x + 2 * y + (1 - core if other else core), gy)

    beside = [(1, 0), (3, 0), (0, 1), (0, 3)]
    opposite = [(2, 0), (0, 2)]
    offsets = [(dx, dy, other) for dx in (2, 1, 3, 0) for dy in (2, 1, 3, 0) for other in (0, 1)]
    offsets = sorted(offsets[:-2], key=lambda o: -(min(o[0], 4 - o[0]) + min(o[1], 4 - o[1]))) + [(0, 0, 1)]

    def greet_chips(semaphore, chips, cores=(0,)):
        for dx, dy in chips:
            for other in cores:
                pl.semaphore_signal(
                    semaphore, inc=1, device_id=chip_at(dx, dy, other), device_id_type=MESH_ID)

    def exists(dy):
        if dy == 0:
            return None
        return gy + dy < ny if dy > 0 else gy + dy >= 0

    def given(condition, act):
        if condition is None:
            act()
        else:
            pl.when(condition)(act)

    def greet(semaphore, peers):
        for dx, dy in peers:
            given(exists(dy), lambda dx=dx, dy=dy: pl.semaphore_signal(
                semaphore, inc=1, device_id=at(dx, dy), device_id_type=MESH_ID))

    def number(dy):
        return jnp.where(exists(dy), 1, 0)

    south_r[...] = jnp.zeros_like(south_r)

    barrier = pltpu.get_barrier_semaphore()
    greet(barrier, [(dx, dy) for dy in (1, -1) for dx in (-1, 1, 0)] + [(1, 0), (-1, 0)])
    greet_chips(barrier, beside, (0, 1))

    own = (pl.ds(24, 32), pl.ds(128, 256))
    loads = [
        pltpu.make_async_copy(a, b, in_sem.at[i])
        for i, a, b in [
            (0, wet_in, cell_s.at[0]),
            (0, count_in, cell_s.at[1]),
            (1, depth_in, ext.at[(DP, *own)]),
            (1, surface_in, ext.at[(HT, *own)]),
            (2, u_in, u_s),
            (3, v_in, v_s.at[:, pl.ds(8, 32), :]),
            (4, t_in, t_s.at[:, :, pl.ds(16, 32), :]),
            (5, d_in, d_s),
        ]
    ]
    for load in loads[4:6] + loads[:4]:
        load.start()

    def arrived(ref, semaphore):
        pltpu.make_async_copy(ref, ref, semaphore).wait()

    @pl.when(gy == 0)
    def _():
        ext[:, 8:24, 128:384] = jnp.zeros((5, 16, 256), F32)
        v_s[:, 0:8, :] = jnp.zeros((levels, 8, 256), F32)
        t_s[:, :, 8:16, :] = jnp.zeros((2, levels, 8, 256), F32)
        got_sw[...] = jnp.zeros_like(got_sw)
        got_se[...] = jnp.zeros_like(got_se)
        raw_s[...] = jnp.zeros_like(raw_s)

    @pl.when(gy == ny - 1)
    def _():
        ext[:, 56:72, 128:384] = jnp.zeros((5, 16, 256), F32)
        t_s[:, :, 48:56, :] = jnp.zeros((2, levels, 8, 256), F32)
        got_nw[...] = jnp.zeros_like(got_nw)
        got_ne[...] = jnp.zeros_like(got_ne)
        raw_n[...] = jnp.zeros_like(raw_n)

    arrived(cell_s, in_sem.at[0])
    arrived(ext.at[(pl.ds(DP, 2), *own)], in_sem.at[1])
    cw = jnp.where(cell_s[0] > 0, cell_s[1], 0).astype(F32)
    ext[CW, 24:56, 128:384] = cw
    m_u = jnp.minimum(cw, east(cw))
    gs[24:56, 128:384] = cw
    gs[56:64, 128:384] = jnp.zeros((8, 256), F32)
    m_v = jnp.minimum(cw, gs[25:57, 128:384])
    loads[4].wait()
    flow = jnp.zeros_like(cw)
    for k in range(levels):
        flow = flow + jnp.where(m_u > k, u_s[k], 0.0)
    flow_e = flow / levels
    ext[FE, 24:56, 128:384] = flow_e
    loads[5].wait()
    loads[6].start()
    loads[7].start()
    flow = jnp.zeros_like(cw)
    for k in range(levels):
        flow = flow + jnp.where(m_v > k, v_s[k, 8:40, :], 0.0)
    flow_n = flow / levels
    ext[FN, 24:56, 128:384] = flow_n

    lane = lanes((32, 128))
    fields = [cw, ext[DP, 24:56, 128:384], ext[HT, 24:56, 128:384], flow_e, flow_n]
    to_e = jnp.zeros((32, 128), F32)
    to_w = jnp.zeros((32, 128), F32)
    for a, field in enumerate(fields):
        here = jnp.logical_and(lane >= 16 * a, lane < 16 * a + 16)
        to_e = jnp.where(here, turn(field[:, 128:], 16 * a - 112), to_e)
        to_w = jnp.where(here, turn(field[:, :128], 16 * a), to_w)
    for k in range(levels):
        to_e = jnp.where(lane == RAW + k, turn(u_s[k, :, 128:], RAW + k - 127), to_e)
    pack_e[0:32, :] = to_e
    pack_w[0:32, :] = to_w
    pack_e[32:48, :] = jnp.zeros((16, 128), F32)
    pack_w[32:48, :] = jnp.zeros((16, 128), F32)
    for k in range(levels):
        pack_e[32 + k : 33 + k, :] = v_s[k, 39:40, 128:256]
        pack_w[32 + k : 33 + k, :] = v_s[k, 39:40, 0:128]

    pl.semaphore_wait(barrier, 10 + 3 * number(1) + 3 * number(-1))

    X, NORTH, SOUTH, LATER = 0, 1, 2, 3
    side = {0: X, 1: NORTH, -1: SOUTH}

    def start(group, later=0):
        def send(src, dst, dx, dy):
            pltpu.make_async_remote_copy(
                src_ref=src, dst_ref=dst,
                send_sem=send_sem.at[side[dy]], recv_sem=recv_sem.at[later + side[-dy]],
                device_id=at(dx, dy), device_id_type=MESH_ID,
            ).start()

        for dy in (1, -1, 0):
            ours = [entry for entry in group if entry[3] == dy]
            if ours:
                given(exists(dy), lambda ours=ours: [send(*e) for e in ours] and None)

    def wait_for(semaphore, count):
        ref = tally.at[pl.ds(0, count // 128), :]
        return lambda: pltpu.make_async_remote_copy(
            src_ref=ref, dst_ref=ref, send_sem=semaphore, recv_sem=semaphore,
            device_id=chip_at(0, 0, 1), device_id_type=MESH_ID,
        ).wait_recv()

    def size(ref):
        total = 1
        for extent in ref.shape:
            total *= extent
        return total

    def finish(group, later=0):
        for dy in (0, 1, -1):
            total = sum(size(entry[0]) for entry in group if entry[3] == dy)
            if total:
                given(exists(-dy), wait_for(recv_sem.at[later + side[-dy]], total))

    def finish_sends(group):
        for dy in (0, 1, -1):
            total = sum(size(entry[0]) for entry in group if entry[3] == dy)
            given(exists(dy), wait_for(send_sem.at[side[dy]], total))

    wide = pl.ds(128, 256)
    halo = [
        (pack_e.at[pl.ds(16, 32)], got_sw, 1, 1),
        (pack_w.at[pl.ds(16, 32)], got_se, -1, 1),
        (ext.at[:, pl.ds(48, 8), wide], ext.at[:, pl.ds(16, 8), wide], 0, 1),
        (ext.at[:, pl.ds(44, 4), wide], ext.at[:, pl.ds(12, 4), wide], 0, 1),
        (pack_e.at[pl.ds(16, 16)], raw_s, 0, 1),
        (pack_e.at[pl.ds(0, 16)], got_nw, 1, -1),
        (pack_w.at[pl.ds(0, 16)], got_ne, -1, -1),
        (ext.at[:, pl.ds(24, 8), wide], ext.at[:, pl.ds(56, 8), wide], 0, -1),
        (ext.at[:, pl.ds(32, 4), wide], ext.at[:, pl.ds(64, 4), wide], 0, -1),
        (pack_e.at[pl.ds(0, 16)], raw_n, 0, -1),
        (pack_e, got_w, 1, 0),
        (pack_w, got_e, -1, 0),
    ]
    start(halo)
    row_copies = [
        (pltpu.make_async_remote_copy(
            src_ref=src, dst_ref=dst, send_sem=send_sem.at[3 + i], recv_sem=recv_sem.at[6 + i],
            device_id=at(0, dy), device_id_type=MESH_ID), dy)
        for i, (src, dst, dy) in enumerate([
            (v_s.at[:, pl.ds(39, 1), :], v_s.at[:, pl.ds(7, 1), :], 1),
            (ext.at[:, pl.ds(43, 1), wide], ext.at[:, pl.ds(11, 1), wide], 1),
            (ext.at[:, pl.ds(36, 1), wide], ext.at[:, pl.ds(68, 1), wide], -1),
        ])
    ]
    for copy, dy in row_copies:
        pl.when(exists(dy))(copy.start)
    greet_chips(gx_greet.at[0], beside)
    greet(gy_greet.at[0], [(0, 1), (0, -1)])

    loads[6].wait()
    tracer_y = [
        (t_s.at[:, :, pl.ds(46, 2), :], t_s.at[:, :, pl.ds(14, 2), :], 0, 1),
        (t_s.at[:, :, pl.ds(16, 2), :], t_s.at[:, :, pl.ds(48, 2), :], 0, -1),
    ]
    start(tracer_y, LATER)
    to_e = jnp.zeros((32, 128), F32)
    to_w = jnp.zeros((32, 128), F32)
    for tr in range(2):
        for k in range(levels):
            at_lane = 4 * (tr * levels + k)
            first = (at_lane - 2) % 128
            to_e = jnp.where((lane == first) | (lane == first + 1),
                             turn(t_s[tr, k, 16:48, 128:256], at_lane), to_e)
            to_w = jnp.where((lane == at_lane) | (lane == at_lane + 1),
                             turn(t_s[tr, k, 16:48, 0:128], at_lane), to_w)
    tr_e[...] = to_e
    tr_w[...] = to_w
    tracer_x = [(tr_e, got_tw, 1, 0), (tr_w, got_te, -1, 0)]
    start(tracer_x, LATER)

    py = jnp.zeros_like(cw)
    sv = jnp.zeros_like(cw)
    for k in range(levels):
        py = py + (0.3 * t_s[1, k, 16:48, :] - 0.7 * t_s[0, k, 16:48, :])
        pp[k, 8:40, :] = py
        pp[k, 40:48, :] = jnp.zeros((8, 256), F32)
        vv = v_s[k, 8:40, :] - PRESS * (pp[k, 9:41, :] - py)
        tv[k, 8:40, :] = vv
        sv = sv + jnp.where(m_v > k, vv, 0.0)

    loads[7].wait()
    below_kappa = jnp.zeros_like(cw)
    below_ratio = jnp.zeros_like(cw)
    for k in range(levels - 1, -1, -1):
        above = jnp.where(cw > k, d_s[k - 1], 0.0) if k else jnp.zeros_like(cw)
        factor = 1.0 / (1.0 + above + below_kappa - below_kappa * below_ratio)
        below_ratio = above * factor
        inv[k] = factor
        ratio[k] = below_ratio
        below_kappa = above

    pl.semaphore_wait(gx_greet.at[0], 4)
    greet_chips(gx_greet.at[1], opposite)
    pl.semaphore_wait(gy_greet.at[0], number(1) + number(-1))
    greet(gy_greet.at[1], [(0, 2), (0, -2)])

    finish(halo)
    for copy, dy in row_copies:
        pl.when(exists(-dy))(copy.wait_recv)

    lane = lanes((64, 128))
    from_w = jnp.concatenate([got_sw[0:16], got_w[0:32], got_nw[...]], axis=0)
    from_e = jnp.concatenate([got_se[0:16], got_e[0:32], got_ne[...]], axis=0)
    edge = [
        jnp.where(lane < 64, turn(from_e, -16 * a), turn(from_w, 112 - 16 * a)) for a in range(5)
    ]
    for a in range(3):
        ext[a, 8:72, 0:128] = edge[a]
    cells = ext[CW, 8:72, :]
    ext[CW, 72:80, :] = jnp.zeros((8, 384), F32)
    mask_e = jnp.minimum(cells, east(cells))
    mask_n = jnp.minimum(cells, ext[CW, 9:73, :])
    me[...] = mask_e[16:48]
    mn[...] = mask_n[8:48, 128:384]
    deep = ext[DP, 8:72, :]
    half = 0.5 * WAVE
    ed[...] = jnp.where(mask_e > 0.0, half * (deep + east(deep)), 0.0)
    ew[...] = jnp.where(mask_e > 0.0, WAVE, 0.0)
    ext[DP, 72:80, :] = jnp.zeros((8, 384), F32)
    nd[...] = jnp.where(mask_n > 0.0, half * (deep + ext[DP, 9:73, :]), 0.0)
    nw[...] = jnp.where(mask_n > 0.0, WAVE, 0.0)

    def column_mean(raw, cut):
        hold = jnp.logical_and(lane >= RAW, (lane - RAW).astype(F32) < cut)
        return jnp.sum(jnp.where(hold, raw, 0.0), axis=1, keepdims=True) / levels

    raw_own = jnp.concatenate([raw_s[...], pack_e[0:32], raw_n[...]], axis=0)
    fe_x[:, 0:128] = jnp.where(lane == 127, column_mean(from_w, mask_e[:, 127:128]), edge[FE])
    fe_x[:, 128:256] = ext[FE, 8:72, 128:256]
    fe_x[:, 256:384] = jnp.where(
        lane == 127, column_mean(raw_own, mask_e[:, 383:384]), ext[FE, 8:72, 256:384]
    )
    fn_x[:, 0:128] = edge[FN]
    fn_x[:, 128:384] = ext[FN, 8:72, 128:384]
    for first, tile in ((8, 0), (40, 32)):
        cut = mask_n[first : first + 8, 128:384]
        total = jnp.zeros_like(cut)
        for k in range(levels):
            total = total + jnp.where(cut > k, v_s[k, tile : tile + 8, :], 0.0)
        fn_x[first : first + 8, 128:384] = jnp.where(
            rows((8, 256)) == 7, total / levels, ext[FN, 8 + first : 16 + first, 128:384]
        )
    lane = lanes((16, 128))
    level = rows((16, 128)).astype(F32)
    for line, a, b in ((15, got_se[16:32], got_sw[16:32]), (47, got_e[32:48], got_w[32:48])):
        raw = jnp.where(lane < 64, a, b)
        hold = level < mask_n[line : line + 1, 0:128]
        mean = jnp.sum(jnp.where(hold, raw, 0.0), axis=0, keepdims=True) / levels
        fn_x[line : line + 1, 0:128] = mean

    tiles = [slice(128 * t, 128 * t + 128) for t in range(3)]
    fx = ed[...] * fe_x[...]
    fy = nd[...] * fn_x[...]
    gs[0:8, :] = jnp.zeros((8, 384), F32)
    gs[8:72, :] = fy
    divergence = fx - west(fx) + fy - gs[7:71, :]
    height = ext[HT, 8:72, :] - divergence
    a_e = WAVE * ed[...]
    a_n = WAVE * nd[...]
    a_w = west(a_e)
    gs[8:72, :] = a_n
    a_s = gs[7:71, :]
    a_0 = a_e + a_w + a_n + a_s
    for t, tile in enumerate(tiles):
        for i, value in enumerate((divergence, a_e, a_w, a_n, a_s, a_0)):
            coef[i, t] = value[:, tile]
        for b in range(2):
            hb[b, t, 0:8, :] = jnp.zeros((8, 128), F32)
            hb[b, t, 72:80, :] = jnp.zeros((8, 128), F32)
        hb[0, t, 8:72, :] = height[:, tile]
        hw[t, 0:48, :] = (SUBSTEPS * 1.0) * height[8:56, tile]
        hw[t, 48:56, :] = jnp.zeros((8, 128), F32)
    lane = lanes((8, 128))

    def substep(old, weight, first, last, final=False):
        new = 1 - old
        for at_row in range(first, last, 8):
            here, inner = slice(8 + at_row, 16 + at_row), slice(at_row, at_row + 8)
            north, south = slice(9 + at_row, 17 + at_row), slice(7 + at_row, 15 + at_row)
            h = [hb[old, t, here, :] for t in range(3)]
            to_w = [pltpu.roll(x, 127, 1) for x in h]
            to_e = [pltpu.roll(x, 1, 1) for x in h]
            for t in range(3):
                h_e = jnp.where(lane == 127, to_w[(t + 1) % 3], to_w[t])
                h_w = jnp.where(lane == 0, to_e[(t + 2) % 3], to_e[t])
                change = (
                    (coef[1, t, inner, :] * h_e + coef[2, t, inner, :] * h_w)
                    + (coef[3, t, inner, :] * hb[old, t, north, :]
                       + coef[4, t, inner, :] * hb[old, t, south, :])
                    - coef[5, t, inner, :] * h[t]
                )
                div = coef[0, t, inner, :] - change
                value = h[t] - div
                if not final:
                    coef[0, t, inner, :] = div
                hb[new, t, here, :] = value
                if 8 <= at_row < 56:
                    hw[t, at_row - 8 : at_row, :] += weight * value

    for step in range(2, 5):
        substep(step % 2, SUBSTEPS + 1.0 - step, 0, 64)
    pl.semaphore_wait(gy_greet.at[1], number(2) + number(-2))
    greet(gy_greet.at[2], [(0, -4)])
    for step in range(5, SUBSTEPS + 1):
        substep(step % 2, SUBSTEPS + 1.0 - step, 8, 56, step == SUBSTEPS)

    finish(tracer_y, LATER)
    m_n = mn[...]
    pn = jnp.zeros((8, 256), F32)
    ps = jnp.zeros((8, 256), F32)
    ends = [jnp.zeros((8, 256), F32)] * 2
    for k in range(levels):
        pn = pn + (0.3 * t_s[1, k, 48:56, :] - 0.7 * t_s[0, k, 48:56, :])
        ps = ps + (0.3 * t_s[1, k, 8:16, :] - 0.7 * t_s[0, k, 8:16, :])
        pp[k, 40:48, :] = pn
        pp[k, 0:8, :] = ps
        for i, first in enumerate((0, 32)):
            vv = v_s[k, first : first + 8, :] - PRESS * (
                pp[k, first + 1 : first + 9, :] - pp[k, first : first + 8, :])
            tv[k, first : first + 8, :] = vv
            ends[i] = ends[i] + jnp.where(m_n[first : first + 8] > k, vv, 0.0)
    sv = jnp.concatenate([ends[0], sv[0:24], ends[1]], axis=0)
    scale = levels / SUBSTEPS
    wide_n = [hw[t, 0:40, :] for t in (1, 2)]
    next_n = [hw[t, 1:41, :] for t in (1, 2)]
    step_n = jnp.concatenate([b - a for a, b in zip(wide_n, next_n)], axis=1)
    sum_n = SUBSTEPS * fn_x[8:48, 128:384] - nw[8:48, 128:384] * step_n
    fix_v = (scale * sum_n - sv) / jnp.maximum(m_n, 1.0)
    for k in range(levels):
        vv = jnp.where(m_n > k, tv[k] + fix_v, 0.0)
        tv[k] = vv
        fv_b[k] = vv[8:40]
        sums[k] = vv[8:40, 0:128] + vv[8:40, 128:256]
    sums[levels:12] = jnp.zeros((12 - levels, 32, 128), F32)

    part = jnp.zeros((8, 128), F32)
    for r in range(3):
        pick = (rows((8, 128)) == r).astype(F32)
        part = part + exact_dot(
            pick, sums[4 * r : 4 * r + 4].reshape(128, 128), ((1,), (1,)), False
        )
    own_r[...] = part[0:3]

    def share(src, dst, i, peer, send_to, recv_to):
        return pltpu.make_async_remote_copy(
            src_ref=src, dst_ref=dst.at[i], send_sem=send_to.at[i], recv_sem=recv_to.at[i],
            device_id=peer, device_id_type=MESH_ID,
        )

    pl.semaphore_wait(gx_greet.at[1], 2)
    def first_copy(i):
        to = jnp.where(i >= gx, i + 1, i)
        return pltpu.make_async_remote_copy(
            src_ref=own_r, dst_ref=peer_r.at[jnp.where(gx > to, gx - 1, gx)],
            send_sem=gx_send.at[0], recv_sem=gx_recv.at[0], device_id=(to, gy), device_id_type=MESH_ID,
        )

    def all_shares():
        return pltpu.make_async_remote_copy(
            src_ref=peer_r, dst_ref=peer_r, send_sem=gx_send.at[0], recv_sem=gx_recv.at[0],
            device_id=chip_at(0, 0, 1), device_id_type=MESH_ID,
        )

    first_share = [first_copy(i) for i in range(nx - 1)]
    for copy in first_share:
        copy.start()

    h_b[:, 0:128] = hb[1, 1, 24:56, :]
    h_b[:, 128:256] = hb[1, 2, 24:56, :]
    stores = [
        pltpu.make_async_copy(a, b, in_sem.at[i])
        for i, (a, b) in enumerate([(h_b, h_out), (fv_b, fv_out), (fu_b, fu_out), (m_b, m_out)])
    ]
    stores[0].start()
    stores[1].start()
    weighted = jnp.concatenate([hw[t, 8:40, :] for t in range(3)], axis=1)
    sum_e = SUBSTEPS * fe_x[16:48, :] - ew[16:48, :] * (east(weighted) - weighted)
    finish(tracer_x, LATER)
    lane = lanes((32, 128))
    both = jnp.where(lane % 4 >= 2, got_tw[...], got_te[...])
    m_e = me[...]
    p0 = jnp.zeros((32, 128), F32)
    su = jnp.zeros((32, 384), F32)
    for k in range(levels):
        for tr in range(2):
            t0[tr, k] = turn(both, -4 * (tr * levels + k))
        p0 = p0 + (0.3 * t0[1, k] - 0.7 * t0[0, k])
        px = jnp.concatenate([p0, pp[k, 8:40, :]], axis=1)
        uu = jnp.concatenate([turn(got_w[0:32, :], 127 - RAW - k), u_s[k]], axis=1)
        uu = uu - PRESS * (east(px) - px)
        tu[k] = uu
        su = su + jnp.where(m_e > k, uu, 0.0)
    fix_u = (scale * sum_e - su) / jnp.maximum(m_e, 1.0)
    for k in range(levels):
        uu = jnp.where(m_e > k, tu[k] + fix_u, 0.0)
        tu[k] = uu
        fu_b[k] = uu[:, 128:384]
    stores[2].start()

    def tracer_level(turn_index, carry):
        k = levels - 1 - turn_index
        up = jnp.maximum(k - 1, 0)
        level = k.astype(F32)
        w_below, wt, value = carry[0], carry[1:3], carry[3:5]
        fu = tu[k]
        fv = tv[k]
        div = (fu - west(fu))[:, 128:384] + fv[8:40] - tv[k, 7:39, :]
        w_top = w_below - div
        kappa = jnp.where(cw > level + 1.0, d_s[k], 0.0)
        new_wt, new_value = [], []
        for tr in range(2):
            own_t = t_s[tr, k, 16:48, :]
            tx = jnp.concatenate([t0[tr, k], own_t], axis=1)
            te1 = east(tx)
            face = (7.0 * (tx + te1) - (west(tx) + east(te1))) * (1.0 / 12.0)
            flux = fu * face
            out = (flux - west(flux))[:, 128:384]
            ty = t_s[tr, k, 8:48, :]
            face = (7.0 * (ty + t_s[tr, k, 9:49, :])
                    - (t_s[tr, k, 7:47, :] + t_s[tr, k, 10:50, :])) * (1.0 / 12.0)
            flux = fv * face
            fyb[...] = flux
            out = out + (flux[8:40] - fyb[7:39, :])
            top = jnp.where(k == 0, own_t, 0.5 * (own_t + t_s[tr, up, 16:48, :]))
            through = w_top * top
            source = jnp.where(cw > level, own_t - DT * (out + (through - wt[tr])), 0.0)
            val = (source + kappa * value[tr]) * inv[k]
            m_b[tr, k] = val
            new_wt.append(through)
            new_value.append(val)
        return (w_top, *new_wt, *new_value)

    zero = jnp.zeros((32, 256), F32)
    lax.fori_loop(0, levels, tracer_level, (zero,) * 5)

    def back(k, carry):
        out = []
        for tr in range(2):
            val = m_b[tr, k] + ratio[k] * carry[tr]
            m_b[tr, k] = val
            out.append(val)
        return tuple(out)

    lax.fori_loop(0, levels, back, (zero,) * 2)
    stores[3].start()

    a, b = rows((128, 128)), lanes((128, 128))
    block = (a // 32) == (b // 32)
    upto = jnp.where(jnp.logical_and(block, a <= b), 1.0, 0.0)
    whole = jnp.where(block, 1.0, 0.0)
    all_shares().wait_recv()
    total = own_r[...]
    for i in range(nx - 1):
        total = total + peer_r[i]
    all_r[...] = total
    pl.when(exists(4))(lambda: pl.semaphore_wait(gy_greet.at[2], 1))
    second_share = [
        share(all_r, south_r, i, at(0, i + 1), gy_send, gy_recv) for i in range(ny - 1)
    ]
    for i, copy in enumerate(second_share):
        pl.when(exists(i + 1))(lambda copy=copy: copy.start())
    total = jnp.concatenate([total, jnp.zeros((5, 128), F32)], axis=0)
    running = exact_dot(total, upto, ((1,), (0,)), True)
    all_shares().wait_send()
    finish_sends(halo + tracer_x + tracer_y)
    for copy, dy in row_copies:
        pl.when(exists(dy))(copy.wait_send)
    for store in stores:
        store.wait()
    for i, copy in enumerate(second_share):
        pl.when(exists(-i - 1))(lambda copy=copy: copy.wait_recv())
    south = jnp.zeros((3, 128), F32)
    for i in range(ny - 1):
        south = south + jnp.where(gy >= i + 1, south_r[i], 0.0)
    south = jnp.concatenate([south, jnp.zeros((5, 128), F32)], axis=0)
    running = (running + exact_dot(south, whole, ((1,), (0,)), True)) * (nx * 256 * ny * 32) ** -0.5
    for k in range(levels):
        ov_out[k : k + 1, :] = running[k // 4 : k // 4 + 1, 32 * (k % 4) : 32 * (k % 4) + 32]
    for i, copy in enumerate(second_share):
        pl.when(exists(i + 1))(lambda copy=copy: copy.wait_send())


def store_kernel(*refs):
    held, results, sem = refs[:5], refs[5:10], refs[10]
    copies = [
        pltpu.make_async_copy(a, b, sem.at[i]) for i, (a, b) in enumerate(zip(held, results))
    ]
    for copy in copies:
        copy.start()
    for copy in copies:
        copy.wait()


def solution(mesh):
    nx, ny = mesh.shape["gx"], mesh.shape["gy"]
    vmem, anywhere = pltpu.VMEM, pl.ANY
    dma = pltpu.SemaphoreType.DMA

    def shape(*s):
        return jax.ShapeDtypeStruct(s, F32)

    def per_device(u, v, t, d, surface, depth, wet, count):
        operands = [
            pltpu.with_memory_space_constraint(a, pltpu.HBM)
            for a in (u, v, t, d, surface, depth, wet, count)
        ]

        def buf(*s):
            return vmem(s, F32)

        def ibuf(*s):
            return vmem(s, jnp.int32)

        scratch = [
            buf(5, 80, 384), buf(10, 32, 256), buf(10, 40, 256), buf(10, 32, 256),
            buf(2, 10, 56, 256), ibuf(2, 32, 256), buf(64, 384), buf(64, 384),
            buf(10, 32, 256), buf(10, 32, 256), buf(2, 10, 32, 256), buf(32, 256), buf(320, 128),
            buf(48, 128), buf(48, 128), buf(48, 128), buf(48, 128),
            buf(32, 128), buf(16, 128), buf(32, 128), buf(16, 128), buf(16, 128), buf(16, 128),
            buf(32, 128), buf(32, 128), buf(32, 128), buf(32, 128),
            buf(64, 384), buf(64, 384), buf(64, 384), buf(64, 384),
            buf(32, 384), buf(40, 256), buf(80, 384), buf(2, 3, 80, 128), buf(6, 3, 64, 128), buf(3, 56, 128),
            buf(10, 32, 384), buf(10, 40, 256), buf(2, 10, 32, 128), buf(10, 48, 256), buf(10, 32, 256), buf(10, 32, 256),
            buf(12, 32, 128), buf(3, 128), buf(nx - 1, 3, 128), buf(3, 128), buf(ny - 1, 3, 128),
            buf(40, 256),
            dma((6,)), dma((6,)), dma((9,)), dma((1,)), dma((1,)),
            dma((ny - 1,)), dma((ny - 1,)),
            pltpu.SemaphoreType.REGULAR((2,)), pltpu.SemaphoreType.REGULAR((3,)),
        ]
        sizes = [(10, 32, 256), (10, 32, 256), (2, 10, 32, 256), (32, 256), (10, 32)]

        def body(*refs):
            step_kernel(*refs, nx=nx, ny=ny)

        held = pl.pallas_call(
            body,
            name="ocean_step",
            out_shape=[pltpu.VMEM(s, F32) for s in sizes],
            in_specs=[pl.BlockSpec(memory_space=anywhere)] * 8,
            out_specs=[pl.BlockSpec(memory_space=anywhere)] * 4 + [pl.BlockSpec(memory_space=vmem)],
            scratch_shapes=scratch,
            compiler_params=pltpu.CompilerParams(
                collective_id=0, has_side_effects=True, vmem_limit_bytes=32 << 20
            ),
        )(*operands)
        return pl.pallas_call(
            store_kernel,
            name="store_results",
            out_shape=[shape(10, 32, 256), shape(10, 32, 256), shape(2, 10, 32, 256),
                       shape(32, 256), shape(10, 32)],
            in_specs=[pl.BlockSpec(memory_space=anywhere)] * 5,
            out_specs=[pl.BlockSpec(memory_space=anywhere)] * 5,
            scratch_shapes=[dma((5,))],
            compiler_params=pltpu.CompilerParams(vmem_limit_bytes=4 << 20),
        )(*held)

    field, flat = P(None, "gy", "gx"), P("gy", "gx")
    tracer = P(None, None, "gy", "gx")
    return jax.shard_map(
        per_device,
        mesh=mesh,
        in_specs=(field, field, tracer, field, flat, flat, flat, flat),
        out_specs=(field, field, tracer, flat, P(None, "gy")),
        check_vma=False,
    )
```
